32 devices in a mesh: seq: 8 (over z, y), batch: 4 (over x, core).
Axes of the slice: x: 2, y: 2, z: 4, core: 2. Of those that a mesh axis runs over, the one named last changes fastest.
Arguments:
- inputs: bfloat16 [4, 2048, 1024], P('batch', 'seq'), may hold values from -6 to 6
- domain_ids: int32 [4], P('batch'), may hold values from 0 to 3
- norm1_gain: bfloat16 [1024], P(('seq', 'batch')), may hold values from 0.099609375 to 1.8984375
- w_qkv: bfloat16 [1024, 3072], P(('seq', 'batch')), may hold values from -0.1875 to 0.1875
- w_beta: bfloat16 [1024, 8], P(('seq', 'batch')), may hold values from -0.1875 to 0.1875
- conv_weight: bfloat16 [3072, 4], P(('seq', 'batch')), may hold values from -3 to 3
- domain_bias: bfloat16 [4, 8], replicated, may hold values from -7 to 3
- head_gain: bfloat16 [128], replicated, may hold values from 0.099609375 to 1.8984375
- w_out: bfloat16 [1024, 1024], P(('seq', 'batch')), may hold values from -0.1875 to 0.1875
- norm2_gain: bfloat16 [1024], P(('seq', 'batch')), may hold values from 0.099609375 to 1.8984375
- w_gate_up: bfloat16 [1024, 5632], P(('seq', 'batch')), may hold values from -0.1875 to 0.1875
- w_down: bfloat16 [2816, 1024], P(('seq', 'batch')), may hold values from -0.15625 to 0.15625
- cotangent: bfloat16 [4, 2048, 1024], P('batch', 'seq'), may hold values from -6 to 6
Outputs:
- output: bfloat16 [4, 2048, 1024], P('batch', 'seq')
- grad_input: float32 [4, 2048, 1024], P('batch', 'seq')
- grad_norm1: float32 [1024], P(('seq', 'batch'))
- grad_qkv: float32 [1024, 3072], P(('seq', 'batch'))
- grad_beta: float32 [1024, 8], P(('seq', 'batch'))
- grad_conv: float32 [3072, 4], P(('seq', 'batch'))
- grad_domain_bias: float32 [4, 8], replicated
- grad_head_gain: float32 [128], replicated
- grad_out_proj: float32 [1024, 1024], P(('seq', 'batch'))
- grad_norm2: float32 [1024], P(('seq', 'batch'))
- grad_gate_up: float32 [1024, 5632], P(('seq', 'batch'))
- grad_down: float32 [2816, 1024], P(('seq', 'batch'))
The draws below stay inside these ranges and needn't reach their ends.
All inputs are finite; a program needn't handle non-finite values.
Results may differ from the reference program's by a relative error of at most 0.02.
Values may be sent and summed in bfloat16 or wider, within the bound.
No kernel may reach another device: no remote copies, remote signals or barrier semaphores. Data moves between devices by JAX's collectives and lax.ppermute only.
A program may use at most 256 MiB of HBM per device.

```python
import math
import jax
import jax.numpy as jnp
import numpy as np
from jax import lax

D = 1024
H = 8
DK = 128
FF = 2816
BLOCK = 64
CONV = 4
NDOM = 4
SEQLEN = 2048
SEQS = 4


def with_ends(result, own_key, smallest, largest):
    longest = result.shape.index(max(result.shape))
    spots = []
    for shift in (0, 1):
        where = [jax.random.randint(jax.random.fold_in(own_key, axis), (), 0, length) for axis, length in enumerate(result.shape)]
        where[longest] = (where[longest] + shift) % result.shape[longest]
        spots.append(tuple(where))
    return result.at[spots[0]].set(smallest).at[spots[1]].set(largest)


def level_of(rng, shape, shards, least, top_value):
    level, own = 1.0, jax.random.fold_in(rng, 6)
    for axis_at, blocks in shards:
        heights = jnp.exp(jax.random.uniform(jax.random.fold_in(own, axis_at), (blocks,), jnp.float32, least / len(shards), top_value / len(shards)))
        level = level * jnp.repeat(heights, shape[axis_at] // blocks).reshape([-1 if axis == axis_at else 1 for axis in range(len(shape))])
    return level


def rank_bounds(amount, skew):
    loads = [(1 << 20) // math.isqrt(standing ** skew) + 1 for standing in range(1, amount + 1)]
    scale = 1 + sum(loads) // (1 << 30)
    return np.cumsum(np.array([max(1, weight // scale) for weight in loads]))


def ranked(stream_key, dims, amount, skew):
    grid = rank_bounds(amount, skew)
    lot = jax.random.randint(jax.random.fold_in(stream_key, 1), dims, 0, int(grid[amount - 1]))
    standing = jnp.searchsorted(jnp.asarray(grid, jnp.int32), lot, side="right")
    return jax.random.permutation(jax.random.fold_in(stream_key, 2), amount)[standing].astype(jnp.int32)


def centred(key, shape, spread, limit, pieces=(), kind=jnp.bfloat16):
    result = spread * jax.random.normal(key, shape, jnp.float32)
    if pieces:
        result = result * level_of(key, shape, pieces, -0.22, 0.18)
    return jnp.clip(result, -limit, limit).astype(kind)


def setup_inputs(seed: int = 0) -> dict:
    splits = jax.random.split(jax.random.key(seed), 14)
    return {
        "inputs": centred(splits[0], (SEQS, SEQLEN, D), 1.0, 6.0, ((0, 4), (1, 8))),
        "domain_ids": with_ends(ranked(splits[1], (SEQS,), NDOM, 2), jax.random.fold_in(splits[1], 3), 0, NDOM - 1).astype(jnp.int32),
        "norm1_gain": jnp.clip(1.0 + 0.18 * jax.random.normal(splits[2], (D,), jnp.float32), 0.099609375, 1.8984375).astype(jnp.bfloat16),
        "w_qkv": centred(splits[3], (D, 3 * D), D ** -0.5, 0.1875, ((0, 32),)),
        "w_beta": centred(splits[4], (D, H), D ** -0.5, 0.1875, ((0, 32),)),
        "conv_weight": centred(splits[5], (3 * D, CONV), CONV ** -0.5, 3.0, ((0, 32),)),
        "domain_bias": jnp.clip(jax.random.uniform(splits[6], (NDOM, H), jnp.float32, -7.0, 3.0), -7.0, 3.0).astype(jnp.bfloat16),
        "head_gain": jnp.clip(1.0 + 0.18 * jax.random.normal(splits[7], (DK,), jnp.float32), 0.099609375, 1.8984375).astype(jnp.bfloat16),
        "w_out": centred(splits[8], (D, D), D ** -0.5, 0.1875, ((0, 32),)),
        "norm2_gain": jnp.clip(1.0 + 0.18 * jax.random.normal(splits[9], (D,), jnp.float32), 0.099609375, 1.8984375).astype(jnp.bfloat16),
        "w_gate_up": centred(splits[10], (D, 2 * FF), D ** -0.5, 0.1875, ((0, 32),)),
        "w_down": centred(splits[11], (FF, D), (FF // 2) ** -0.5, 0.15625, ((0, 32),)),
        "cotangent": centred(splits[12], (SEQS, SEQLEN, D), 1.0, 6.0, ((0, 4), (1, 8))),
    }


PRECISE = lax.Precision.HIGHEST
EPS = 1e-06

@jax.custom_vjp
def low(v):
    return lax.optimization_barrier(v.astype(jnp.bfloat16)).astype(jnp.float32)

@jax.custom_vjp
def low_back(v):
    return v

def low_keep(v):
    return (low(v), None)

def low_pass(kept, grad):
    return (grad,)

def back_keep(v):
    return (v, None)

def back_low(kept, grad):
    return (low(grad),)
low.defvjp(low_keep, low_pass)
low_back.defvjp(back_keep, back_low)

def matmul_hi(left, right):
    return jnp.dot(left.astype(jnp.float32), right.astype(jnp.float32), precision=PRECISE, preferred_element_type=jnp.float32)

def rms_scale(values, gain):
    return values * lax.rsqrt(lax.optimization_barrier(jnp.mean(values * values, axis=-1, keepdims=True)) + EPS) * gain

def unit_rows(values):
    return values * lax.rsqrt(lax.optimization_barrier(jnp.sum(values * values, axis=-1, keepdims=True)) + EPS)

def conv_piece(extended, conv_taps):
    out_len = extended.shape[-2] - CONV + 1
    mixed_sum = conv_taps[:, 0] * extended[..., 0:out_len, :]
    for position in range(1, CONV):
        mixed_sum = mixed_sum + conv_taps[:, position] * extended[..., position:position + out_len, :]
    activated = jax.nn.silu(mixed_sum)
    shape_out = activated.shape[:-1] + (H, DK)
    query_part = unit_rows(activated[..., :D].reshape(shape_out)) * DK ** (-0.5)
    key_part = unit_rows(activated[..., D:2 * D].reshape(shape_out))
    value_part = activated[..., 2 * D:].reshape(shape_out)
    return (query_part, key_part, value_part)

def block_weights(key_rows, value_rows, beta_rates):
    key_inner = jnp.einsum('...cd,...ed->...ce', key_rows, key_rows, precision=PRECISE)
    lower_part = jnp.tril(key_inner * beta_rates[..., :, None], -1)
    system = lower_part + jnp.eye(BLOCK, dtype=jnp.float32)
    right_side = jnp.concatenate([key_rows, value_rows], axis=-1) * beta_rates[..., :, None]
    solved = lax.linalg.triangular_solve(system, right_side, left_side=True, lower=True, unit_diagonal=True)
    return (solved[..., :DK], solved[..., DK:])

def block_step(state_now, block_data):
    queries, key_rows, value_rows, beta_rates = block_data
    w_factor, u_factor = block_weights(key_rows, value_rows, beta_rates)
    fresh_values = u_factor - jnp.einsum('hcd,hde->hce', w_factor, state_now, precision=PRECISE)
    scores = jnp.tril(jnp.einsum('hcd,hed->hce', queries, key_rows, precision=PRECISE))
    block_out = jnp.einsum('hcd,hde->hce', queries, state_now, precision=PRECISE)
    block_out = block_out + jnp.einsum('hce,hef->hcf', scores, fresh_values, precision=PRECISE)
    state_next = state_now + jnp.einsum('hcd,hce->hde', key_rows, fresh_values, precision=PRECISE)
    return (state_next, block_out)

def forward(params, seq_in, choose):
    gain_one, w_qkv, w_beta, conv_taps, bias_table, head_gain, w_out, gain_two, w_gate_up, w_down = params
    length = seq_in.shape[0]
    count = length // BLOCK
    normed = low(rms_scale(seq_in, gain_one))
    pre_conv = low_back(low(matmul_hi(normed, w_qkv)))
    extended = jnp.concatenate([jnp.zeros((CONV - 1, 3 * D), jnp.float32), pre_conv], axis=0)
    queries, key_rows, value_rows = conv_piece(extended, conv_taps)
    queries, key_rows, value_rows = (low(queries), low(key_rows), low(value_rows))
    beta_rates = jax.nn.sigmoid(low_back(matmul_hi(normed, w_beta)) + matmul_hi(choose, bias_table))

    def split_blocks(values):
        return values.reshape(count, BLOCK, H, DK).transpose(0, 2, 1, 3)
    rate_blocks = beta_rates.reshape(count, BLOCK, H).transpose(0, 2, 1)
    start_state = jnp.zeros((H, DK, DK), jnp.float32)
    final_state, block_outs = lax.scan(jax.checkpoint(block_step), start_state, (split_blocks(queries), split_blocks(key_rows), split_blocks(value_rows), rate_blocks))
    mixed_rows = block_outs.transpose(0, 2, 1, 3).reshape(length, H, DK)
    heads_out = low(rms_scale(mixed_rows, head_gain).reshape(length, D))
    middle = seq_in + low_back(matmul_hi(heads_out, w_out))
    normed_two = low(rms_scale(middle, gain_two))
    gate_up = low_back(matmul_hi(normed_two, w_gate_up))
    hidden = low(jax.nn.silu(gate_up[:, :FF]) * gate_up[:, FF:])
    return middle + low_back(matmul_hi(hidden, w_down))

def reference(inputs, domain_ids, norm1_gain, w_qkv, w_beta, conv_weight, domain_bias, head_gain, w_out, norm2_gain, w_gate_up, w_down, cotangent):
    params = tuple((weight.astype(jnp.float32) for weight in (norm1_gain, w_qkv, w_beta, conv_weight, domain_bias, head_gain, w_out, norm2_gain, w_gate_up, w_down)))

    def per_sequence(totals, seq_item):
        seq_in, seq_cot, domain = seq_item
        choose = (domain == jnp.arange(NDOM, dtype=jnp.int32)).astype(jnp.float32)

        def run_block(weights, tokens):
            return forward(weights, tokens, choose)
        result_rows, pull_back = jax.vjp(run_block, params, seq_in.astype(jnp.float32))
        weight_grads, input_grad = pull_back(seq_cot.astype(jnp.float32))
        totals = tuple((total + part for total, part in zip(totals, weight_grads)))
        return (totals, (result_rows.astype(jnp.bfloat16), input_grad))
    zero_grads = tuple((jnp.zeros_like(weight) for weight in params))
    grad_sums, (outputs, input_grads) = lax.scan(per_sequence, zero_grads, (inputs, cotangent, domain_ids))
    return (outputs, input_grads, grad_sums[0], grad_sums[1], grad_sums[2], grad_sums[3], grad_sums[4], grad_sums[5], grad_sums[6], grad_sums[7], grad_sums[8], grad_sums[9])
```

```python
import functools

import jax
import jax.numpy as jnp
from jax import lax
from jax.experimental import pallas as pl
from jax.experimental.pallas import tpu as pltpu
from jax.sharding import Mesh
from jax.sharding import PartitionSpec as P

D = 1024
H = 8
DK = 128
FF = 2816
CONV = 4
NDOM = 4
EPS = 1e-06
HALO = 16
F32 = jnp.float32
BF16 = jnp.bfloat16
SEQ = ("z", "y")
ALL = ("z", "y", "x", "core")
VMEM_LIMIT = 48 * 1024 * 1024


def swap(a):
    return lax.ppermute(a, "core", [(0, 1), (1, 0)])


def turned(a, axis, by):
    n = lax.axis_size(axis)
    return lax.ppermute(a, axis, [(i, (i + by) % n) for i in range(n)])


def gather_axis(a, axis, dim):
    n, me = lax.axis_size(axis), lax.axis_index(axis)
    if n == 1:
        return jnp.expand_dims(a, dim)
    got = [turned(a, axis, k) for k in range(1, n)]
    if n == 2:
        first = me == 0
        return jnp.stack([jnp.where(first, a, got[0]), jnp.where(first, got[0], a)], axis=dim)
    back = got[::-1] + [a]
    return lax.dynamic_slice_in_dim(jnp.stack(back + back, axis=dim), n - 1 - me, n, axis=dim)


def scatter_axis(a, axis, dim):
    n, me = lax.axis_size(axis), lax.axis_index(axis)
    total = lax.dynamic_index_in_dim(a, me, dim, False).astype(F32)
    sent = []
    for k in range(1, n):
        part = lax.dynamic_index_in_dim(a, (me + k) % n, dim, False).astype(BF16)
        sent.append(turned(part, axis, k))
    for part in sent:
        total = total + part.astype(F32)
    return total


def gather_chips(pair):
    flat = gather_axis(pair, "z", 0)
    one = gather_axis(gather_axis(flat[:, 0], "x", 1), "y", 1)
    two = gather_axis(gather_axis(flat[:, 1], "y", 1), "x", 2)
    n = pair.shape[-1]
    return one.reshape(-1, n), two.reshape(-1, n)


def scatter_chips(one, two):
    nz, ny, nx = (lax.axis_size(a) for a in ("z", "y", "x"))
    n = one.shape[-1]
    one = one.reshape(nz, ny, nx, -1, n)
    two = two.reshape(nz, ny, nx, -1, n)
    one = scatter_axis(one, "y", 1).astype(BF16)
    two = scatter_axis(two, "x", 2).astype(BF16)
    one = scatter_axis(one, "x", 1).astype(BF16)
    two = scatter_axis(two, "y", 1).astype(BF16)
    return scatter_axis(jnp.stack([one, two], axis=1), "z", 0)


def core_pick(a, core):
    return (
        lax.dynamic_index_in_dim(a, core, 0, False),
        lax.dynamic_index_in_dim(a, 1 - core, 0, False),
    )


def chip_rows(by_core, core):
    mine, other = core_pick(by_core, core)
    got = swap(other)
    first = core == 0
    return jnp.concatenate(
        [jnp.where(first, mine, got), jnp.where(first, got, mine)], axis=-2
    )


def own_rows(total, core):
    k, both, n = total.shape
    parts = total.reshape(k, 2, both // 2, n).transpose(1, 0, 2, 3)
    mine, other = core_pick(parts, core)
    got = swap(other)
    first = core == 0
    return jnp.stack([jnp.where(first, mine, got), jnp.where(first, got, mine)], axis=0)


def reduce_small(a):
    a = a + swap(a)
    for axis in ("x", "y", "z"):
        every = gather_axis(a, axis, 0)
        total = every[0]
        for k in range(1, every.shape[0]):
            total = total + every[k]
        a = total
    return a


def dot1(a, b, dims=((1,), (0,))):
    return lax.dot_general(
        a.astype(BF16), b.astype(BF16), (dims, ((), ())), preferred_element_type=F32
    )


TN = ((0,), (0,))
NT = ((1,), (1,))


def split(a):
    high = a.astype(BF16)
    return high, (a - high.astype(F32)).astype(BF16)


def dot3(a, b):
    ah, al = split(a)
    bh, bl = split(b)
    return dot1(ah, bh) + (dot1(ah, bl) + dot1(al, bh))


def sigmoid(v):
    return 1.0 / (1.0 + jnp.exp(-v))


def grid_masks(n):
    i = lax.broadcasted_iota(jnp.int32, (n, n), 0)
    j = lax.broadcasted_iota(jnp.int32, (n, n), 1)
    return i, j


def unit_inverse(lower, i, j):
    n = lower.shape[0]
    level = jnp.where(i > j, i ^ j, 0)
    eye = jnp.where(i == j, 1.0, 0.0).astype(F32)
    inverse = eye - jnp.where(level == 1, lower, 0.0)
    size = 2
    while size < n:
        corner = jnp.where((level >= size) & (level < 2 * size), lower, 0.0).astype(BF16)
        low = inverse.astype(BF16)
        inverse = inverse - dot1(low, dot1(corner, low))
        size *= 2
    rest = eye - inverse - dot3(lower, inverse)
    return inverse + dot1(inverse, rest)


def conv_of(ext, taps, rows):
    total = taps[0:1, :] * ext[HALO - 3 : HALO - 3 + rows]
    for i in range(1, CONV):
        total = total + taps[i : i + 1, :] * ext[HALO - 3 + i : HALO - 3 + i + rows]
    return total


def first_kernel(x_ref, g_ref, w_ref, wb_ref, cv_ref, bias_ref, n_ref, pre_ref, qkv_ref, t_ref, wu_ref, pd_ref, b_ref):
    rows = qkv_ref.shape[1] // 2
    frame = rows + HALO

    @pl.when(pl.program_id(0) == 0)
    def _():
        x = x_ref[...].astype(F32)
        scale = lax.rsqrt(jnp.mean(x * x, axis=-1, keepdims=True) + EPS)
        n_ref[...] = (x * scale * g_ref[...]).astype(BF16)

    normed = n_ref[...]
    pre = dot1(normed, w_ref[0]).astype(BF16)
    pre_ref[0] = pre
    linear = dot1(normed, wb_ref[0])
    i, j = grid_masks(rows)
    for q in range(2):
        rate = sigmoid(linear[q * frame + HALO : (q + 1) * frame] + bias_ref[0, q : q + 1, :])
        b_ref[0, q * rows : (q + 1) * rows, :] = rate
        ext = pre[q * frame : (q + 1) * frame].astype(F32)
        conv = conv_of(ext, cv_ref[0], rows)
        act = conv * sigmoid(conv)
        for h in range(2):
            place = pl.ds(q * rows, rows)
            parts = []
            for kind in range(3):
                lane = (kind * 2 + h) * DK
                one = act[:, lane : lane + DK]
                if kind < 2:
                    one = one * lax.rsqrt(jnp.sum(one * one, axis=-1, keepdims=True) + EPS)
                if kind == 0:
                    one = one * DK ** (-0.5)
                one = one.astype(BF16)
                qkv_ref[0, place, lane : lane + DK] = one
                parts.append(one)
            key, value = parts[1], parts[2]
            col = rate[:, h : h + 1]
            lower = jnp.where(i > j, dot1(key, key, NT) * col, 0.0)
            inverse = unit_inverse(lower, i, j)
            right = jnp.concatenate([key, value], axis=1).astype(F32) * col
            both = dot3(inverse, right)
            p = q * 2 + h
            t_ref[0, p] = inverse.astype(BF16)
            wu_ref[0, p] = both.astype(BF16)
            pd_ref[0, p] = dot1(key, both, TN).astype(BF16)


def state_kernel(pd_ref, s_ref):
    count = pd_ref.shape[0]
    state = jnp.zeros((DK, DK), F32)
    for s in range(count):
        s_ref[s] = state.astype(BF16)
        if s + 1 < count:
            high, low = split(state)
            move = pd_ref[s, :, :DK]
            state = state - (dot1(move, high) + dot1(move, low)) + pd_ref[s, :, DK:].astype(F32)


def adjoint_kernel(pd_ref, g_ref, l_ref):
    count = pd_ref.shape[0]
    adjoint = jnp.zeros((DK, DK), F32)
    for s in range(count - 1, -1, -1):
        l_ref[s] = adjoint.astype(BF16)
        if s > 0:
            high, low = split(adjoint)
            move = pd_ref[s, :, :DK]
            adjoint = (
                adjoint - (dot1(move, high, TN) + dot1(move, low, TN)) + g_ref[s].astype(F32)
            )


def second_kernel(qkv_ref, wu_ref, s_ref, hg_ref, f_ref, m_ref, h_ref):
    rows = qkv_ref.shape[1] // 2
    i, j = grid_masks(rows)
    for q in range(2):
        place = pl.ds(q * rows, rows)
        for h in range(2):
            p = q * 2 + h
            lanes = pl.ds(h * DK, DK)
            query = qkv_ref[0, place, pl.ds(h * DK, DK)]
            key = qkv_ref[0, place, pl.ds((2 + h) * DK, DK)]
            state = s_ref[p]
            fresh = wu_ref[0, p, :, DK:].astype(F32) - dot1(wu_ref[0, p, :, :DK], state)
            scores = jnp.where(i >= j, dot1(query, key, NT), 0.0)
            mixed = dot1(query, state) + dot1(scores, fresh)
            scale = lax.rsqrt(jnp.mean(mixed * mixed, axis=-1, keepdims=True) + EPS)
            f_ref[place, lanes] = fresh.astype(BF16)
            m_ref[place, lanes] = mixed
            h_ref[place, lanes] = (mixed * scale * hg_ref[...]).astype(BF16)


def third_kernel(qkv_ref, wu_ref, s_ref, f_ref, m_ref, dh_ref, hg_ref, sg_ref, gf_ref, gq_ref, gk_ref, ghg_ref):
    rows = qkv_ref.shape[1] // 2
    i, j = grid_masks(rows)
    gain = hg_ref[...]
    gain_grad = jnp.zeros((1, DK), F32)
    for q in range(2):
        place = pl.ds(q * rows, rows)
        for h in range(2):
            p = q * 2 + h
            lanes = pl.ds(h * DK, DK)
            query = qkv_ref[0, place, pl.ds(h * DK, DK)]
            key = qkv_ref[0, place, pl.ds((2 + h) * DK, DK)]
            mixed = m_ref[place, lanes]
            up = dh_ref[place, lanes].astype(F32)
            scale = lax.rsqrt(jnp.mean(mixed * mixed, axis=-1, keepdims=True) + EPS)
            unit = mixed * scale
            gain_grad = gain_grad + jnp.sum(up * unit, axis=0, keepdims=True)
            inner = up * gain
            grad = scale * (inner - unit * jnp.mean(inner * unit, axis=-1, keepdims=True))
            grad = grad.astype(BF16)
            state = s_ref[p]
            fresh = f_ref[place, lanes]
            scores = jnp.where(i >= j, dot1(query, key, NT), 0.0)
            fresh_grad = dot1(scores, grad, TN)
            gf_ref[place, lanes] = fresh_grad
            sg_ref[0, p] = (
                dot1(query, grad, TN) - dot1(wu_ref[0, p, :, :DK], fresh_grad, TN)
            ).astype(BF16)
            score_grad = jnp.where(i >= j, dot1(grad, fresh, NT), 0.0).astype(BF16)
            gq_ref[place, lanes] = dot1(grad, state, NT) + dot1(score_grad, key)
            gk_ref[place, lanes] = dot1(score_grad, query, TN)
    ghg_ref[0] = jnp.broadcast_to(gain_grad, ghg_ref.shape[1:])


def fourth_kernel(qkv_ref, pre_ref, cv_ref, b_ref, t_ref, wu_ref, s_ref, l_ref, f_ref, gf_ref, gq_ref, gk_ref, eg_ref, gc_ref, lg_ref, gb_ref):
    rows = qkv_ref.shape[1] // 2
    frame = rows + HALO
    i, j = grid_masks(rows)
    taps = cv_ref[0]
    lane = lax.broadcasted_iota(jnp.int32, (rows, DK), 1)
    conv_grad = [[jnp.zeros((1, DK), F32) for _ in range(CONV)] for _ in range(6)]
    for q in range(2):
        place = pl.ds(q * rows, rows)
        rate_grads = []
        for h in range(2):
            p = q * 2 + h
            lanes = pl.ds(h * DK, DK)
            query = qkv_ref[0, place, pl.ds(h * DK, DK)]
            key = qkv_ref[0, place, pl.ds((2 + h) * DK, DK)]
            value = qkv_ref[0, place, pl.ds((4 + h) * DK, DK)]
            col = b_ref[0, place, h : h + 1]
            state, adjoint = s_ref[p], l_ref[p]
            both = wu_ref[0, p]
            fresh_grad = gf_ref[place, lanes] + dot1(key, adjoint)
            key_grad = gk_ref[place, lanes] + dot1(f_ref[place, lanes], adjoint, NT)
            factor_grad = jnp.concatenate([-dot1(fresh_grad, state, NT), fresh_grad], axis=1)
            solved = dot1(t_ref[0, p], factor_grad, TN)
            key32, value32 = key.astype(F32), value.astype(F32)
            rate_grad = jnp.sum(
                solved[:, :DK] * key32 + solved[:, DK:] * value32, axis=-1, keepdims=True
            )
            key_grad = key_grad + col * solved[:, :DK]
            value_grad = col * solved[:, DK:]
            system_grad = jnp.where(i > j, -dot1(solved, both, NT), 0.0)
            inner = dot1(key, key, NT)
            rate_grad = rate_grad + jnp.sum(system_grad * inner, axis=-1, keepdims=True)
            inner_grad = (system_grad * col).astype(BF16)
            key_grad = key_grad + dot1(inner_grad, key) + dot1(inner_grad, key, TN)
            rate_grads.append(rate_grad * col * (1.0 - col))
            grads = (gq_ref[place, lanes], key_grad, value_grad)
            for kind in range(3):
                at = kind * 2 + h
                cols = pl.ds(at * DK, DK)
                ext = pre_ref[0, q * frame : (q + 1) * frame, cols].astype(F32)
                tap = cv_ref[0, :, cols]
                conv = conv_of(ext, tap, rows)
                sig = sigmoid(conv)
                act = conv * sig
                grad = grads[kind]
                if kind < 2:
                    scale = lax.rsqrt(jnp.sum(act * act, axis=-1, keepdims=True) + EPS)
                    unit = act * scale
                    grad = grad * DK ** (-0.5) if kind == 0 else grad
                    grad = scale * (grad - unit * jnp.sum(grad * unit, axis=-1, keepdims=True))
                grad = grad * (sig * (1.0 + conv * (1.0 - sig)))
                zero = jnp.zeros((HALO, DK), F32)
                wide = jnp.concatenate([zero, grad, zero], axis=0)
                total = tap[0:1, :] * wide[3 : 3 + frame]
                for t in range(1, CONV):
                    total = total + tap[t : t + 1, :] * wide[3 - t : 3 - t + frame]
                eg_ref[0, q * frame : (q + 1) * frame, cols] = total.astype(BF16)
                for t in range(CONV):
                    conv_grad[at][t] = conv_grad[at][t] + jnp.sum(
                        grad * ext[HALO - 3 + t : HALO - 3 + t + rows], axis=0, keepdims=True
                    )
        logit = jnp.where(lane == 0, rate_grads[0], jnp.where(lane == 1, rate_grads[1], 0.0))
        lg_ref[0, place, :] = logit.astype(BF16)
        gb_ref[0, q : q + 1, :] = jnp.sum(logit, axis=0, keepdims=True)
    for at in range(6):
        for t in range(CONV):
            gc_ref[0, t : t + 1, at * DK : (at + 1) * DK] = conv_grad[at][t]


def lead(*shape):
    return pl.BlockSpec((1,) + shape, lambda p: (p,) + (0,) * len(shape))


def whole(*shape):
    return pl.BlockSpec(shape, lambda p: (0,) * len(shape))


def columns(rows, cols):
    return pl.BlockSpec((rows, cols), lambda p: (0, p))


def quarter():
    return pl.BlockSpec((4, DK, DK), lambda p: (p, 0, 0))


def on_core(kernel, outs, in_specs, out_specs, flops, name):
    return pl.pallas_call(
        kernel,
        out_shape=outs,
        grid=(2,),
        in_specs=in_specs,
        out_specs=out_specs,
        compiler_params=pltpu.CompilerParams(
            vmem_limit_bytes=VMEM_LIMIT, dimension_semantics=("arbitrary",)
        ),
        cost_estimate=pl.CostEstimate(flops=flops, bytes_accessed=8_000_000, transcendentals=0),
        name=name,
    )


def sds(shape, kind):
    return jax.ShapeDtypeStruct(shape, kind)


def scan_states(pd):
    count = lax.axis_size("z") * lax.axis_size("y")
    if count == pd.shape[0]:
        every = lax.all_to_all(pd, SEQ, 0, 0, tiled=True)
        states = pl.pallas_call(
            state_kernel, out_shape=sds((count, DK, DK), BF16), name="state_scan"
        )(every)
        return lax.all_to_all(states, SEQ, 0, 0, tiled=True), every
    every = lax.all_gather(pd, SEQ)
    me = lax.axis_index(SEQ)

    def step(s, state):
        one = lax.dynamic_index_in_dim(every, s, 0, False).astype(F32)
        moved = jnp.einsum(
            "pij,pjk->pik", one[:, :, :DK], state, precision=lax.Precision.HIGHEST
        )
        return state - moved + one[:, :, DK:]

    state = lax.fori_loop(0, me, step, jnp.zeros((pd.shape[0], DK, DK), F32))
    return state.astype(BF16), every


def scan_adjoints(every, start):
    count = lax.axis_size("z") * lax.axis_size("y")
    if count == start.shape[0]:
        grads = lax.all_to_all(start, SEQ, 0, 0, tiled=True)
        adjoints = pl.pallas_call(
            adjoint_kernel, out_shape=sds((count, DK, DK), BF16), name="adjoint_scan"
        )(every, grads)
        return lax.all_to_all(adjoints, SEQ, 0, 0, tiled=True)
    grads = lax.all_gather(start, SEQ)
    me = lax.axis_index(SEQ)

    def step(k, adjoint):
        s = count - 1 - k
        one = lax.dynamic_index_in_dim(every, s, 0, False).astype(F32)
        moved = jnp.einsum(
            "pji,pjk->pik", one[:, :, :DK], adjoint, precision=lax.Precision.HIGHEST
        )
        return adjoint - moved + lax.dynamic_index_in_dim(grads, s, 0, False).astype(F32)

    adjoint = lax.fori_loop(0, count - 1 - me, step, jnp.zeros((start.shape[0], DK, DK), F32))
    return adjoint.astype(BF16)


def shards(
    inputs,
    domain_ids,
    norm1_gain,
    w_qkv,
    w_beta,
    conv_weight,
    domain_bias,
    head_gain,
    w_out,
    norm2_gain,
    w_gate_up,
    w_down,
    cotangent,
):
    core = lax.axis_index("core")
    nz, ny, nx = (lax.axis_size(a) for a in ("z", "y", "x"))
    chips = nz * ny * nx
    seq_devices = nz * ny
    rows = inputs.shape[1]
    frame = rows + HALO
    drows = w_qkv.shape[0]
    frows = w_down.shape[0]
    first = core == 0
    half = H // 2

    qkv_part = chip_rows(
        w_qkv.reshape(drows, 3, 2, 2, 256).transpose(2, 3, 0, 1, 4).reshape(2, 2, drows, 768), core
    )
    w_q_one, w_q_two = gather_chips(qkv_part)

    grows = conv_weight.shape[0]
    small = jnp.concatenate(
        [norm1_gain, norm2_gain, w_beta.reshape(-1), conv_weight.reshape(-1)]
    ).reshape(1, -1)
    smalls = gather_axis(small, "core", 0)
    for axis in ("x", "y", "z"):
        smalls = gather_axis(smalls, axis, 0)
    smalls = smalls.reshape(2 * chips, -1)
    gain_one = smalls[:, :drows].reshape(1, D).astype(F32)
    gain_two = smalls[:, drows : 2 * drows].reshape(1, D).astype(F32)
    full_beta = smalls[:, 2 * drows : 2 * drows + drows * H].reshape(D, 2, half)
    full_conv = smalls[:, 2 * drows + drows * H :].reshape(3, 2, 2, 256, CONV)
    beta_mine = lax.dynamic_index_in_dim(full_beta, core, 1, False)
    conv_mine = (
        lax.dynamic_index_in_dim(full_conv, core, 1, False)
        .transpose(1, 3, 0, 2)
        .reshape(2, CONV, 768)
        .astype(F32)
    )
    beta_pairs = jnp.pad(
        beta_mine.reshape(D, 2, 2).transpose(1, 0, 2), ((0, 0), (0, 0), (0, DK - 2))
    )

    x_own = inputs.reshape(rows, D)
    halo = lax.ppermute(
        x_own[rows - HALO :], SEQ, [(i, i + 1) for i in range(seq_devices - 1)]
    )
    choose = (domain_ids[0] == jnp.arange(NDOM, dtype=jnp.int32)).astype(BF16)
    bias_own = jnp.sum(domain_bias.astype(F32) * choose.astype(F32)[:, None], axis=0)
    extra = jnp.pad(jnp.concatenate([bias_own.astype(BF16), choose]), (0, D - H - NDOM))
    extra = jnp.pad(extra.reshape(1, D), ((0, HALO - 1), (0, 0)))
    frame_own = jnp.concatenate([halo, x_own, extra], axis=0)
    frame_other = swap(frame_own)
    x_frames = jnp.concatenate([frame_own[:frame], frame_other[:frame]], axis=0)
    x_both = jnp.concatenate([x_own, frame_other[HALO:frame]], axis=0).astype(F32)
    bias_both = jnp.stack([extra[0, :H], frame_other[frame, :H]]).astype(F32)
    choose_both = jnp.stack(
        [extra[0, H : H + NDOM], frame_other[frame, H : H + NDOM]]
    ).astype(F32)
    bias_mine = lax.dynamic_index_in_dim(bias_both.reshape(2, 2, half), core, 1, False)
    bias_pairs = jnp.pad(
        bias_mine.reshape(2, 2, 2).transpose(1, 0, 2), ((0, 0), (0, 0), (0, DK - 2))
    )
    g_own = cotangent.reshape(rows, D)
    g_both = jnp.concatenate([g_own, swap(g_own)], axis=0)

    out_cols = w_out.reshape(drows, 2, 2, 256).transpose(1, 2, 0, 3)
    gu_cols = (
        w_gate_up.reshape(drows, 2, chips, 2, frows)
        .transpose(3, 1, 0, 2, 4)
        .reshape(2, 2, drows, FF // 2)
    )
    gu_one, gu_two = gather_chips(
        chip_rows(jnp.concatenate([gu_cols, out_cols], axis=-1), core)
    )
    w_gate, w_up = gu_one[:, : FF // 2], gu_two[:, : FF // 2]
    out_mine = jnp.concatenate([gu_one[:, FF // 2 :], gu_two[:, FF // 2 :]], axis=1)
    out_got = swap(out_mine)
    full_out = jnp.concatenate(
        [jnp.where(first, out_mine, out_got), jnp.where(first, out_got, out_mine)], axis=1
    )
    down_one, down_two = gather_chips(w_down.reshape(frows, 2, D // 2).transpose(1, 0, 2))
    w_down_mine = jnp.concatenate([down_one, down_two], axis=1)

    w_q = jnp.stack([w_q_one, w_q_two])
    tall = 2 * rows
    normed, pre, qkv, inverse, factors, pd, rates = on_core(
        first_kernel,
        (
            sds((2 * frame, D), BF16),
            sds((2, 2 * frame, 768), BF16),
            sds((2, tall, 768), BF16),
            sds((2, 4, rows, rows), BF16),
            sds((2, 4, rows, 2 * DK), BF16),
            sds((2, 4, DK, 2 * DK), BF16),
            sds((2, tall, DK), F32),
        ),
        [
            whole(2 * frame, D),
            whole(1, D),
            lead(D, 768),
            lead(D, DK),
            lead(CONV, 768),
            lead(2, DK),
        ],
        (
            whole(2 * frame, D),
            lead(2 * frame, 768),
            lead(tall, 768),
            lead(4, rows, rows),
            lead(4, rows, 2 * DK),
            lead(4, DK, 2 * DK),
            lead(tall, DK),
        ),
        10_000_000_000,
        "delta_local",
    )(x_frames, gain_one, w_q, beta_pairs, conv_mine, bias_pairs)

    states, every = scan_states(pd.reshape(H, DK, 2 * DK))
    gain_head = head_gain.astype(F32).reshape(1, DK)
    fresh, mixed, heads_mine = on_core(
        second_kernel,
        (sds((tall, 512), BF16), sds((tall, 512), F32), sds((tall, 512), BF16)),
        [lead(tall, 768), lead(4, rows, 2 * DK), quarter(), whole(1, DK)],
        (columns(tall, 256), columns(tall, 256), columns(tall, 256)),
        2_000_000_000,
        "delta_mix",
    )(qkv, factors, states, gain_head)

    heads_got = swap(heads_mine)
    heads_got = jnp.concatenate([heads_got[rows:], heads_got[:rows]], axis=0)
    heads = jnp.concatenate(
        [jnp.where(first, heads_mine, heads_got), jnp.where(first, heads_got, heads_mine)], axis=1
    )
    middle = x_both + jnp.dot(heads, full_out, preferred_element_type=F32)
    scale_two = lax.rsqrt(jnp.mean(middle * middle, axis=-1, keepdims=True) + EPS)
    unit_two = middle * scale_two
    normed_two = (unit_two * gain_two).astype(BF16)
    gate = jnp.dot(normed_two, w_gate, preferred_element_type=F32)
    up = jnp.dot(normed_two, w_up, preferred_element_type=F32)
    sig = jax.nn.sigmoid(gate)
    hidden = (gate * sig * up).astype(BF16)
    hidden_grad = jnp.einsum("nd,fd->nf", g_both, w_down_mine, preferred_element_type=F32)
    up_grad = (hidden_grad * gate * sig).astype(BF16)
    gate_grad = (hidden_grad * up * sig * (1.0 + gate * (1.0 - sig))).astype(BF16)
    normed_two_part = jnp.einsum(
        "nf,df->nd", gate_grad, w_gate, preferred_element_type=F32
    ) + jnp.einsum("nf,df->nd", up_grad, w_up, preferred_element_type=F32)
    part_got = swap(normed_two_part.astype(BF16))
    part_got = jnp.concatenate([part_got[rows:], part_got[:rows]], axis=0)
    normed_two_grad = normed_two_part + part_got.astype(F32)
    grad_norm2 = jnp.sum(normed_two_grad[:rows] * unit_two[:rows], axis=0)
    inner = normed_two_grad * gain_two
    middle_grad = g_both.astype(F32) + scale_two * (
        inner - unit_two * jnp.mean(inner * unit_two, axis=-1, keepdims=True)
    )
    middle_low = middle_grad.astype(BF16)
    out_rows = lax.dynamic_slice_in_dim(full_out, core * 512, 512, 0)
    heads_grad = jnp.einsum("ne,de->nd", middle_low, out_rows, preferred_element_type=F32)

    start_grad, fresh_grad, query_grad, key_grad, gain_part = on_core(
        third_kernel,
        (
            sds((2, 4, DK, DK), BF16),
            sds((tall, 512), F32),
            sds((tall, 512), F32),
            sds((tall, 512), F32),
            sds((2, 8, DK), F32),
        ),
        [
            lead(tall, 768),
            lead(4, rows, 2 * DK),
            quarter(),
            columns(tall, 256),
            columns(tall, 256),
            columns(tall, 256),
            whole(1, DK),
        ],
        (
            lead(4, DK, DK),
            columns(tall, 256),
            columns(tall, 256),
            columns(tall, 256),
            lead(8, DK),
        ),
        4_000_000_000,
        "delta_back_local",
    )(qkv, factors, states, fresh, mixed, heads_grad, gain_head)
    adjoints = scan_adjoints(every, start_grad.reshape(H, DK, DK))

    grad_down = jnp.einsum("nf,nd->fd", hidden, g_both, preferred_element_type=F32).astype(BF16)
    down_sum = scatter_chips(grad_down[:, : D // 2], grad_down[:, D // 2 :])
    own_down = down_sum.transpose(1, 0, 2).reshape(frows, D)
    grad_gate = jnp.einsum("nd,nf->df", normed_two, gate_grad, preferred_element_type=F32)
    grad_up = jnp.einsum("nd,nf->df", normed_two, up_grad, preferred_element_type=F32)
    low_cols = lax.dynamic_slice_in_dim(middle_low, core * 512, 512, 1)
    grad_out = jnp.einsum("nd,ne->de", heads, low_cols, preferred_element_type=F32)
    gu_sum = scatter_chips(
        jnp.concatenate([grad_gate.astype(BF16), grad_out[:, :256].astype(BF16)], axis=1),
        jnp.concatenate([grad_up.astype(BF16), grad_out[:, 256:].astype(BF16)], axis=1),
    )
    gu_own = own_rows(gu_sum, core)
    own_gu = (
        gu_own[..., : FF // 2]
        .reshape(2, 2, drows, chips, frows)
        .transpose(2, 1, 3, 0, 4)
        .reshape(drows, 2 * FF)
    )
    own_out = gu_own[..., FF // 2 :].transpose(2, 0, 1, 3).reshape(drows, D)

    down_part = jnp.dot(hidden, w_down_mine, preferred_element_type=F32)
    output = (middle[:rows] + down_part[:rows]) + swap(down_part[rows:].astype(BF16)).astype(F32)
    output = output.astype(BF16).reshape(1, rows, D)

    ext_grad, conv_part, logit_low, bias_part = on_core(
        fourth_kernel,
        (
            sds((2, 2 * frame, 768), BF16),
            sds((2, CONV, 768), F32),
            sds((2, tall, DK), BF16),
            sds((2, 2, DK), F32),
        ),
        [
            lead(tall, 768),
            lead(2 * frame, 768),
            lead(CONV, 768),
            lead(tall, DK),
            lead(4, rows, rows),
            lead(4, rows, 2 * DK),
            quarter(),
            quarter(),
            columns(tall, 256),
            columns(tall, 256),
            columns(tall, 256),
            columns(tall, 256),
        ],
        (lead(2 * frame, 768), lead(CONV, 768), lead(tall, DK), lead(2, DK)),
        8_000_000_000,
        "delta_back",
    )(qkv, pre, conv_mine, rates, inverse, factors, states, adjoints, fresh, fresh_grad, query_grad, key_grad)
    ext_frames = ext_grad.reshape(2, 2, frame, 768)
    sent_back = lax.ppermute(
        ext_frames[:, :, :HALO], SEQ, [(i + 1, i) for i in range(seq_devices - 1)]
    )
    grad_q = jnp.einsum("nd,pnf->pdf", normed, ext_grad, preferred_element_type=F32).astype(BF16)
    q_sum = scatter_chips(grad_q[0], grad_q[1])
    q_own = own_rows(q_sum, core)
    own_qkv = (
        q_own.reshape(2, 2, drows, 3, 256).transpose(2, 3, 0, 1, 4).reshape(drows, 3 * D)
    )

    normed_tokens = normed.reshape(2, frame, D)[:, HALO:].reshape(tall, D)
    grad_beta = jnp.einsum(
        "nd,pnh->dph", normed_tokens, logit_low[:, :, :2], preferred_element_type=F32
    ).reshape(D, half)
    tail = ext_frames[:, :, frame - HALO :].astype(F32) + sent_back.astype(F32)
    pre_low = jnp.concatenate(
        [ext_frames[:, :, HALO : frame - HALO], tail.astype(BF16)], axis=2
    ).reshape(2, tall, 768)
    normed_part = (
        jnp.einsum("nf,df->nd", pre_low[0], w_q[0], preferred_element_type=F32)
        + jnp.einsum("nf,df->nd", pre_low[1], w_q[1], preferred_element_type=F32)
        + jnp.einsum("pnh,pdh->nd", logit_low, beta_pairs, preferred_element_type=F32)
    )
    normed_grad = normed_part[:rows] + swap(normed_part[rows:].astype(BF16)).astype(F32)
    x32 = x_both[:rows]
    scale_one = lax.rsqrt(jnp.mean(x32 * x32, axis=-1, keepdims=True) + EPS)
    unit_one = x32 * scale_one
    grad_norm1 = jnp.sum(normed_grad * unit_one, axis=0)
    inner_one = normed_grad * gain_one
    grad_input = middle_grad[:rows] + scale_one * (
        inner_one - unit_one * jnp.mean(inner_one * unit_one, axis=-1, keepdims=True)
    )
    grad_input = grad_input.reshape(1, rows, D)

    beta_full = jnp.where(
        first,
        jnp.pad(grad_beta, ((0, 0), (0, half))),
        jnp.pad(grad_beta, ((0, 0), (half, 0))),
    )
    conv_cols = conv_part.reshape(2, CONV, 3, 256).transpose(2, 0, 3, 1).reshape(3, 512, CONV)
    conv_full = jnp.where(
        first,
        jnp.pad(conv_cols, ((0, 0), (0, 512), (0, 0))),
        jnp.pad(conv_cols, ((0, 0), (512, 0), (0, 0))),
    )
    bias_heads = bias_part[:, :, :2].transpose(1, 0, 2).reshape(2, half)
    bias_heads = jnp.where(
        first,
        jnp.pad(bias_heads, ((0, 0), (0, half))),
        jnp.pad(bias_heads, ((0, 0), (half, 0))),
    )
    bias_grad = jnp.sum(choose_both[:, :, None] * bias_heads[:, None, :], axis=0)
    head_grad = gain_part[0, 0] + gain_part[1, 0]
    pack = jnp.concatenate(
        [
            grad_norm1,
            grad_norm2,
            beta_full.reshape(-1),
            conv_full.reshape(-1),
            bias_grad.reshape(-1),
            head_grad,
        ]
    )
    pack = jnp.pad(pack, (0, -pack.shape[0] % 1024)).reshape(-1, DK)
    pack = reduce_small(pack).reshape(-1)
    me = lax.axis_index(ALL)
    at = 2 * D
    own_g1 = lax.dynamic_slice_in_dim(pack[:D], me * drows, drows)
    own_g2 = lax.dynamic_slice_in_dim(pack[D:at], me * drows, drows)
    own_beta = lax.dynamic_slice_in_dim(
        pack[at : at + D * H].reshape(D, H), me * drows, drows
    )
    at += D * H
    own_conv = lax.dynamic_slice_in_dim(
        pack[at : at + 3 * D * CONV].reshape(3 * D, CONV), me * grows, grows
    )
    at += 3 * D * CONV
    bias_total = pack[at : at + NDOM * H].reshape(NDOM, H)
    at += NDOM * H
    gain_total = pack[at : at + DK]
    return (
        output,
        grad_input,
        own_g1,
        own_qkv,
        own_beta,
        own_conv,
        bias_total,
        gain_total,
        own_out,
        own_g2,
        own_gu,
        own_down,
    )


def solution(mesh):
    seq, batch = mesh.shape["seq"], mesh.shape["batch"]
    fine = Mesh(mesh.devices.reshape(seq // 2, 2, batch // 2, 2), ALL)
    tokens = P(("x", "core"), ("z", "y"), None)
    rows = P(ALL, None)
    vector = P(ALL)
    return jax.shard_map(
        shards,
        mesh=fine,
        in_specs=(
            tokens,
            P(("x", "core")),
            vector,
            rows,
            rows,
            rows,
            P(),
            P(),
            rows,
            vector,
            rows,
            rows,
            tokens,
        ),
        out_specs=(
            tokens,
            tokens,
            vector,
            rows,
            rows,
            rows,
            P(),
            P(),
            rows,
            vector,
            rows,
            rows,
        ),
        check_vma=False,
    )
```

```python
import functools

import jax
import jax.numpy as jnp
from jax import lax
from jax.experimental import pallas as pl
from jax.experimental.pallas import tpu as pltpu
from jax.sharding import Mesh
from jax.sharding import PartitionSpec as P

D = 1024
H = 8
DK = 128
FF = 2816
CONV = 4
NDOM = 4
EPS = 1e-06
HALO = 16
F32 = jnp.float32
BF16 = jnp.bfloat16
SEQ = ("z", "y")
ALL = ("z", "y", "x", "core")
VMEM_LIMIT = 48 * 1024 * 1024


def swap(a):
    return lax.ppermute(a, "core", [(0, 1), (1, 0)])


def turned(a, axis, by):
    n = lax.axis_size(axis)
    return lax.ppermute(a, axis, [(i, (i + by) % n) for i in range(n)])


def after(a, *others):
    return lax.optimization_barrier((a, others))[0]


def in_place(parts, me):
    n = len(parts)
    if n == 2:
        first = me == 0
        return [jnp.where(first, *parts), jnp.where(first, *parts[::-1])]
    if n <= 4:
        return [lax.select_n((me - i) % n, *parts) for i in range(n)]
    back = parts[:0:-1] + parts[:1]
    wide = jnp.stack(back + back)
    return list(lax.dynamic_slice_in_dim(wide, n - 1 - me, n, axis=0))


def fetched(a, axis):
    return [a] + [turned(a, axis, k) for k in range(1, lax.axis_size(axis))]


def gather_axis(a, axis, dim):
    if lax.axis_size(axis) == 1:
        return jnp.expand_dims(a, dim)
    return jnp.stack(in_place(fetched(a, axis), lax.axis_index(axis)), axis=dim)


def sends(a, axis, dim):
    n, me = lax.axis_size(axis), lax.axis_index(axis)
    own = lax.dynamic_index_in_dim(a, me, dim, False)
    got = [
        turned(lax.dynamic_index_in_dim(a, (me + k) % n, dim, False), axis, k) for k in range(1, n)
    ]
    return own, got


def added(own, got):
    total = own.astype(F32)
    for part in got:
        total = total + part.astype(F32)
    return total


def stacked_near(parts):
    return jnp.stack([a[0] for a in parts]), jnp.stack([a[1] for a in parts])


def gather_near(one, two):
    return fetched(one, "x"), fetched(two, "y")


def gather_last(ones, twos):
    one = jnp.stack(in_place(ones, lax.axis_index("x")))
    two = jnp.stack(in_place(twos, lax.axis_index("y")))
    return fetched(one, "y"), fetched(two, "x")


def gather_end(ones, twos):
    one = jnp.stack(in_place(ones, lax.axis_index("y")))
    two = jnp.stack(in_place(twos, lax.axis_index("x")), axis=1)
    return one, two


def scatter_near(one, two):
    nz, ny, nx = (lax.axis_size(a) for a in ("z", "y", "x"))
    n = one.shape[-1]
    return (
        sends(one.reshape(nz, ny, nx, -1, n), "y", 1),
        sends(two.reshape(nz, ny, nx, -1, n), "x", 2),
    )


def scatter_mid(stage):
    one, two = (added(*s).astype(BF16) for s in stage)
    return sends(one, "x", 1), sends(two, "y", 1)


def scatter_far(stage):
    one, two = (added(*s).astype(BF16) for s in stage)
    return sends(jnp.stack([one, two], axis=1), "z", 0)


def scatter_first(total):
    nz, ny, nx = (lax.axis_size(a) for a in ("z", "y", "x"))
    return sends(total.reshape(nz, ny, nx, -1, total.shape[-1]), "z", 0)


def scatter_second(stage):
    total = added(*stage).astype(BF16)
    n = total.shape[-1] // 2
    return sends(total[..., :n], "x", 1), sends(total[..., n:], "y", 0)


def scatter_third(stage):
    one, two = (added(*s).astype(BF16) for s in stage)
    return sends(one, "y", 0), sends(two, "x", 0)


def core_pick(a, core):
    return (
        lax.dynamic_index_in_dim(a, core, 0, False),
        lax.dynamic_index_in_dim(a, 1 - core, 0, False),
    )


def chip_rows(mine, got, core):
    first = core == 0
    return jnp.concatenate(
        [jnp.where(first, mine, got), jnp.where(first, got, mine)], axis=-2
    )


def own_rows(total, core):
    k, both, n = total.shape
    parts = total.reshape(k, 2, both // 2, n).transpose(1, 0, 2, 3)
    mine, other = core_pick(parts, core)
    got = swap(other)
    first = core == 0
    return jnp.stack([jnp.where(first, mine, got), jnp.where(first, got, mine)], axis=0)


def sum_axis(a, axis):
    every = gather_axis(a, axis, 0)
    total = every[0]
    for k in range(1, every.shape[0]):
        total = total + every[k]
    return total


def dot1(a, b, dims=((1,), (0,))):
    return lax.dot_general(
        a.astype(BF16), b.astype(BF16), (dims, ((), ())), preferred_element_type=F32
    )


TN = ((0,), (0,))
NT = ((1,), (1,))


def split(a):
    high = a.astype(BF16)
    return high, (a - high.astype(F32)).astype(BF16)


def dot3(a, b):
    ah, al = split(a)
    bh, bl = split(b)
    return dot1(ah, bh) + (dot1(ah, bl) + dot1(al, bh))


def sigmoid(v):
    return 1.0 / (1.0 + jnp.exp(-v))


def grid_masks(n):
    i = lax.broadcasted_iota(jnp.int32, (n, n), 0)
    j = lax.broadcasted_iota(jnp.int32, (n, n), 1)
    return i, j


def unit_inverses(lowers, i, j):
    n = lowers[0].shape[0]
    level = jnp.where(i > j, i ^ j, 0)
    eye = jnp.where(i == j, 1.0, 0.0).astype(F32)
    highs = [a.astype(BF16) for a in lowers]
    lows = [(a - h.astype(F32)).astype(BF16) for a, h in zip(lowers, highs)]
    inverses = [eye - jnp.where(level == 1, a, 0.0) for a in lowers]
    size = 2
    while size < n:
        corner = (level >= size) & (level < 2 * size)
        lefts = [t.astype(BF16) for t in inverses]
        inner = [dot1(jnp.where(corner, h, jnp.zeros_like(h)), t) for h, t in zip(highs, lefts)]
        inverses = [t - dot1(b, c) for t, b, c in zip(inverses, lefts, inner)]
        size *= 2
    parts = [split(t) for t in inverses]
    rests = [
        eye - t - (dot1(h, th) + (dot1(h, tl) + dot1(lo, th)))
        for t, h, lo, (th, tl) in zip(inverses, highs, lows, parts)
    ]
    return [t + dot1(th, r) for t, (th, _), r in zip(inverses, parts, rests)]


def conv_of(ext, taps, rows):
    total = taps[0:1, :] * ext[HALO - 3 : HALO - 3 + rows]
    for i in range(1, CONV):
        total = total + taps[i : i + 1, :] * ext[HALO - 3 + i : HALO - 3 + i + rows]
    return total


def first_kernel(half, count, me_ref, *refs):
    parts, refs = refs[:count], refs[count:]
    if half == 0:
        x_ref, g_ref, beta_ref, cv_ref, bias_ref = refs[:5]
        n_ref, w_ref, pre_ref, qkv_ref, t_ref, wu_ref, pd_ref, b_ref, sem = refs[5:]
    else:
        n_ref, beta_ref, cv_ref, bias_ref = refs[:4]
        w_ref, pre_ref, qkv_ref, t_ref, wu_ref, pd_ref, b_ref, sem = refs[-8:]
    rows = qkv_ref.shape[1] // 2
    frame = rows + HALO
    copies = []
    for k, part in enumerate(parts):
        place = lax.rem(me_ref[half] + (count - k), count)
        inner = part.shape[0]
        for i in range(inner):
            to = w_ref.at[:, place, i] if half == 0 else w_ref.at[:, i, place]
            copies.append(pltpu.make_async_copy(part.at[i], to, sem.at[k * inner + i]))
            copies[-1].start()
    if half == 0:
        x = x_ref[...].astype(F32)
        scale = lax.rsqrt(jnp.mean(x * x, axis=-1, keepdims=True) + EPS)
        n_ref[...] = (x * scale * g_ref[...]).astype(BF16)
    normed = n_ref[...]
    for copy in copies:
        copy.wait()
    pre_ref[0] = dot1(normed, w_ref[...].reshape(D, 768)).astype(BF16)
    linear = dot1(normed, beta_ref[0])
    i, j = grid_masks(rows)
    keys, rights, lowers = [], [], []
    for q in range(2):
        rate = sigmoid(linear[q * frame + HALO : (q + 1) * frame] + bias_ref[0, q : q + 1, :])
        b_ref[0, q * rows : (q + 1) * rows, :] = rate
        ext = pre_ref[0, q * frame : (q + 1) * frame, :].astype(F32)
        conv = conv_of(ext, cv_ref[0], rows)
        act = conv * sigmoid(conv)
        for h in range(2):
            place = pl.ds(q * rows, rows)
            parts = []
            for kind in range(3):
                lane = (kind * 2 + h) * DK
                one = act[:, lane : lane + DK]
                if kind < 2:
                    one = one * lax.rsqrt(jnp.sum(one * one, axis=-1, keepdims=True) + EPS)
                if kind == 0:
                    one = one * DK ** (-0.5)
                one = one.astype(BF16)
                qkv_ref[0, place, lane : lane + DK] = one
                parts.append(one)
            key, value = parts[1], parts[2]
            col = rate[:, h : h + 1]
            keys.append(key)
            rights.append(jnp.concatenate([key, value], axis=1).astype(F32) * col)
            lowers.append(jnp.where(i > j, dot1(key, key, NT) * col, 0.0))
    inverses = unit_inverses(lowers, i, j)
    boths = [dot3(t, r) for t, r in zip(inverses, rights)]
    for p in range(4):
        t_ref[0, p] = inverses[p].astype(BF16)
        wu_ref[0, p] = boths[p].astype(BF16)
    for p in range(4):
        pd_ref[0, p] = dot1(keys[p], boths[p], TN).astype(BF16)


def state_kernel(pd_ref, s_ref):
    count = pd_ref.shape[0]
    state = jnp.zeros((DK, DK), F32)
    for s in range(count):
        s_ref[s] = state.astype(BF16)
        if s + 1 < count:
            high, low = split(state)
            move = pd_ref[s, :, :DK]
            state = state - (dot1(move, high) + dot1(move, low)) + pd_ref[s, :, DK:].astype(F32)


def adjoint_kernel(pd_ref, g_ref, l_ref):
    count = pd_ref.shape[0]
    adjoint = jnp.zeros((DK, DK), F32)
    for s in range(count - 1, -1, -1):
        l_ref[s] = adjoint.astype(BF16)
        if s > 0:
            high, low = split(adjoint)
            move = pd_ref[s, :, :DK]
            adjoint = (
                adjoint - (dot1(move, high, TN) + dot1(move, low, TN)) + g_ref[s].astype(F32)
            )


def pair_places(rows):
    return [
        (q * 2 + h, pl.ds(q * rows, rows), pl.ds(h * DK, DK), h) for q in range(2) for h in range(2)
    ]


def kind_lanes(kind, h):
    return pl.ds((kind * 2 + h) * DK, DK)


def second_kernel(qkv_ref, wu_ref, s_ref, hg_ref, f_ref, m_ref, h_ref):
    rows = qkv_ref.shape[1] // 2
    i, j = grid_masks(rows)
    pairs = pair_places(rows)
    queries = [qkv_ref[0, at, kind_lanes(0, h)] for _, at, _, h in pairs]
    keys = [qkv_ref[0, at, kind_lanes(1, h)] for _, at, _, h in pairs]
    scores = [jnp.where(i >= j, dot1(a, b, NT), 0.0).astype(BF16) for a, b in zip(queries, keys)]
    freshes = [
        (wu_ref[0, p, :, DK:].astype(F32) - dot1(wu_ref[0, p, :, :DK], s_ref[p])).astype(BF16)
        for p, _, _, _ in pairs
    ]
    mixes = [
        dot1(queries[p], s_ref[p]) + dot1(scores[p], freshes[p]) for p, _, _, _ in pairs
    ]
    for p, at, lanes, _ in pairs:
        mixed = mixes[p]
        scale = lax.rsqrt(jnp.mean(mixed * mixed, axis=-1, keepdims=True) + EPS)
        f_ref[at, lanes] = freshes[p]
        m_ref[at, lanes] = mixed
        h_ref[at, lanes] = (mixed * scale * hg_ref[...]).astype(BF16)


def third_kernel(qkv_ref, wu_ref, s_ref, f_ref, m_ref, dh_ref, hg_ref, sg_ref, gf_ref, gq_ref, gk_ref, ghg_ref):
    rows = qkv_ref.shape[1] // 2
    i, j = grid_masks(rows)
    gain = hg_ref[...]
    gain_grad = jnp.zeros((1, DK), F32)
    pairs = pair_places(rows)
    queries = [qkv_ref[0, at, kind_lanes(0, h)] for _, at, _, h in pairs]
    keys = [qkv_ref[0, at, kind_lanes(1, h)] for _, at, _, h in pairs]
    scores = [jnp.where(i >= j, dot1(a, b, NT), 0.0).astype(BF16) for a, b in zip(queries, keys)]
    grads = []
    for _, at, lanes, _ in pairs:
        mixed = m_ref[at, lanes]
        up = dh_ref[at, lanes].astype(F32)
        scale = lax.rsqrt(jnp.mean(mixed * mixed, axis=-1, keepdims=True) + EPS)
        unit = mixed * scale
        gain_grad = gain_grad + jnp.sum(up * unit, axis=0, keepdims=True)
        inner = up * gain
        grad = scale * (inner - unit * jnp.mean(inner * unit, axis=-1, keepdims=True))
        grads.append(grad.astype(BF16))
    ghg_ref[0] = jnp.broadcast_to(gain_grad, ghg_ref.shape[1:])
    fresh_grads = [dot1(a, g, TN) for a, g in zip(scores, grads)]
    starts = [
        dot1(queries[p], grads[p], TN) - dot1(wu_ref[0, p, :, :DK], fresh_grads[p], TN)
        for p in range(4)
    ]
    score_grads = [
        jnp.where(i >= j, dot1(grads[p], f_ref[at, lanes], NT), 0.0).astype(BF16)
        for p, at, lanes, _ in pairs
    ]
    for p, at, lanes, _ in pairs:
        gf_ref[at, lanes] = fresh_grads[p]
        sg_ref[0, p] = starts[p].astype(BF16)
        gq_ref[at, lanes] = dot1(grads[p], s_ref[p], NT) + dot1(score_grads[p], keys[p])
        gk_ref[at, lanes] = dot1(score_grads[p], queries[p], TN)


def fourth_kernel(qkv_ref, pre_ref, cv_ref, b_ref, t_ref, wu_ref, s_ref, l_ref, f_ref, gf_ref, gq_ref, gk_ref, eg_ref, gc_ref, lg_ref, gb_ref):
    rows = qkv_ref.shape[1] // 2
    frame = rows + HALO
    i, j = grid_masks(rows)
    lane = lax.broadcasted_iota(jnp.int32, (rows, DK), 1)
    pairs = pair_places(rows)
    keys = [qkv_ref[0, at, kind_lanes(1, h)] for _, at, _, h in pairs]
    values = [qkv_ref[0, at, kind_lanes(2, h)] for _, at, _, h in pairs]
    cols = [b_ref[0, at, h : h + 1] for _, at, _, h in pairs]
    fresh_grads = [
        gf_ref[at, lanes] + dot1(keys[p], l_ref[p]) for p, at, lanes, _ in pairs
    ]
    lows = [g.astype(BF16) for g in fresh_grads]
    factor_grads = [
        jnp.concatenate([-dot1(lows[p], s_ref[p], NT).astype(BF16), lows[p]], axis=1)
        for p in range(4)
    ]
    solved = [dot1(t_ref[0, p], factor_grads[p], TN) for p in range(4)]
    inners = [dot1(k, k, NT) for k in keys]
    system_grads = [
        jnp.where(i > j, -dot1(solved[p], wu_ref[0, p], NT), 0.0) for p in range(4)
    ]
    inner_grads = [(g * c).astype(BF16) for g, c in zip(system_grads, cols)]
    key_grads = [
        gk_ref[at, lanes]
        + dot1(f_ref[at, lanes], l_ref[p], NT)
        + cols[p] * solved[p][:, :DK]
        + dot1(inner_grads[p], keys[p])
        + dot1(inner_grads[p], keys[p], TN)
        for p, at, lanes, _ in pairs
    ]
    rate_grads = [
        (
            jnp.sum(
                solved[p][:, :DK] * keys[p].astype(F32) + solved[p][:, DK:] * values[p].astype(F32),
                axis=-1,
                keepdims=True,
            )
            + jnp.sum(system_grads[p] * inners[p], axis=-1, keepdims=True)
        )
        * cols[p]
        * (1.0 - cols[p])
        for p in range(4)
    ]
    for q in range(2):
        place = pl.ds(q * rows, rows)
        logit = jnp.where(
            lane == 0, rate_grads[2 * q], jnp.where(lane == 1, rate_grads[2 * q + 1], 0.0)
        )
        lg_ref[0, place, :] = logit.astype(BF16)
        gb_ref[0, q : q + 1, :] = jnp.sum(logit, axis=0, keepdims=True)
    zero = jnp.zeros((HALO, DK), F32)
    for kind in range(3):
        for h in range(2):
            at = kind_lanes(kind, h)
            tap = cv_ref[0, :, at]
            conv_grad = [jnp.zeros((1, DK), F32) for _ in range(CONV)]
            for q in range(2):
                p = q * 2 + h
                ext = pre_ref[0, q * frame : (q + 1) * frame, at].astype(F32)
                views = [ext[HALO - 3 + t : HALO - 3 + t + rows] for t in range(CONV)]
                conv = tap[0:1, :] * views[0]
                for t in range(1, CONV):
                    conv = conv + tap[t : t + 1, :] * views[t]
                sig = sigmoid(conv)
                act = conv * sig
                if kind == 0:
                    grad = gq_ref[q * rows : (q + 1) * rows, h * DK : (h + 1) * DK] * DK ** (-0.5)
                elif kind == 1:
                    grad = key_grads[p]
                else:
                    grad = cols[p] * solved[p][:, DK:]
                if kind < 2:
                    scale = lax.rsqrt(jnp.sum(act * act, axis=-1, keepdims=True) + EPS)
                    unit = act * scale
                    grad = scale * (grad - unit * jnp.sum(grad * unit, axis=-1, keepdims=True))
                grad = grad * (sig * (1.0 + conv * (1.0 - sig)))
                wide = jnp.concatenate([zero, grad, zero], axis=0)
                total = tap[0:1, :] * wide[3 : 3 + frame]
                for t in range(1, CONV):
                    total = total + tap[t : t + 1, :] * wide[3 - t : 3 - t + frame]
                eg_ref[0, q * frame : (q + 1) * frame, at] = total.astype(BF16)
                for t in range(CONV):
                    conv_grad[t] = conv_grad[t] + jnp.sum(grad * views[t], axis=0, keepdims=True)
            for t in range(CONV):
                gc_ref[0, t : t + 1, at] = conv_grad[t]


def lead(*shape):
    return pl.BlockSpec((1,) + shape, lambda p: (p,) + (0,) * len(shape))


def at_half(half, *shape):
    return pl.BlockSpec((1,) + shape, lambda p: (half,) + (0,) * len(shape))


def whole(*shape):
    return pl.BlockSpec(shape, lambda p: (0,) * len(shape))


def columns(rows, cols):
    return pl.BlockSpec((rows, cols), lambda p: (0, p))


def quarter():
    return pl.BlockSpec((4, DK, DK), lambda p: (p, 0, 0))


def cost(microseconds):
    return pl.CostEstimate(
        flops=int(microseconds * 1.15e9), bytes_accessed=0, transcendentals=0
    )


def on_core(kernel, outs, in_specs, out_specs, name, microseconds):
    return pl.pallas_call(
        kernel,
        out_shape=outs,
        grid=(2,),
        in_specs=in_specs,
        out_specs=out_specs,
        compiler_params=pltpu.CompilerParams(
            vmem_limit_bytes=VMEM_LIMIT, dimension_semantics=("arbitrary",)
        ),
        cost_estimate=cost(microseconds),
        name=name,
    )


def sds(shape, kind):
    return jax.ShapeDtypeStruct(shape, kind)


def all_ranges(a):
    if lax.axis_size("z") * lax.axis_size("y") == a.shape[0]:
        return lax.all_to_all(a, SEQ, 0, 0, tiled=True)
    return lax.all_gather(a, SEQ)


def scan_states(every):
    count = lax.axis_size("z") * lax.axis_size("y")
    if every.ndim == 3:
        return pl.pallas_call(
            state_kernel,
            out_shape=sds((count, DK, DK), BF16),
            cost_estimate=cost(3),
            name="state_scan",
        )(every)

    def step(s, state):
        one = lax.dynamic_index_in_dim(every, s, 0, False).astype(F32)
        moved = jnp.einsum(
            "pij,pjk->pik", one[:, :, :DK], state, precision=lax.Precision.HIGHEST
        )
        return state - moved + one[:, :, DK:]

    start = jnp.zeros((every.shape[1], DK, DK), F32)
    return lax.fori_loop(0, lax.axis_index(SEQ), step, start).astype(BF16)


def scan_adjoints(every, grads):
    count = lax.axis_size("z") * lax.axis_size("y")
    if every.ndim == 3:
        return pl.pallas_call(
            adjoint_kernel,
            out_shape=sds((count, DK, DK), BF16),
            cost_estimate=cost(3),
            name="adjoint_scan",
        )(every, grads)

    def step(k, adjoint):
        s = count - 1 - k
        one = lax.dynamic_index_in_dim(every, s, 0, False).astype(F32)
        moved = jnp.einsum(
            "pji,pjk->pik", one[:, :, :DK], adjoint, precision=lax.Precision.HIGHEST
        )
        return adjoint - moved + lax.dynamic_index_in_dim(grads, s, 0, False).astype(F32)

    start = jnp.zeros((every.shape[1], DK, DK), F32)
    steps = count - 1 - lax.axis_index(SEQ)
    return lax.fori_loop(0, steps, step, start).astype(BF16)


def own_range(a):
    if lax.axis_size("z") * lax.axis_size("y") == H:
        return lax.all_to_all(a, SEQ, 0, 0, tiled=True)
    return a


def shards(
    inputs,
    domain_ids,
    norm1_gain,
    w_qkv,
    w_beta,
    conv_weight,
    domain_bias,
    head_gain,
    w_out,
    norm2_gain,
    w_gate_up,
    w_down,
    cotangent,
):
    core = lax.axis_index("core")
    nz, ny, nx = (lax.axis_size(a) for a in ("z", "y", "x"))
    z, y, x = (lax.axis_index(a) for a in ("z", "y", "x"))
    chips = nz * ny * nx
    seq_devices = nz * ny
    rows = inputs.shape[1]
    frame = rows + HALO
    tall = 2 * rows
    drows = w_qkv.shape[0]
    both_rows = 2 * drows
    frows = w_down.shape[0]
    grows = conv_weight.shape[0]
    first = core == 0
    half = H // 2
    fence = lax.optimization_barrier

    q_mine, q_other = core_pick(
        w_qkv.reshape(drows, 3, 2, 2, 256).transpose(2, 3, 0, 1, 4).reshape(2, 2, drows, 768), core
    )
    q_got = swap(q_other)
    small = jnp.concatenate(
        [norm1_gain, norm2_gain, w_beta.reshape(-1), conv_weight.reshape(-1)]
    )
    n_small = small.shape[0]
    small = jnp.pad(small, (0, 768 - n_small)).reshape(1, 768)
    small_got = swap(small)
    x_own = inputs.reshape(rows, D)
    halo = lax.ppermute(
        x_own[rows - HALO :], SEQ, [(i, i + 1) for i in range(seq_devices - 1)]
    )
    small = jnp.stack([jnp.where(first, small, small_got), jnp.where(first, small_got, small)])
    small = jnp.pad(small, ((0, 0), (0, 7), (0, 0)))
    q_part = jnp.concatenate([chip_rows(q_mine, q_got, core), small], axis=1)
    q_part, halo, x_own, w_gate_up, w_out, w_down, cotangent = fence(
        (q_part, halo, x_own, w_gate_up, w_out, w_down, cotangent)
    )

    q_far = fetched(q_part, "z")
    down_ones, down_twos = gather_last(
        *gather_near(w_down[:, : D // 2], w_down[:, D // 2 :])
    )
    out_cols = w_out.reshape(drows, 2, 2, 256).transpose(1, 2, 0, 3)
    gu_cols = (
        w_gate_up.reshape(drows, 2, chips, 2, frows)
        .transpose(3, 1, 0, 2, 4)
        .reshape(2, 2, drows, FF // 2)
    )
    gu_mine, gu_other = core_pick(jnp.concatenate([gu_cols, out_cols], axis=-1), core)
    gu_part = chip_rows(gu_mine, swap(gu_other), core)
    choose = (domain_ids[0] == jnp.arange(NDOM, dtype=jnp.int32)).astype(BF16)
    bias_own = jnp.sum(domain_bias.astype(F32) * choose.astype(F32)[:, None], axis=0)
    extra = jnp.pad(jnp.concatenate([bias_own.astype(BF16), choose]), (0, D - H - NDOM))
    extra = jnp.pad(extra.reshape(1, D), ((0, HALO - 1), (0, 0)))
    frame_own = jnp.concatenate([halo, x_own, extra], axis=0)
    frame_other = swap(frame_own)
    g_own = cotangent.reshape(rows, D)
    g_other = swap(g_own)
    q_far, gu_part, frame_own, frame_other, g_own, g_other = fence(
        (q_far, gu_part, frame_own, frame_other, g_own, g_other)
    )

    q_sorted = in_place(q_far, z)
    q_ones, q_twos = gather_near(*stacked_near([a[:, :both_rows] for a in q_sorted]))
    smalls = jnp.stack([a[:, both_rows] for a in q_sorted])
    smalls = gather_axis(gather_axis(smalls, "x", 1), "y", 1)
    ends = sorted({1, nz - 1})
    gu_ends = [turned(gu_part, "z", k) for k in ends]
    q_ones, q_twos, smalls, gu_part = fence((q_ones, q_twos, smalls, gu_part))

    q_ones, q_twos = gather_last(q_ones, q_twos)
    gu_far = [gu_part, gu_ends[0]]
    gu_far += [turned(gu_part, "z", k) for k in range(2, nz - 1)]
    gu_far += gu_ends[1:]
    smalls = smalls.reshape(2 * chips, 768)[:, :n_small]
    gain_one = smalls[:, :drows].reshape(1, D).astype(F32)
    gain_two = smalls[:, drows : 2 * drows].reshape(1, D).astype(F32)
    full_beta = smalls[:, 2 * drows : 2 * drows + drows * H].reshape(D, 2, half)
    full_conv = smalls[:, 2 * drows + drows * H :].reshape(3, 2, 2, 256, CONV)
    beta_mine = lax.dynamic_index_in_dim(full_beta, core, 1, False)
    conv_mine = (
        lax.dynamic_index_in_dim(full_conv, core, 1, False)
        .transpose(1, 3, 0, 2)
        .reshape(2, CONV, 768)
        .astype(F32)
    )
    beta_pairs = jnp.pad(
        beta_mine.reshape(D, 2, 2).transpose(1, 0, 2), ((0, 0), (0, 0), (0, DK - 2))
    )
    x_frames = jnp.concatenate([frame_own[:frame], frame_other[:frame]], axis=0)
    bias_both = jnp.stack([frame_own[frame, :H], frame_other[frame, :H]]).astype(F32)
    choose_both = jnp.stack(
        [frame_own[frame, H : H + NDOM], frame_other[frame, H : H + NDOM]]
    ).astype(F32)
    bias_mine = lax.dynamic_index_in_dim(bias_both.reshape(2, 2, half), core, 1, False)
    bias_pairs = jnp.pad(
        bias_mine.reshape(2, 2, 2).transpose(1, 0, 2), ((0, 0), (0, 0), (0, DK - 2))
    )
    x_both = jnp.concatenate(
        [frame_own[HALO:frame], frame_other[HALO:frame]], axis=0
    ).astype(F32)
    g_both = jnp.concatenate([g_own, g_other], axis=0)
    (
        q_ones,
        q_twos,
        gu_far,
        gain_one,
        gain_two,
        beta_pairs,
        conv_mine,
        bias_pairs,
        x_frames,
        x_both,
        g_both,
        down_ones,
        down_twos,
    ) = fence(
        (
            q_ones,
            q_twos,
            gu_far,
            gain_one,
            gain_two,
            beta_pairs,
            conv_mine,
            bias_pairs,
            x_frames,
            x_both,
            g_both,
            down_ones,
            down_twos,
        )
    )

    if both_rows % 16 == 0:
        w_shape = sds((nz, ny, nx, both_rows, 768), BF16)
    else:
        w_shape = sds((1, 1, 1, D, 768), BF16)
        q_ones, q_twos = (
            [a.transpose(2, 0, 1, 3, 4).reshape(1, 1, D, 768)] for a in gather_end(q_ones, q_twos)
        )
    place = jnp.stack([y, x]).astype(jnp.int32)
    kept = (
        sds((2, 2 * frame, 768), BF16),
        sds((2, tall, 768), BF16),
        sds((2, 4, rows, rows), BF16),
        sds((2, 4, rows, 2 * DK), BF16),
        sds((2, 4, DK, 2 * DK), BF16),
        sds((2, tall, DK), F32),
    )
    anywhere = pl.BlockSpec(memory_space=pl.ANY)

    def local(number, parts, ins, in_specs, outs, out_specs, held):
        fixed = [at_half(number, D, DK), at_half(number, CONV, 768), at_half(number, 2, DK)]
        first_held = 1 + len(parts) + len(ins) + 3
        return pl.pallas_call(
            functools.partial(first_kernel, number, len(parts)),
            out_shape=outs + (w_shape,) + kept,
            grid=(1,),
            in_specs=[pl.BlockSpec(memory_space=pltpu.SMEM)]
            + [anywhere] * len(parts)
            + in_specs
            + fixed
            + [anywhere] * len(held),
            out_specs=out_specs
            + (whole(*w_shape.shape),)
            + tuple(at_half(number, *k.shape[1:]) for k in kept),
            scratch_shapes=[pltpu.SemaphoreType.DMA((len(parts) * parts[0].shape[0],))],
            input_output_aliases={
                first_held + k: len(outs) + 1 + k for k in range(len(held))
            },
            compiler_params=pltpu.CompilerParams(vmem_limit_bytes=VMEM_LIMIT),
            cost_estimate=cost(10),
            name="delta_local",
        )(place, *parts, *ins, beta_pairs, conv_mine, bias_pairs, *held)

    gu_stacks = stacked_near(in_place(gu_far, z))
    gu_ones, gu_twos = gather_near(*gu_stacks)
    down_part = jnp.concatenate(gather_end(down_ones, down_twos), axis=-1)
    down_ends = [turned(down_part, "z", k) for k in ends]
    normed, w_q_one, *held = local(
        0,
        q_ones,
        (after(x_frames, gu_stacks, down_part), gain_one),
        [whole(2 * frame, D), whole(1, D)],
        (sds((2 * frame, D), BF16),),
        (whole(2 * frame, D),),
        (),
    )
    w_q_two, *held = local(
        1,
        q_twos,
        (normed,),
        [whole(2 * frame, D)],
        (),
        (),
        tuple(held),
    )
    pre, qkv, inverse, factors, pd, rates = held
    w_q_one = w_q_one.reshape(D, 768)
    w_q_two = w_q_two.reshape(D, 768)
    (
        normed,
        w_q_one,
        w_q_two,
        pre,
        qkv,
        inverse,
        factors,
        pd,
        rates,
        gu_ones,
        gu_twos,
        down_part,
        down_ends[0],
    ) = fence(
        (
            normed,
            w_q_one,
            w_q_two,
            pre,
            qkv,
            inverse,
            factors,
            pd,
            rates,
            gu_ones,
            gu_twos,
            down_part,
            down_ends[0],
        )
    )

    every = all_ranges(pd.reshape(H, DK, 2 * DK))
    gu_ones, gu_twos = gather_last(gu_ones, gu_twos)
    every, down_ends = fence((every, down_ends))

    states = scan_states(every)
    down_part = after(down_part, states)
    down_far = [down_part, down_ends[0]]
    down_far += [turned(down_part, "z", k) for k in range(2, nz - 1)]
    down_far += down_ends[1:]
    states = own_range(states)
    gain_head = head_gain.astype(F32).reshape(1, DK)
    fresh, mixed, heads_mine = on_core(
        second_kernel,
        (sds((tall, 512), BF16), sds((tall, 512), F32), sds((tall, 512), BF16)),
        [lead(tall, 768), lead(4, rows, 2 * DK), quarter(), whole(1, DK)],
        (columns(tall, 256), columns(tall, 256), columns(tall, 256)),
        "delta_mix",
        2,
    )(qkv, factors, states, gain_head)
    heads_got = swap(heads_mine)
    gu_ones, gu_twos, down_far, states, fresh, mixed, heads_mine, heads_got = fence(
        (gu_ones, gu_twos, down_far, states, fresh, mixed, heads_mine, heads_got)
    )

    gu_one, gu_two = (
        a.transpose(2, 0, 1, 3, 4).reshape(D, -1) for a in gather_end(gu_ones, gu_twos)
    )
    w_gate, w_up = gu_one[:, : FF // 2], gu_two[:, : FF // 2]
    out_mine = jnp.concatenate([gu_one[:, FF // 2 :], gu_two[:, FF // 2 :]], axis=1)
    out_got = swap(out_mine)
    full_out = jnp.concatenate(
        [jnp.where(first, out_mine, out_got), jnp.where(first, out_got, out_mine)], axis=1
    )
    heads_got = jnp.concatenate([heads_got[rows:], heads_got[:rows]], axis=0)
    heads = jnp.concatenate(
        [jnp.where(first, heads_mine, heads_got), jnp.where(first, heads_got, heads_mine)], axis=1
    )
    middle = x_both + jnp.dot(heads, full_out, preferred_element_type=F32)
    scale_two = lax.rsqrt(jnp.mean(middle * middle, axis=-1, keepdims=True) + EPS)
    unit_two = middle * scale_two
    normed_two = (unit_two * gain_two).astype(BF16)
    gate = jnp.dot(normed_two, w_gate, preferred_element_type=F32)
    up = jnp.dot(normed_two, w_up, preferred_element_type=F32)
    w_down_mine = jnp.stack(in_place(after(down_far, gate, up), z)).reshape(chips * frows, D)
    sig = jax.nn.sigmoid(gate)
    hidden = (gate * sig * up).astype(BF16)
    hidden_grad = jnp.einsum("nd,fd->nf", g_both, w_down_mine, preferred_element_type=F32)
    up_grad = (hidden_grad * gate * sig).astype(BF16)
    gate_grad = (hidden_grad * up * sig * (1.0 + gate * (1.0 - sig))).astype(BF16)
    hidden, up_grad, gate_grad = fence((hidden, up_grad, gate_grad))

    normed_two_part = jnp.einsum(
        "nf,df->nd", gate_grad, w_gate, preferred_element_type=F32
    ) + jnp.einsum("nf,df->nd", up_grad, w_up, preferred_element_type=F32)
    part_low = normed_two_part.astype(BF16)
    part_got = swap(part_low)
    grad_down = jnp.einsum(
        "nf,nd->fd", after(hidden, part_low), g_both, preferred_element_type=F32
    ).astype(BF16)
    down_stage = scatter_near(grad_down[:, : D // 2], grad_down[:, D // 2 :])
    rows_two = after(normed_two, grad_down)
    grad_gate = jnp.einsum("nd,nf->df", rows_two, gate_grad, preferred_element_type=F32)
    grad_up = jnp.einsum("nd,nf->df", rows_two, up_grad, preferred_element_type=F32)
    grad_gate, grad_up = grad_gate.astype(BF16), grad_up.astype(BF16)
    part_got = after(part_got, grad_gate, grad_up)
    part_got = jnp.concatenate([part_got[rows:], part_got[:rows]], axis=0)
    normed_two_grad = normed_two_part + part_got.astype(F32)
    grad_norm2 = jnp.sum(normed_two_grad[:rows] * unit_two[:rows], axis=0)
    inner = normed_two_grad * gain_two
    middle_grad = g_both.astype(F32) + scale_two * (
        inner - unit_two * jnp.mean(inner * unit_two, axis=-1, keepdims=True)
    )
    middle_low = middle_grad.astype(BF16)
    out_rows = lax.dynamic_slice_in_dim(full_out, core * 512, 512, 0)
    heads_grad = jnp.einsum("ne,de->nd", middle_low, out_rows, preferred_element_type=F32)
    start_grad, fresh_grad, query_grad, key_grad, gain_part = on_core(
        third_kernel,
        (
            sds((2, 4, DK, DK), BF16),
            sds((tall, 512), F32),
            sds((tall, 512), F32),
            sds((tall, 512), F32),
            sds((2, 8, DK), F32),
        ),
        [
            lead(tall, 768),
            lead(4, rows, 2 * DK),
            quarter(),
            columns(tall, 256),
            columns(tall, 256),
            columns(tall, 256),
            whole(1, DK),
        ],
        (
            lead(4, DK, DK),
            columns(tall, 256),
            columns(tall, 256),
            columns(tall, 256),
            lead(8, DK),
        ),
        "delta_back_local",
        5,
    )(qkv, factors, states, fresh, mixed, heads_grad, gain_head)
    (
        start_grad,
        fresh_grad,
        query_grad,
        key_grad,
        gain_part,
        down_stage,
        grad_gate,
        grad_up,
        grad_norm2,
        middle_grad,
        middle_low,
        hidden,
    ) = fence(
        (
            start_grad,
            fresh_grad,
            query_grad,
            key_grad,
            gain_part,
            down_stage,
            grad_gate,
            grad_up,
            grad_norm2,
            middle_grad[:rows],
            middle_low,
            hidden,
        )
    )

    start_grads = all_ranges(start_grad.reshape(H, DK, DK))
    down_stage = scatter_mid(down_stage)
    gu_stage = scatter_near(grad_gate, grad_up)
    low_cols = lax.dynamic_slice_in_dim(middle_low, core * 512, 512, 1)
    grad_out = jnp.einsum("nd,ne->de", heads, low_cols, preferred_element_type=F32).astype(BF16)
    adjoints = scan_adjoints(every, start_grads)
    gu_stage = scatter_mid(after(gu_stage, adjoints))
    adjoints = own_range(adjoints)
    down_part = jnp.dot(hidden, w_down_mine, preferred_element_type=F32)
    output = (middle[:rows] + down_part[:rows]) + swap(down_part[rows:].astype(BF16)).astype(F32)
    output = output.astype(BF16).reshape(1, rows, D)
    adjoints = after(adjoints, gu_stage[0][0], gu_stage[1][0], grad_out, output)
    down_stage = scatter_far(after(down_stage, adjoints))
    out_stage = scatter_first(after(grad_out, adjoints))
    adjoints = after(adjoints, down_stage[0], out_stage[0])
    ext_grad, conv_part, logit_low, bias_part = on_core(
        fourth_kernel,
        (
            sds((2, 2 * frame, 768), BF16),
            sds((2, CONV, 768), F32),
            sds((2, tall, DK), BF16),
            sds((2, 2, DK), F32),
        ),
        [
            lead(tall, 768),
            lead(2 * frame, 768),
            lead(CONV, 768),
            lead(tall, DK),
            lead(4, rows, rows),
            lead(4, rows, 2 * DK),
            quarter(),
            quarter(),
            columns(tall, 256),
            columns(tall, 256),
            columns(tall, 256),
            columns(tall, 256),
        ],
        (lead(2 * frame, 768), lead(CONV, 768), lead(tall, DK), lead(2, DK)),
        "delta_back",
        15,
    )(qkv, pre, conv_mine, rates, inverse, factors, states, adjoints, fresh, fresh_grad, query_grad, key_grad)
    ext_grad, conv_part, logit_low, bias_part, gu_stage, down_stage, out_stage = fence(
        (ext_grad, conv_part, logit_low, bias_part, gu_stage, down_stage, out_stage)
    )

    ext_frames = ext_grad.reshape(2, 2, frame, 768)
    grad_q = [
        jnp.einsum("nd,nf->df", normed, e, preferred_element_type=F32).astype(BF16)
        for e in (ext_grad[0], ext_grad[1])
    ]
    q_stage = scatter_near(*grad_q)
    ext_frames = after(ext_frames, grad_q)
    sent_back = lax.ppermute(
        ext_frames[:, :, :HALO], SEQ, [(i + 1, i) for i in range(seq_devices - 1)]
    )
    gu_stage = scatter_far(gu_stage)
    out_stage = scatter_second(after(out_stage, grad_q))
    tail = ext_frames[:, :, frame - HALO :].astype(F32) + sent_back.astype(F32)
    pre_low = jnp.concatenate(
        [ext_frames[:, :, HALO : frame - HALO], tail.astype(BF16)], axis=2
    ).reshape(2, tall, 768)
    normed_part = (
        jnp.einsum("nf,df->nd", pre_low[0], w_q_one, preferred_element_type=F32)
        + jnp.einsum("nf,df->nd", pre_low[1], w_q_two, preferred_element_type=F32)
        + jnp.einsum("pnh,pdh->nd", logit_low, beta_pairs, preferred_element_type=F32)
    )
    normed_grad = normed_part[:rows] + swap(normed_part[rows:].astype(BF16)).astype(F32)
    normed_tokens = normed.reshape(2, frame, D)[:, HALO:].reshape(tall, D)
    grad_beta = jnp.einsum(
        "nd,pnh->dph", normed_tokens, logit_low[:, :, :2], preferred_element_type=F32
    ).reshape(D, half)
    q_stage, out_stage, normed_grad, grad_beta, x_both = fence(
        (q_stage, out_stage, normed_grad, grad_beta, x_both)
    )

    q_stage = scatter_mid(q_stage)
    out_stage = scatter_third(out_stage)
    x32 = x_both[:rows]
    scale_one = lax.rsqrt(jnp.mean(x32 * x32, axis=-1, keepdims=True) + EPS)
    unit_one = x32 * scale_one
    grad_norm1 = jnp.sum(normed_grad * unit_one, axis=0)
    inner_one = normed_grad * gain_one
    grad_input = middle_grad + scale_one * (
        inner_one - unit_one * jnp.mean(inner_one * unit_one, axis=-1, keepdims=True)
    )
    grad_input = grad_input.reshape(1, rows, D)
    beta_full = jnp.where(
        first,
        jnp.pad(grad_beta, ((0, 0), (0, half))),
        jnp.pad(grad_beta, ((0, 0), (half, 0))),
    )
    conv_cols = conv_part.reshape(2, CONV, 3, 256).transpose(2, 0, 3, 1).reshape(3, 512, CONV)
    conv_full = jnp.where(
        first,
        jnp.pad(conv_cols, ((0, 0), (0, 512), (0, 0))),
        jnp.pad(conv_cols, ((0, 0), (512, 0), (0, 0))),
    )
    bias_heads = bias_part[:, :, :2].transpose(1, 0, 2).reshape(2, half)
    bias_heads = jnp.where(
        first,
        jnp.pad(bias_heads, ((0, 0), (0, half))),
        jnp.pad(bias_heads, ((0, 0), (half, 0))),
    )
    bias_grad = jnp.sum(choose_both[:, :, None] * bias_heads[:, None, :], axis=0)
    head_grad = gain_part[0, 0] + gain_part[1, 0]
    pack = jnp.concatenate(
        [
            grad_norm1,
            grad_norm2,
            beta_full.reshape(-1),
            conv_full.reshape(-1),
            bias_grad.reshape(-1),
            head_grad,
        ]
    )
    pack = jnp.pad(pack, (0, -pack.shape[0] % 1024)).reshape(-1, DK)
    pack = sum_axis(pack + swap(pack), "x")
    q_stage, gu_stage, out_stage, pack, grad_input = fence(
        (q_stage, gu_stage, out_stage, pack, grad_input)
    )

    q_stage = scatter_far(q_stage)
    pack = sum_axis(pack, "y")
    gu_own = own_rows(added(*gu_stage), core)
    own_gu = (
        gu_own.reshape(2, 2, drows, chips, frows).transpose(2, 1, 3, 0, 4).reshape(drows, 2 * FF)
    )
    own_down = added(*down_stage).transpose(1, 0, 2).reshape(frows, D)
    out_total = jnp.concatenate([added(*s) for s in out_stage], axis=-1)
    out_own = own_rows(out_total.reshape(1, both_rows, D // 2), core)
    own_out = out_own.transpose(2, 0, 1, 3).reshape(drows, D)
    q_stage, pack, own_gu, own_down, own_out = fence((q_stage, pack, own_gu, own_down, own_out))

    pack = sum_axis(pack, "z").reshape(-1)
    q_own = own_rows(added(*q_stage), core)
    own_qkv = (
        q_own.reshape(2, 2, drows, 3, 256).transpose(2, 3, 0, 1, 4).reshape(drows, 3 * D)
    )
    me = lax.axis_index(ALL)
    at = 2 * D
    own_g1 = lax.dynamic_slice_in_dim(pack[:D], me * drows, drows)
    own_g2 = lax.dynamic_slice_in_dim(pack[D:at], me * drows, drows)
    own_beta = lax.dynamic_slice_in_dim(
        pack[at : at + D * H].reshape(D, H), me * drows, drows
    )
    at += D * H
    own_conv = lax.dynamic_slice_in_dim(
        pack[at : at + 3 * D * CONV].reshape(3 * D, CONV), me * grows, grows
    )
    at += 3 * D * CONV
    bias_total = pack[at : at + NDOM * H].reshape(NDOM, H)
    at += NDOM * H
    gain_total = pack[at : at + DK]
    return (
        output,
        grad_input,
        own_g1,
        own_qkv,
        own_beta,
        own_conv,
        bias_total,
        gain_total,
        own_out,
        own_g2,
        own_gu,
        own_down,
    )


def solution(mesh):
    seq, batch = mesh.shape["seq"], mesh.shape["batch"]
    fine = Mesh(mesh.devices.reshape(seq // 2, 2, batch // 2, 2), ALL)
    tokens = P(("x", "core"), ("z", "y"), None)
    rows = P(ALL, None)
    vector = P(ALL)
    return jax.shard_map(
        shards,
        mesh=fine,
        in_specs=(
            tokens,
            P(("x", "core")),
            vector,
            rows,
            rows,
            rows,
            P(),
            P(),
            rows,
            vector,
            rows,
            rows,
            tokens,
        ),
        out_specs=(
            tokens,
            tokens,
            vector,
            rows,
            rows,
            rows,
            P(),
            P(),
            rows,
            vector,
            rows,
            rows,
        ),
        check_vma=False,
    )
```

```python
import functools

import jax
import jax.numpy as jnp
from jax import lax
from jax.experimental import pallas as pl
from jax.experimental.pallas import tpu as pltpu
from jax.sharding import Mesh
from jax.sharding import PartitionSpec as P

D = 1024
H = 8
DK = 128
FF = 2816
CONV = 4
NDOM = 4
EPS = 1e-06
HALO = 16
F32 = jnp.float32
BF16 = jnp.bfloat16
SEQ = ("z", "y")
ALL = ("z", "y", "x", "core")
VMEM_LIMIT = 60 * 1024 * 1024


def swap(a):
    return lax.ppermute(a, "core", [(0, 1), (1, 0)])


def turned(a, axis, by):
    n = lax.axis_size(axis)
    return lax.ppermute(a, axis, [(i, (i + by) % n) for i in range(n)])


def after(a, *others):
    return lax.optimization_barrier((a, others))[0]


def in_place(parts, me):
    n = len(parts)
    if n == 2:
        first = me == 0
        return [jnp.where(first, *parts), jnp.where(first, *parts[::-1])]
    if n <= 4:
        return [lax.select_n((me - i) % n, *parts) for i in range(n)]
    back = parts[:0:-1] + parts[:1]
    wide = jnp.stack(back + back)
    return list(lax.dynamic_slice_in_dim(wide, n - 1 - me, n, axis=0))


def fetched(a, axis):
    return [a] + [turned(a, axis, k) for k in range(1, lax.axis_size(axis))]


def gather_axis(a, axis, dim):
    if lax.axis_size(axis) == 1:
        return jnp.expand_dims(a, dim)
    return jnp.stack(in_place(fetched(a, axis), lax.axis_index(axis)), axis=dim)


def shares(a, axis, dim):
    n, me = lax.axis_size(axis), lax.axis_index(axis)
    return [lax.dynamic_index_in_dim(a, (me + k) % n, dim, False) for k in range(n)]


def sent(parts, axis):
    return parts[0], [turned(a, axis, k) for k, a in enumerate(parts) if k]


def sends(a, axis, dim):
    return sent(shares(a, axis, dim), axis)


def added(own, got):
    total = own.astype(F32)
    for part in got:
        total = total + part.astype(F32)
    return total


def crossed(a, early, by):
    n = lax.axis_size("x")
    pairs = []
    for y in range(n):
        for x in range(n):
            for core in range(2):
                along_x = (core == 0) == early
                to_x = (x + by) % n if along_x else x
                to_y = y if along_x else (y + by) % n
                pairs.append(((y * n + x) * 2 + core, (to_y * n + to_x) * 2 + core))
    return lax.ppermute(a, ("y", "x", "core"), pairs)


def cross_place(early):
    along_x = (lax.axis_index("core") == 0) == early
    return jnp.where(along_x, lax.axis_index("x"), lax.axis_index("y"))


def cross_fetched(a, early):
    return [a] + [crossed(a, early, k) for k in range(1, lax.axis_size("x"))]


def cross_stack(parts):
    return jnp.stack(in_place(parts, cross_place(True)))


def cross_end(parts):
    every = jnp.stack(in_place(parts, cross_place(False)))
    first = lax.axis_index("core") == 0
    return jnp.where(first, every, jnp.swapaxes(every, 0, 1)).transpose(2, 0, 1, 3, 4)


def grid_of(a):
    nz, ny, nx = (lax.axis_size(axis) for axis in ("z", "y", "x"))
    return a.reshape(nz, ny, nx, -1, a.shape[-1])


def late_shares(a):
    n = lax.axis_size("x")
    first = lax.axis_index("core") == 0
    y, x = lax.axis_index("y"), lax.axis_index("x")
    return [
        jnp.where(
            first,
            lax.dynamic_index_in_dim(a, (y + k) % n, 1, False),
            lax.dynamic_index_in_dim(a, (x + k) % n, 2, False),
        )
        for k in range(n)
    ]


def early_shares(stage):
    total = added(*stage).astype(BF16)
    n, me = lax.axis_size("x"), cross_place(True)
    return [lax.dynamic_index_in_dim(total, (me + k) % n, 1, False) for k in range(n)]


def cross_sent(parts, early):
    return parts[0], [crossed(a, early, k) for k, a in enumerate(parts) if k]


def core_pick(a, core):
    return (
        lax.dynamic_index_in_dim(a, core, 0, False),
        lax.dynamic_index_in_dim(a, 1 - core, 0, False),
    )


def chip_rows(mine, got, core):
    first = core == 0
    return jnp.concatenate(
        [jnp.where(first, mine, got), jnp.where(first, got, mine)], axis=-2
    )


def own_rows(total, core):
    mine, other = core_pick(total.reshape(2, -1, total.shape[-1]), core)
    got = swap(other)
    first = core == 0
    return jnp.stack([jnp.where(first, mine, got), jnp.where(first, got, mine)], axis=0)


def z_sum(a):
    parts = in_place([p if k == 0 else turned(p, "z", k) for k, p in enumerate(shares(a, "z", 0))], lax.axis_index("z"))
    total = parts[0]
    for part in parts[1:]:
        total = total + part
    return total


def plane_step(a, k):
    n = lax.axis_size("x")
    ky, kx = divmod(k, n)
    pairs = [(j * n + i, (j + ky) % n * n + (i + kx) % n) for j in range(n) for i in range(n)]
    return lax.ppermute(a, ("y", "x"), pairs)


def plane_fetched(a):
    return [a] + [plane_step(a, k) for k in range(1, lax.axis_size("x") ** 2)]


def plane_order(parts):
    n = lax.axis_size("x")
    rows_of = [in_place(parts[k * n : (k + 1) * n], lax.axis_index("x")) for k in range(n)]
    columns_of = [in_place([r[i] for r in rows_of], lax.axis_index("y")) for i in range(n)]
    return [[columns_of[i][j] for i in range(n)] for j in range(n)]


def plane_stack(parts):
    return jnp.stack([jnp.stack(row) for row in plane_order(parts)])


def plane_shares(a):
    n = lax.axis_size("x")
    y, x = lax.axis_index("y"), lax.axis_index("x")
    out = []
    for k in range(n * n):
        ky, kx = divmod(k, n)
        one = lax.dynamic_index_in_dim(a, (y + ky) % n, 1, False)
        out.append(lax.dynamic_index_in_dim(one, (x + kx) % n, 1, False))
    return out


def plane_sum(shares):
    parts = [a if k == 0 else plane_step(a, k) for k, a in enumerate(shares)]
    total = None
    for row in plane_order(parts):
        for part in row:
            total = part if total is None else total + part
    return total


def dot1(a, b, dims=((1,), (0,))):
    return lax.dot_general(
        a.astype(BF16), b.astype(BF16), (dims, ((), ())), preferred_element_type=F32
    )


TN = ((0,), (0,))
NT = ((1,), (1,))


def split(a):
    high = a.astype(BF16)
    return high, (a - high.astype(F32)).astype(BF16)


def dot3(a, b):
    ah, al = split(a)
    bh, bl = split(b)
    return dot1(ah, bh) + (dot1(ah, bl) + dot1(al, bh))


def sigmoid(v):
    return 1.0 / (1.0 + jnp.exp(-v))


def grid_masks(n):
    i = lax.broadcasted_iota(jnp.int32, (n, n), 0)
    j = lax.broadcasted_iota(jnp.int32, (n, n), 1)
    return i, j


def unit_inverses(lowers, i, j):
    n = lowers[0].shape[0]
    level = jnp.where(i > j, i ^ j, 0)
    eye = jnp.where(i == j, 1.0, 0.0).astype(F32)
    highs = [a.astype(BF16) for a in lowers]
    lows = [(a - h.astype(F32)).astype(BF16) for a, h in zip(lowers, highs)]
    inverses = [eye - jnp.where(level == 1, a, 0.0) for a in lowers]
    size = 2
    while size < n:
        corner = (level >= size) & (level < 2 * size)
        lefts = [t.astype(BF16) for t in inverses]
        inner = [dot1(jnp.where(corner, h, jnp.zeros_like(h)), t) for h, t in zip(highs, lefts)]
        inverses = [t - dot1(b, c) for t, b, c in zip(inverses, lefts, inner)]
        size *= 2
    parts = [split(t) for t in inverses]
    rests = [
        eye - t - (dot1(h, th) + (dot1(h, tl) + dot1(lo, th)))
        for t, h, lo, (th, tl) in zip(inverses, highs, lows, parts)
    ]
    return [t + dot1(th, r) for t, (th, _), r in zip(inverses, parts, rests)]


def conv_of(ext, taps, rows):
    total = taps[0:1, :] * ext[HALO - 3 : HALO - 3 + rows]
    for i in range(1, CONV):
        total = total + taps[i : i + 1, :] * ext[HALO - 3 + i : HALO - 3 + i + rows]
    return total


def first_kernel(half, count, me_ref, *refs):
    parts, refs = refs[:count], refs[count:]
    if half == 0:
        x_ref, g_ref, beta_ref, cv_ref, bias_ref = refs[:5]
        n_ref, w_ref, pre_ref, qkv_ref, t_ref, wu_ref, pd_ref, b_ref, sem = refs[5:]
    else:
        n_ref, beta_ref, cv_ref, bias_ref = refs[:4]
        w_ref, pre_ref, qkv_ref, t_ref, wu_ref, pd_ref, b_ref, sem = refs[-8:]
    rows = qkv_ref.shape[1] // 2
    frame = rows + HALO
    copies = []
    columns_of = pl.ds(half * 768, 768)
    for k, part in enumerate(parts):
        inner = part.shape[0]
        late = lax.rem(jnp.where(me_ref[0] == 0, me_ref[1], me_ref[2]) + (count - k), count)
        for i in range(inner):
            to_y = jnp.where(me_ref[0] == 0, late, i)
            to_x = jnp.where(me_ref[0] == 0, i, late)
            copies.append(
                pltpu.make_async_copy(
                    part.at[i, :, :, columns_of], w_ref.at[:, to_y, to_x], sem.at[k * inner + i]
                )
            )
            copies[-1].start()
    if half == 0:
        x = x_ref[...].astype(F32)
        scale = lax.rsqrt(jnp.mean(x * x, axis=-1, keepdims=True) + EPS)
        n_ref[...] = (x * scale * g_ref[...]).astype(BF16)
    normed = n_ref[...]
    for copy in copies:
        copy.wait()
    pre_ref[0] = dot1(normed, w_ref[...].reshape(D, 768)).astype(BF16)
    linear = dot1(normed, beta_ref[0])
    i, j = grid_masks(rows)
    keys, rights, lowers = [], [], []
    for q in range(2):
        rate = sigmoid(linear[q * frame + HALO : (q + 1) * frame] + bias_ref[0, q : q + 1, :])
        b_ref[0, q * rows : (q + 1) * rows, :] = rate
        ext = pre_ref[0, q * frame : (q + 1) * frame, :].astype(F32)
        conv = conv_of(ext, cv_ref[0], rows)
        act = conv * sigmoid(conv)
        for h in range(2):
            place = pl.ds(q * rows, rows)
            parts = []
            for kind in range(3):
                lane = (kind * 2 + h) * DK
                one = act[:, lane : lane + DK]
                if kind < 2:
                    one = one * lax.rsqrt(jnp.sum(one * one, axis=-1, keepdims=True) + EPS)
                if kind == 0:
                    one = one * DK ** (-0.5)
                one = one.astype(BF16)
                qkv_ref[0, place, lane : lane + DK] = one
                parts.append(one)
            key, value = parts[1], parts[2]
            col = rate[:, h : h + 1]
            keys.append(key)
            rights.append(jnp.concatenate([key, value], axis=1).astype(F32) * col)
            lowers.append(jnp.where(i > j, dot1(key, key, NT) * col, 0.0))
    inverses = unit_inverses(lowers, i, j)
    boths = [dot3(t, r) for t, r in zip(inverses, rights)]
    for p in range(4):
        t_ref[0, p] = inverses[p].astype(BF16)
        wu_ref[0, p] = boths[p].astype(BF16)
    for p in range(4):
        pd_ref[0, p] = dot1(keys[p], boths[p], TN).astype(BF16)


def state_kernel(pd_ref, s_ref):
    count = pd_ref.shape[0]
    state = jnp.zeros((DK, DK), F32)
    for s in range(count):
        s_ref[s] = state.astype(BF16)
        if s + 1 < count:
            high, low = split(state)
            move = pd_ref[s, :, :DK]
            state = state - (dot1(move, high) + dot1(move, low)) + pd_ref[s, :, DK:].astype(F32)


def adjoint_kernel(pd_ref, g_ref, l_ref):
    count = pd_ref.shape[0]
    adjoint = jnp.zeros((DK, DK), F32)
    for s in range(count - 1, -1, -1):
        l_ref[s] = adjoint.astype(BF16)
        if s > 0:
            high, low = split(adjoint)
            move = pd_ref[s, :, :DK]
            adjoint = (
                adjoint - (dot1(move, high, TN) + dot1(move, low, TN)) + g_ref[s].astype(F32)
            )


def pair_places(rows):
    return [
        (q * 2 + h, pl.ds(q * rows, rows), pl.ds(h * DK, DK), h) for q in range(2) for h in range(2)
    ]


def kind_lanes(kind, h):
    return pl.ds((kind * 2 + h) * DK, DK)


def second_kernel(qkv_ref, wu_ref, s_ref, hg_ref, f_ref, m_ref, h_ref):
    rows = qkv_ref.shape[1] // 2
    i, j = grid_masks(rows)
    pairs = pair_places(rows)
    queries = [qkv_ref[0, at, kind_lanes(0, h)] for _, at, _, h in pairs]
    keys = [qkv_ref[0, at, kind_lanes(1, h)] for _, at, _, h in pairs]
    scores = [jnp.where(i >= j, dot1(a, b, NT), 0.0).astype(BF16) for a, b in zip(queries, keys)]
    freshes = [
        (wu_ref[0, p, :, DK:].astype(F32) - dot1(wu_ref[0, p, :, :DK], s_ref[p])).astype(BF16)
        for p, _, _, _ in pairs
    ]
    mixes = [
        dot1(queries[p], s_ref[p]) + dot1(scores[p], freshes[p]) for p, _, _, _ in pairs
    ]
    for p, at, lanes, _ in pairs:
        mixed = mixes[p]
        scale = lax.rsqrt(jnp.mean(mixed * mixed, axis=-1, keepdims=True) + EPS)
        f_ref[at, lanes] = freshes[p]
        m_ref[at, lanes] = mixed
        h_ref[at, lanes] = (mixed * scale * hg_ref[...]).astype(BF16)


def third_kernel(qkv_ref, wu_ref, s_ref, f_ref, m_ref, dh_ref, hg_ref, sg_ref, gf_ref, gq_ref, gk_ref, ghg_ref):
    rows = qkv_ref.shape[1] // 2
    i, j = grid_masks(rows)
    gain = hg_ref[...]
    gain_grad = jnp.zeros((1, DK), F32)
    pairs = pair_places(rows)
    queries = [qkv_ref[0, at, kind_lanes(0, h)] for _, at, _, h in pairs]
    keys = [qkv_ref[0, at, kind_lanes(1, h)] for _, at, _, h in pairs]
    scores = [jnp.where(i >= j, dot1(a, b, NT), 0.0).astype(BF16) for a, b in zip(queries, keys)]
    grads = []
    for _, at, lanes, _ in pairs:
        mixed = m_ref[at, lanes]
        up = dh_ref[at, lanes].astype(F32)
        scale = lax.rsqrt(jnp.mean(mixed * mixed, axis=-1, keepdims=True) + EPS)
        unit = mixed * scale
        gain_grad = gain_grad + jnp.sum(up * unit, axis=0, keepdims=True)
        inner = up * gain
        grad = scale * (inner - unit * jnp.mean(inner * unit, axis=-1, keepdims=True))
        grads.append(grad.astype(BF16))
    ghg_ref[0] = jnp.broadcast_to(gain_grad, ghg_ref.shape[1:])
    fresh_grads = [dot1(a, g, TN) for a, g in zip(scores, grads)]
    starts = [
        dot1(queries[p], grads[p], TN) - dot1(wu_ref[0, p, :, :DK], fresh_grads[p], TN)
        for p in range(4)
    ]
    score_grads = [
        jnp.where(i >= j, dot1(grads[p], f_ref[at, lanes], NT), 0.0).astype(BF16)
        for p, at, lanes, _ in pairs
    ]
    for p, at, lanes, _ in pairs:
        gf_ref[at, lanes] = fresh_grads[p]
        sg_ref[0, p] = starts[p].astype(BF16)
        gq_ref[at, lanes] = dot1(grads[p], s_ref[p], NT) + dot1(score_grads[p], keys[p])
        gk_ref[at, lanes] = dot1(score_grads[p], queries[p], TN)


def fourth_kernel(qkv_ref, pre_ref, cv_ref, b_ref, t_ref, wu_ref, s_ref, l_ref, f_ref, gf_ref, gq_ref, gk_ref, eg_ref, gc_ref, lg_ref, gb_ref):
    rows = qkv_ref.shape[1] // 2
    frame = rows + HALO
    i, j = grid_masks(rows)
    lane = lax.broadcasted_iota(jnp.int32, (rows, DK), 1)
    pairs = pair_places(rows)
    keys = [qkv_ref[0, at, kind_lanes(1, h)] for _, at, _, h in pairs]
    values = [qkv_ref[0, at, kind_lanes(2, h)] for _, at, _, h in pairs]
    cols = [b_ref[0, at, h : h + 1] for _, at, _, h in pairs]
    fresh_grads = [
        gf_ref[at, lanes] + dot1(keys[p], l_ref[p]) for p, at, lanes, _ in pairs
    ]
    lows = [g.astype(BF16) for g in fresh_grads]
    factor_grads = [
        jnp.concatenate([-dot1(lows[p], s_ref[p], NT).astype(BF16), lows[p]], axis=1)
        for p in range(4)
    ]
    solved = [dot1(t_ref[0, p], factor_grads[p], TN) for p in range(4)]
    inners = [dot1(k, k, NT) for k in keys]
    system_grads = [
        jnp.where(i > j, -dot1(solved[p], wu_ref[0, p], NT), 0.0) for p in range(4)
    ]
    inner_grads = [(g * c).astype(BF16) for g, c in zip(system_grads, cols)]
    key_grads = [
        gk_ref[at, lanes]
        + dot1(f_ref[at, lanes], l_ref[p], NT)
        + cols[p] * solved[p][:, :DK]
        + dot1(inner_grads[p], keys[p])
        + dot1(inner_grads[p], keys[p], TN)
        for p, at, lanes, _ in pairs
    ]
    rate_grads = [
        (
            jnp.sum(
                solved[p][:, :DK] * keys[p].astype(F32) + solved[p][:, DK:] * values[p].astype(F32),
                axis=-1,
                keepdims=True,
            )
            + jnp.sum(system_grads[p] * inners[p], axis=-1, keepdims=True)
        )
        * cols[p]
        * (1.0 - cols[p])
        for p in range(4)
    ]
    for q in range(2):
        place = pl.ds(q * rows, rows)
        logit = jnp.where(
            lane == 0, rate_grads[2 * q], jnp.where(lane == 1, rate_grads[2 * q + 1], 0.0)
        )
        lg_ref[0, place, :] = logit.astype(BF16)
        gb_ref[0, q : q + 1, :] = jnp.sum(logit, axis=0, keepdims=True)
    zero = jnp.zeros((HALO, DK), F32)
    for kind in range(3):
        for h in range(2):
            at = kind_lanes(kind, h)
            tap = cv_ref[0, :, at]
            conv_grad = [jnp.zeros((1, DK), F32) for _ in range(CONV)]
            for q in range(2):
                p = q * 2 + h
                ext = pre_ref[0, q * frame : (q + 1) * frame, at].astype(F32)
                views = [ext[HALO - 3 + t : HALO - 3 + t + rows] for t in range(CONV)]
                conv = tap[0:1, :] * views[0]
                for t in range(1, CONV):
                    conv = conv + tap[t : t + 1, :] * views[t]
                sig = sigmoid(conv)
                act = conv * sig
                if kind == 0:
                    grad = gq_ref[q * rows : (q + 1) * rows, h * DK : (h + 1) * DK] * DK ** (-0.5)
                elif kind == 1:
                    grad = key_grads[p]
                else:
                    grad = cols[p] * solved[p][:, DK:]
                if kind < 2:
                    scale = lax.rsqrt(jnp.sum(act * act, axis=-1, keepdims=True) + EPS)
                    unit = act * scale
                    grad = scale * (grad - unit * jnp.sum(grad * unit, axis=-1, keepdims=True))
                grad = grad * (sig * (1.0 + conv * (1.0 - sig)))
                wide = jnp.concatenate([zero, grad, zero], axis=0)
                total = tap[0:1, :] * wide[3 : 3 + frame]
                for t in range(1, CONV):
                    total = total + tap[t : t + 1, :] * wide[3 - t : 3 - t + frame]
                eg_ref[0, q * frame : (q + 1) * frame, at] = total.astype(BF16)
                for t in range(CONV):
                    conv_grad[t] = conv_grad[t] + jnp.sum(grad * views[t], axis=0, keepdims=True)
            for t in range(CONV):
                gc_ref[0, t : t + 1, at] = conv_grad[t]


def lead(*shape):
    return pl.BlockSpec((1,) + shape, lambda p: (p,) + (0,) * len(shape))


def at_half(half, *shape):
    return pl.BlockSpec((1,) + shape, lambda p: (half,) + (0,) * len(shape))


def whole(*shape):
    return pl.BlockSpec(shape, lambda p: (0,) * len(shape))


def columns(rows, cols):
    return pl.BlockSpec((rows, cols), lambda p: (0, p))


def quarter():
    return pl.BlockSpec((4, DK, DK), lambda p: (p, 0, 0))


def cost(microseconds):
    return pl.CostEstimate(
        flops=int(microseconds * 1.15e9), bytes_accessed=0, transcendentals=0
    )


def on_core(kernel, outs, in_specs, out_specs, name, microseconds):
    return pl.pallas_call(
        kernel,
        out_shape=outs,
        grid=(2,),
        in_specs=in_specs,
        out_specs=out_specs,
        compiler_params=pltpu.CompilerParams(
            vmem_limit_bytes=VMEM_LIMIT, dimension_semantics=("arbitrary",)
        ),
        cost_estimate=cost(microseconds),
        name=name,
    )


def sds(shape, kind):
    return jax.ShapeDtypeStruct(shape, kind)


def all_ranges(a):
    if lax.axis_size("z") * lax.axis_size("y") == a.shape[0]:
        return lax.all_to_all(a, SEQ, 0, 0, tiled=True)
    return lax.all_gather(a, SEQ)


def scan_states(every):
    count = lax.axis_size("z") * lax.axis_size("y")
    if every.ndim == 3:
        return pl.pallas_call(
            state_kernel,
            out_shape=sds((count, DK, DK), BF16),
            cost_estimate=cost(3),
            name="state_scan",
        )(every)

    def step(s, state):
        one = lax.dynamic_index_in_dim(every, s, 0, False).astype(F32)
        moved = jnp.einsum(
            "pij,pjk->pik", one[:, :, :DK], state, precision=lax.Precision.HIGHEST
        )
        return state - moved + one[:, :, DK:]

    start = jnp.zeros((every.shape[1], DK, DK), F32)
    return lax.fori_loop(0, lax.axis_index(SEQ), step, start).astype(BF16)


def scan_adjoints(every, grads):
    count = lax.axis_size("z") * lax.axis_size("y")
    if every.ndim == 3:
        return pl.pallas_call(
            adjoint_kernel,
            out_shape=sds((count, DK, DK), BF16),
            cost_estimate=cost(3),
            name="adjoint_scan",
        )(every, grads)

    def step(k, adjoint):
        s = count - 1 - k
        one = lax.dynamic_index_in_dim(every, s, 0, False).astype(F32)
        moved = jnp.einsum(
            "pji,pjk->pik", one[:, :, :DK], adjoint, precision=lax.Precision.HIGHEST
        )
        return adjoint - moved + lax.dynamic_index_in_dim(grads, s, 0, False).astype(F32)

    start = jnp.zeros((every.shape[1], DK, DK), F32)
    steps = count - 1 - lax.axis_index(SEQ)
    return lax.fori_loop(0, steps, step, start).astype(BF16)


def own_range(a):
    if lax.axis_size("z") * lax.axis_size("y") == H:
        return lax.all_to_all(a, SEQ, 0, 0, tiled=True)
    return a


def shards(
    inputs,
    domain_ids,
    norm1_gain,
    w_qkv,
    w_beta,
    conv_weight,
    domain_bias,
    head_gain,
    w_out,
    norm2_gain,
    w_gate_up,
    w_down,
    cotangent,
):
    core = lax.axis_index("core")
    nz, ny, nx = (lax.axis_size(a) for a in ("z", "y", "x"))
    z, y, x = (lax.axis_index(a) for a in ("z", "y", "x"))
    chips = nz * ny * nx
    seq_devices = nz * ny
    rows = inputs.shape[1]
    frame = rows + HALO
    tall = 2 * rows
    drows = w_qkv.shape[0]
    both_rows = 2 * drows
    frows = w_down.shape[0]
    grows = conv_weight.shape[0]
    first = core == 0
    half = H // 2
    fence = lax.optimization_barrier

    q_mine, q_other = core_pick(
        w_qkv.reshape(drows, 3, 2, 2, 256).transpose(2, 0, 3, 1, 4).reshape(2, drows, 1536), core
    )
    q_got = swap(q_other)
    small = jnp.concatenate(
        [norm1_gain, norm2_gain, w_beta.reshape(-1), conv_weight.reshape(-1)]
    )
    n_small = small.shape[0]
    small = jnp.pad(small, (0, 768 - n_small)).reshape(1, 768)
    small_got = swap(small)
    x_own = inputs.reshape(rows, D)
    halo = lax.ppermute(
        x_own[rows - HALO :], SEQ, [(i, i + 1) for i in range(seq_devices - 1)]
    )
    small = jnp.concatenate(
        [jnp.where(first, small, small_got), jnp.where(first, small_got, small)], axis=1
    )
    small = jnp.pad(small, ((0, 7), (0, 0)))
    q_part = jnp.concatenate([chip_rows(q_mine, q_got, core), small], axis=0)
    q_part, halo, x_own, w_gate_up, w_out, w_down, cotangent = fence(
        (q_part, halo, x_own, w_gate_up, w_out, w_down, cotangent)
    )

    q_far = fetched(q_part, "z")
    out_cols = w_out.reshape(drows, 2, 2, 256).transpose(1, 2, 0, 3)
    gu_cols = (
        w_gate_up.reshape(drows, 2, chips, 2, frows)
        .transpose(3, 1, 0, 2, 4)
        .reshape(2, 2, drows, FF // 2)
    )
    wide_cols = jnp.concatenate(
        [gu_cols[:, 0], gu_cols[:, 1], out_cols[:, 0], out_cols[:, 1]], axis=-1
    )
    wide_mine, wide_other = core_pick(wide_cols, core)
    wide_part = chip_rows(wide_mine, swap(wide_other), core)
    choose = (domain_ids[0] == jnp.arange(NDOM, dtype=jnp.int32)).astype(BF16)
    bias_own = jnp.sum(domain_bias.astype(F32) * choose.astype(F32)[:, None], axis=0)
    extra = jnp.pad(jnp.concatenate([bias_own.astype(BF16), choose]), (0, D - H - NDOM))
    extra = jnp.pad(extra.reshape(1, D), ((0, HALO - 1), (0, 0)))
    frame_own = jnp.concatenate([halo, x_own, extra], axis=0)
    frame_other = swap(frame_own)
    g_own = cotangent.reshape(rows, D)
    g_other = swap(g_own)
    q_far, frame_own, frame_other, g_own, g_other, wide_part, w_down = fence(
        (q_far, frame_own, frame_other, g_own, g_other, wide_part, w_down)
    )

    q_sorted = in_place(q_far, z)
    q_parts = cross_fetched(jnp.stack([a[:both_rows] for a in q_sorted]), True)
    smalls = jnp.stack([a[both_rows].reshape(2, 768) for a in q_sorted])
    smalls = plane_fetched(smalls)
    ends = sorted({1, nz - 1})
    wide_z = [wide_part, turned(wide_part, "z", 1)]
    q_parts, wide_z, w_down = fence((q_parts, wide_z, w_down))

    q_parts = cross_fetched(cross_stack(q_parts), False)
    wide_z += [turned(wide_z[0], "z", k) for k in range(2, nz - 1)]
    smalls = plane_stack(smalls).transpose(2, 0, 1, 3, 4).reshape(2 * chips, 768)[:, :n_small]
    gain_one = smalls[:, :drows].reshape(1, D).astype(F32)
    gain_two = smalls[:, drows : 2 * drows].reshape(1, D).astype(F32)
    full_beta = smalls[:, 2 * drows : 2 * drows + drows * H].reshape(D, 2, half)
    full_conv = smalls[:, 2 * drows + drows * H :].reshape(3, 2, 2, 256, CONV)
    beta_mine = lax.dynamic_index_in_dim(full_beta, core, 1, False)
    conv_mine = (
        lax.dynamic_index_in_dim(full_conv, core, 1, False)
        .transpose(1, 3, 0, 2)
        .reshape(2, CONV, 768)
        .astype(F32)
    )
    beta_pairs = jnp.pad(
        beta_mine.reshape(D, 2, 2).transpose(1, 0, 2), ((0, 0), (0, 0), (0, DK - 2))
    )
    x_frames = jnp.concatenate([frame_own[:frame], frame_other[:frame]], axis=0)
    bias_both = jnp.stack([frame_own[frame, :H], frame_other[frame, :H]]).astype(F32)
    choose_both = jnp.stack(
        [frame_own[frame, H : H + NDOM], frame_other[frame, H : H + NDOM]]
    ).astype(F32)
    bias_mine = lax.dynamic_index_in_dim(bias_both.reshape(2, 2, half), core, 1, False)
    bias_pairs = jnp.pad(
        bias_mine.reshape(2, 2, 2).transpose(1, 0, 2), ((0, 0), (0, 0), (0, DK - 2))
    )
    x_both = jnp.concatenate(
        [frame_own[HALO:frame], frame_other[HALO:frame]], axis=0
    ).astype(F32)
    g_both = jnp.concatenate([g_own, g_other], axis=0)
    (
        q_parts,
        wide_z,
        w_down,
        gain_one,
        gain_two,
        beta_pairs,
        conv_mine,
        bias_pairs,
        x_frames,
        x_both,
        g_both,
    ) = fence(
        (
            q_parts,
            wide_z,
            w_down,
            gain_one,
            gain_two,
            beta_pairs,
            conv_mine,
            bias_pairs,
            x_frames,
            x_both,
            g_both,
        )
    )

    if both_rows % 16 == 0:
        w_shape = sds((nz, ny, nx, both_rows, 768), BF16)
    else:
        w_shape = sds((1, 1, 1, D, 768), BF16)
        q_parts = [cross_end(q_parts).reshape(1, 1, D, 1536)]
    place = jnp.stack([core, y, x]).astype(jnp.int32)
    kept = (
        sds((2, 2 * frame, 768), BF16),
        sds((2, tall, 768), BF16),
        sds((2, 4, rows, rows), BF16),
        sds((2, 4, rows, 2 * DK), BF16),
        sds((2, 4, DK, 2 * DK), BF16),
        sds((2, tall, DK), F32),
    )
    anywhere = pl.BlockSpec(memory_space=pl.ANY)

    def local(number, parts, ins, in_specs, outs, out_specs, held):
        fixed = [at_half(number, D, DK), at_half(number, CONV, 768), at_half(number, 2, DK)]
        first_held = 1 + len(parts) + len(ins) + 3
        return pl.pallas_call(
            functools.partial(first_kernel, number, len(parts)),
            out_shape=outs + (w_shape,) + kept,
            grid=(1,),
            in_specs=[pl.BlockSpec(memory_space=pltpu.SMEM)]
            + [anywhere] * len(parts)
            + in_specs
            + fixed
            + [anywhere] * len(held),
            out_specs=out_specs
            + (whole(*w_shape.shape),)
            + tuple(at_half(number, *k.shape[1:]) for k in kept),
            scratch_shapes=[pltpu.SemaphoreType.DMA((len(parts) * parts[0].shape[0],))],
            input_output_aliases={
                first_held + k: len(outs) + 1 + k for k in range(len(held))
            },
            compiler_params=pltpu.CompilerParams(vmem_limit_bytes=VMEM_LIMIT),
            cost_estimate=cost(10),
            name="delta_local",
        )(place, *parts, *ins, beta_pairs, conv_mine, bias_pairs, *held)

    wide_z += [turned(wide_z[0], "z", k) for k in ends[1:]]
    normed, w_q_one, *held = local(
        0,
        q_parts,
        (x_frames, gain_one),
        [whole(2 * frame, D), whole(1, D)],
        (sds((2 * frame, D), BF16),),
        (whole(2 * frame, D),),
        (),
    )
    normed, w_q_one, held, wide_z, q_parts, w_down = fence(
        (normed, w_q_one, held, wide_z, q_parts, w_down)
    )

    wide_stack = jnp.stack(in_place(wide_z, z)).reshape(nz * both_rows, -1)
    wide_parts = cross_fetched(wide_stack, True)
    down_z = fetched(w_down, "z")
    w_q_two, *held = local(
        1,
        q_parts,
        (after(normed, wide_stack),),
        [whole(2 * frame, D)],
        (),
        (),
        tuple(held),
    )
    pre, qkv, inverse, factors, pd, rates = held
    w_q_one = w_q_one.reshape(D, 768)
    w_q_two = w_q_two.reshape(D, 768)
    (
        normed,
        w_q_one,
        w_q_two,
        pre,
        qkv,
        inverse,
        factors,
        pd,
        rates,
        down_z,
    ) = fence(
        (
            normed,
            w_q_one,
            w_q_two,
            pre,
            qkv,
            inverse,
            factors,
            pd,
            rates,
            down_z,
        )
    )

    every = all_ranges(pd.reshape(H, DK, 2 * DK))
    down_stack = jnp.stack(in_place(down_z, z))
    down_parts = cross_fetched(down_stack, True)
    wide_stack = cross_stack(after(wide_parts, pd))
    every, wide_stack = fence((every, wide_stack))

    states = scan_states(every)
    down_parts = cross_fetched(cross_stack(after(down_parts, states)), False)
    wide_parts = cross_fetched(after(wide_stack, states), False)
    states = own_range(states)
    gain_head = head_gain.astype(F32).reshape(1, DK)
    fresh, mixed, heads_mine = on_core(
        second_kernel,
        (sds((tall, 512), BF16), sds((tall, 512), F32), sds((tall, 512), BF16)),
        [lead(tall, 768), lead(4, rows, 2 * DK), quarter(), whole(1, DK)],
        (columns(tall, 256), columns(tall, 256), columns(tall, 256)),
        "delta_mix",
        2,
    )(qkv, factors, states, gain_head)
    heads_got = swap(heads_mine)
    wide_parts, states, fresh, mixed, heads_mine, heads_got = fence(
        (wide_parts, states, fresh, mixed, heads_mine, heads_got)
    )

    wide = [a.reshape(a.shape[0], nz, both_rows, -1) for a in wide_parts]
    cuts = ((0, FF // 2), (FF // 2, FF), (FF, FF + D // 2))
    w_gate, w_up, out_mine = (
        cross_end([a[..., lo:hi] for a in wide]).reshape(D, hi - lo) for lo, hi in cuts
    )
    out_got = swap(out_mine)
    full_out = jnp.concatenate(
        [jnp.where(first, out_mine, out_got), jnp.where(first, out_got, out_mine)], axis=1
    )
    heads_got = jnp.concatenate([heads_got[rows:], heads_got[:rows]], axis=0)
    heads = jnp.concatenate(
        [jnp.where(first, heads_mine, heads_got), jnp.where(first, heads_got, heads_mine)], axis=1
    )
    middle = x_both + jnp.dot(heads, full_out, preferred_element_type=F32)
    scale_two = lax.rsqrt(jnp.mean(middle * middle, axis=-1, keepdims=True) + EPS)
    unit_two = middle * scale_two
    normed_two = (unit_two * gain_two).astype(BF16)
    gate = jnp.dot(normed_two, w_gate, preferred_element_type=F32)
    up = jnp.dot(normed_two, w_up, preferred_element_type=F32)
    w_down_mine = cross_end(after(down_parts, gate, up)).reshape(chips * frows, D)
    sig = jax.nn.sigmoid(gate)
    hidden = (gate * sig * up).astype(BF16)
    hidden_grad = jnp.einsum("nd,fd->nf", g_both, w_down_mine, preferred_element_type=F32)
    up_grad = (hidden_grad * gate * sig).astype(BF16)
    gate_grad = (hidden_grad * up * sig * (1.0 + gate * (1.0 - sig))).astype(BF16)
    hidden, up_grad, gate_grad = fence((hidden, up_grad, gate_grad))

    normed_two_part = jnp.einsum(
        "nf,df->nd", gate_grad, w_gate, preferred_element_type=F32
    ) + jnp.einsum("nf,df->nd", up_grad, w_up, preferred_element_type=F32)
    part_low = normed_two_part.astype(BF16)
    part_got = swap(part_low)
    grad_down = jnp.einsum(
        "nf,nd->fd", after(hidden, part_low), g_both, preferred_element_type=F32
    ).astype(BF16)
    down_stage = cross_sent(late_shares(grid_of(grad_down)), False)
    grad_gate = jnp.einsum(
        "nd,nf->df", after(normed_two, grad_down), gate_grad, preferred_element_type=F32
    )
    gate_stage = cross_sent(late_shares(grid_of(grad_gate.astype(BF16))), False)
    part_got = after(part_got, grad_gate)
    part_got = jnp.concatenate([part_got[rows:], part_got[:rows]], axis=0)
    normed_two_grad = normed_two_part + part_got.astype(F32)
    grad_norm2 = jnp.sum(normed_two_grad[:rows] * unit_two[:rows], axis=0)
    inner = normed_two_grad * gain_two
    middle_grad = g_both.astype(F32) + scale_two * (
        inner - unit_two * jnp.mean(inner * unit_two, axis=-1, keepdims=True)
    )
    middle_low = middle_grad.astype(BF16)
    out_rows = lax.dynamic_slice_in_dim(full_out, core * 512, 512, 0)
    heads_grad = jnp.einsum("ne,de->nd", middle_low, out_rows, preferred_element_type=F32)
    start_grad, fresh_grad, query_grad, key_grad, gain_part = on_core(
        third_kernel,
        (
            sds((2, 4, DK, DK), BF16),
            sds((tall, 512), F32),
            sds((tall, 512), F32),
            sds((tall, 512), F32),
            sds((2, 8, DK), F32),
        ),
        [
            lead(tall, 768),
            lead(4, rows, 2 * DK),
            quarter(),
            columns(tall, 256),
            columns(tall, 256),
            columns(tall, 256),
            whole(1, DK),
        ],
        (
            lead(4, DK, DK),
            columns(tall, 256),
            columns(tall, 256),
            columns(tall, 256),
            lead(8, DK),
        ),
        "delta_back_local",
        5,
    )(qkv, factors, states, fresh, mixed, heads_grad, gain_head)
    (
        start_grad,
        fresh_grad,
        query_grad,
        key_grad,
        gain_part,
        up_grad,
        middle_low,
        hidden,
    ) = fence(
        (
            start_grad,
            fresh_grad,
            query_grad,
            key_grad,
            gain_part,
            up_grad,
            middle_low,
            hidden,
        )
    )

    start_grads = all_ranges(start_grad.reshape(H, DK, DK))
    grad_up = jnp.einsum("nd,nf->df", normed_two, up_grad, preferred_element_type=F32)
    low_cols = lax.dynamic_slice_in_dim(middle_low, core * 512, 512, 1)
    grad_out = jnp.einsum("nd,ne->de", heads, low_cols, preferred_element_type=F32)
    up_shares = [
        jnp.concatenate(cut, axis=-1)
        for cut in zip(*(late_shares(grid_of(a.astype(BF16))) for a in (grad_up, grad_out)))
    ]
    up_stage = cross_sent(up_shares, False)
    adjoints = scan_adjoints(every, after(start_grads, up_shares))
    down_shares = early_shares(after(down_stage, adjoints))
    down_stage = cross_sent(down_shares, True)
    gate_shares = early_shares(after(gate_stage, down_shares))
    gate_stage = cross_sent(gate_shares, True)
    up_shares = early_shares(after(up_stage, adjoints))
    up_stage = cross_sent(up_shares, True)
    down_part = jnp.dot(after(hidden, adjoints), w_down_mine, preferred_element_type=F32)
    output = (middle[:rows] + down_part[:rows]) + swap(down_part[rows:].astype(BF16)).astype(F32)
    output = output.astype(BF16).reshape(1, rows, D)
    adjoints = own_range(adjoints)
    down_shares = shares(added(*after(down_stage, gate_shares)).astype(BF16), "z", 0)
    down_stage = sent(down_shares, "z")
    adjoints = after(adjoints, up_shares, down_shares, output)
    ext_grad, conv_part, logit_low, bias_part = on_core(
        fourth_kernel,
        (
            sds((2, 2 * frame, 768), BF16),
            sds((2, CONV, 768), F32),
            sds((2, tall, DK), BF16),
            sds((2, 2, DK), F32),
        ),
        [
            lead(tall, 768),
            lead(2 * frame, 768),
            lead(CONV, 768),
            lead(tall, DK),
            lead(4, rows, rows),
            lead(4, rows, 2 * DK),
            quarter(),
            quarter(),
            columns(tall, 256),
            columns(tall, 256),
            columns(tall, 256),
            columns(tall, 256),
        ],
        (lead(2 * frame, 768), lead(CONV, 768), lead(tall, DK), lead(2, DK)),
        "delta_back",
        15,
    )(qkv, pre, conv_mine, rates, inverse, factors, states, adjoints, fresh, fresh_grad, query_grad, key_grad)
    ext_grad, conv_part, logit_low, bias_part, gate_stage, up_stage, down_stage = fence(
        (ext_grad, conv_part, logit_low, bias_part, gate_stage, up_stage, down_stage)
    )

    ext_frames = ext_grad.reshape(2, 2, frame, 768)
    grad_q = [
        jnp.einsum("nd,nf->df", normed, e, preferred_element_type=F32).astype(BF16)
        for e in (ext_grad[0], ext_grad[1])
    ]
    q_shares = [
        jnp.concatenate(cut, axis=-1) for cut in zip(*(late_shares(grid_of(g)) for g in grad_q))
    ]
    ext_frames, gate_stage, up_stage, q_shares = fence(
        (ext_frames, gate_stage, up_stage, q_shares)
    )
    q_stage = cross_sent(q_shares, False)
    sent_back = lax.ppermute(
        ext_frames[:, :, :HALO], SEQ, [(i + 1, i) for i in range(seq_devices - 1)]
    )
    wide_part = jnp.concatenate([added(*gate_stage), added(*up_stage)], axis=-1).astype(BF16)
    wide_stage = sent(shares(wide_part, "z", 0), "z")
    tail = ext_frames[:, :, frame - HALO :].astype(F32) + sent_back.astype(F32)
    pre_low = jnp.concatenate(
        [ext_frames[:, :, HALO : frame - HALO], tail.astype(BF16)], axis=2
    ).reshape(2, tall, 768)
    normed_part = (
        jnp.einsum("nf,df->nd", pre_low[0], w_q_one, preferred_element_type=F32)
        + jnp.einsum("nf,df->nd", pre_low[1], w_q_two, preferred_element_type=F32)
        + jnp.einsum("pnh,pdh->nd", logit_low, beta_pairs, preferred_element_type=F32)
    )
    normed_grad = normed_part[:rows] + swap(normed_part[rows:].astype(BF16)).astype(F32)
    q_stage, normed_grad, normed, conv_part, logit_low, x_both = fence(
        (q_stage, normed_grad, normed, conv_part, logit_low, x_both)
    )

    q_shares, normed_grad, x_both = fence((early_shares(q_stage), normed_grad, x_both))
    q_stage = cross_sent(q_shares, True)
    x32 = x_both[:rows]
    scale_one = lax.rsqrt(jnp.mean(x32 * x32, axis=-1, keepdims=True) + EPS)
    unit_one = x32 * scale_one
    grad_norm1 = jnp.sum(normed_grad * unit_one, axis=0)
    inner_one = normed_grad * gain_one
    grad_input = middle_grad[:rows] + scale_one * (
        inner_one - unit_one * jnp.mean(inner_one * unit_one, axis=-1, keepdims=True)
    )
    grad_input = grad_input.reshape(1, rows, D)
    normed_tokens = normed.reshape(2, frame, D)[:, HALO:].reshape(tall, D)
    grad_beta = jnp.einsum(
        "nd,pnh->dph", normed_tokens, logit_low[:, :, :2], preferred_element_type=F32
    ).reshape(D, half)
    beta_full = jnp.where(
        first,
        jnp.pad(grad_beta, ((0, 0), (0, half))),
        jnp.pad(grad_beta, ((0, 0), (half, 0))),
    )
    conv_cols = conv_part.reshape(2, CONV, 3, 256).transpose(2, 0, 3, 1).reshape(3, 512, CONV)
    conv_full = jnp.where(
        first,
        jnp.pad(conv_cols, ((0, 0), (0, 512), (0, 0))),
        jnp.pad(conv_cols, ((0, 0), (512, 0), (0, 0))),
    )
    bias_heads = bias_part[:, :, :2].transpose(1, 0, 2).reshape(2, half)
    bias_heads = jnp.where(
        first,
        jnp.pad(bias_heads, ((0, 0), (0, half))),
        jnp.pad(bias_heads, ((0, 0), (half, 0))),
    )
    bias_grad = jnp.sum(choose_both[:, :, None] * bias_heads[:, None, :], axis=0)
    shared = jnp.concatenate([bias_grad.reshape(-1), gain_part[0, 0] + gain_part[1, 0]])
    shared = jnp.broadcast_to(shared, (2 * chips, shared.shape[0]))
    pack = jnp.concatenate(
        [
            grad_norm2.reshape(2 * chips, drows),
            beta_full.reshape(2 * chips, drows * H),
            conv_full.reshape(2 * chips, grows * CONV),
            shared,
        ],
        axis=1,
    )
    pack = jnp.pad(pack, ((0, 0), (0, -pack.shape[1] % DK)))
    norm_rows = jnp.pad(grad_norm1.reshape(2 * chips, drows), ((0, 0), (0, DK - drows)))
    pack = jnp.concatenate([norm_rows, pack], axis=1).reshape(chips, 2, -1)
    pack_own = lax.dynamic_index_in_dim(pack, core, 1, False)
    pack_got = swap(lax.dynamic_index_in_dim(pack, 1 - core, 1, False))
    pack = plane_shares((pack_own + pack_got).reshape(nz, ny, nx, -1))
    q_stage, pack, grad_input, wide_stage = fence((q_stage, pack, grad_input, wide_stage))

    q_shares = fence(shares(added(*q_stage).astype(BF16), "z", 0))
    q_stage = sent(q_shares, "z")
    pack = plane_sum(pack)
    own_down = added(*down_stage)
    wide_own = own_rows(added(*wide_stage), core)
    own_gu = (
        wide_own[..., :FF]
        .reshape(2, drows, 2, chips, frows)
        .transpose(1, 2, 3, 0, 4)
        .reshape(drows, 2 * FF)
    )
    own_out = wide_own[..., FF:].transpose(1, 0, 2).reshape(drows, D)
    q_stage, pack, own_gu, own_down, own_out = fence((q_stage, pack, own_gu, own_down, own_out))

    mine = z_sum(pack)
    q_own = own_rows(added(*q_stage), core)
    own_qkv = (
        q_own.reshape(2, drows, 2, 3, 256).transpose(1, 3, 0, 2, 4).reshape(drows, 3 * D)
    )
    own_g1 = mine[:drows]
    at = DK
    own_g2 = mine[at : at + drows]
    at += drows
    own_beta = mine[at : at + drows * H].reshape(drows, H)
    at += drows * H
    own_conv = mine[at : at + grows * CONV].reshape(grows, CONV)
    at += grows * CONV
    bias_total = mine[at : at + NDOM * H].reshape(NDOM, H)
    at += NDOM * H
    gain_total = mine[at : at + DK]
    return (
        output,
        grad_input,
        own_g1,
        own_qkv,
        own_beta,
        own_conv,
        bias_total,
        gain_total,
        own_out,
        own_g2,
        own_gu,
        own_down,
    )


def solution(mesh):
    seq, batch = mesh.shape["seq"], mesh.shape["batch"]
    plane = batch // 2
    fine = Mesh(mesh.devices.reshape(seq // plane, plane, plane, 2), ALL)
    tokens = P(("x", "core"), ("z", "y"), None)
    rows = P(ALL, None)
    vector = P(ALL)
    return jax.shard_map(
        shards,
        mesh=fine,
        in_specs=(
            tokens,
            P(("x", "core")),
            vector,
            rows,
            rows,
            rows,
            P(),
            P(),
            rows,
            vector,
            rows,
            rows,
            tokens,
        ),
        out_specs=(
            tokens,
            tokens,
            vector,
            rows,
            rows,
            rows,
            P(),
            P(),
            rows,
            vector,
            rows,
            rows,
        ),
        check_vma=False,
    )
```

```python
import functools

import jax
import jax.numpy as jnp
from jax import lax
from jax.experimental import pallas as pl
from jax.experimental.pallas import tpu as pltpu
from jax.sharding import Mesh
from jax.sharding import PartitionSpec as P

D = 1024
H = 8
DK = 128
FF = 2816
CONV = 4
NDOM = 4
EPS = 1e-06
HALO = 16
F32 = jnp.float32
BF16 = jnp.bfloat16
SEQ = ("z", "y")
ALL = ("z", "y", "x", "core")
VMEM_LIMIT = 60 * 1024 * 1024


def swap(a):
    return lax.ppermute(a, "core", [(0, 1), (1, 0)])


def turned(a, axis, by):
    n = lax.axis_size(axis)
    return lax.ppermute(a, axis, [(i, (i + by) % n) for i in range(n)])


def after(a, *others):
    return lax.optimization_barrier((a, others))[0]


def in_place(parts, me):
    n = len(parts)
    if n == 2:
        first = me == 0
        return [jnp.where(first, *parts), jnp.where(first, *parts[::-1])]
    if n <= 4:
        return [lax.select_n((me - i) % n, *parts) for i in range(n)]
    back = parts[:0:-1] + parts[:1]
    wide = jnp.stack(back + back)
    return list(lax.dynamic_slice_in_dim(wide, n - 1 - me, n, axis=0))


def fetched(a, axis):
    return [a] + [turned(a, axis, k) for k in range(1, lax.axis_size(axis))]


def gather_axis(a, axis, dim):
    if lax.axis_size(axis) == 1:
        return jnp.expand_dims(a, dim)
    return jnp.stack(in_place(fetched(a, axis), lax.axis_index(axis)), axis=dim)


def shares(a, axis, dim):
    n, me = lax.axis_size(axis), lax.axis_index(axis)
    return [lax.dynamic_index_in_dim(a, (me + k) % n, dim, False) for k in range(n)]


def sent(parts, axis):
    return parts[0], [turned(a, axis, k) for k, a in enumerate(parts) if k]


def sends(a, axis, dim):
    return sent(shares(a, axis, dim), axis)


def added(own, got):
    total = own.astype(F32)
    for part in got:
        total = total + part.astype(F32)
    return total


def crossed(a, early, by):
    n = lax.axis_size("x")
    pairs = []
    for y in range(n):
        for x in range(n):
            for core in range(2):
                along_x = (core == 0) == early
                to_x = (x + by) % n if along_x else x
                to_y = y if along_x else (y + by) % n
                pairs.append(((y * n + x) * 2 + core, (to_y * n + to_x) * 2 + core))
    return lax.ppermute(a, ("y", "x", "core"), pairs)


def cross_place(early):
    along_x = (lax.axis_index("core") == 0) == early
    return jnp.where(along_x, lax.axis_index("x"), lax.axis_index("y"))


def cross_fetched(a, early):
    return [a] + [crossed(a, early, k) for k in range(1, lax.axis_size("x"))]


def cross_stack(parts):
    return jnp.stack(in_place(parts, cross_place(True)))


def cross_end(parts):
    every = jnp.stack(in_place(parts, cross_place(False)))
    first = lax.axis_index("core") == 0
    return jnp.where(first, every, jnp.swapaxes(every, 0, 1)).transpose(2, 0, 1, 3, 4)


def assembled(groups):
    first = lax.axis_index("core") == 0
    far = []
    for parts in groups:
        every = jnp.stack(in_place(parts, cross_place(False)))
        grid = jnp.where(first, every, jnp.swapaxes(every, 0, 1))
        far += [grid[:, :, j] for j in range(grid.shape[2])]
    return jnp.stack(in_place(far, lax.axis_index("z")))


def spots(groups):
    out, base = [], 0
    for parts in groups:
        for k, part in enumerate(parts):
            out.append((len(out), base, k))
        base += parts[0].shape[1]
    return out


def grid_of(a):
    nz, ny, nx = (lax.axis_size(axis) for axis in ("z", "y", "x"))
    return a.reshape(nz, ny, nx, -1, a.shape[-1])


def late_shares(a):
    n = lax.axis_size("x")
    first = lax.axis_index("core") == 0
    y, x = lax.axis_index("y"), lax.axis_index("x")
    return [
        jnp.where(
            first,
            lax.dynamic_index_in_dim(a, (y + k) % n, 1, False),
            lax.dynamic_index_in_dim(a, (x + k) % n, 2, False),
        )
        for k in range(n)
    ]


def early_shares(stage):
    total = added(*stage).astype(BF16)
    n, me = lax.axis_size("x"), cross_place(True)
    return [lax.dynamic_index_in_dim(total, (me + k) % n, 1, False) for k in range(n)]


def cross_sent(parts, early):
    return parts[0], [crossed(a, early, k) for k, a in enumerate(parts) if k]


def core_pick(a, core):
    return (
        lax.dynamic_index_in_dim(a, core, 0, False),
        lax.dynamic_index_in_dim(a, 1 - core, 0, False),
    )


def chip_rows(mine, got, core):
    first = core == 0
    return jnp.concatenate(
        [jnp.where(first, mine, got), jnp.where(first, got, mine)], axis=-2
    )


def own_rows(total, core):
    mine, other = core_pick(total.reshape(2, -1, total.shape[-1]), core)
    got = swap(other)
    first = core == 0
    return jnp.stack([jnp.where(first, mine, got), jnp.where(first, got, mine)], axis=0)


def z_sum(a):
    parts = in_place([p if k == 0 else turned(p, "z", k) for k, p in enumerate(shares(a, "z", 0))], lax.axis_index("z"))
    total = parts[0]
    for part in parts[1:]:
        total = total + part
    return total


def plane_step(a, k):
    n = lax.axis_size("x")
    ky, kx = divmod(k, n)
    pairs = [(j * n + i, (j + ky) % n * n + (i + kx) % n) for j in range(n) for i in range(n)]
    return lax.ppermute(a, ("y", "x"), pairs)


def plane_fetched(a):
    return [a] + [plane_step(a, k) for k in range(1, lax.axis_size("x") ** 2)]


def plane_order(parts):
    n = lax.axis_size("x")
    rows_of = [in_place(parts[k * n : (k + 1) * n], lax.axis_index("x")) for k in range(n)]
    columns_of = [in_place([r[i] for r in rows_of], lax.axis_index("y")) for i in range(n)]
    return [[columns_of[i][j] for i in range(n)] for j in range(n)]


def plane_stack(parts):
    return jnp.stack([jnp.stack(row) for row in plane_order(parts)])


def plane_shares(a):
    n = lax.axis_size("x")
    y, x = lax.axis_index("y"), lax.axis_index("x")
    out = []
    for k in range(n * n):
        ky, kx = divmod(k, n)
        one = lax.dynamic_index_in_dim(a, (y + ky) % n, 1, False)
        out.append(lax.dynamic_index_in_dim(one, (x + kx) % n, 1, False))
    return out


def plane_sum(shares):
    parts = [a if k == 0 else plane_step(a, k) for k, a in enumerate(shares)]
    total = None
    for row in plane_order(parts):
        for part in row:
            total = part if total is None else total + part
    return total


def dot1(a, b, dims=((1,), (0,))):
    return lax.dot_general(
        a.astype(BF16), b.astype(BF16), (dims, ((), ())), preferred_element_type=F32
    )


TN = ((0,), (0,))
NT = ((1,), (1,))


def split(a):
    high = a.astype(BF16)
    return high, (a - high.astype(F32)).astype(BF16)


def dot3(a, b):
    ah, al = split(a)
    bh, bl = split(b)
    return dot1(ah, bh) + (dot1(ah, bl) + dot1(al, bh))


def sigmoid(v):
    return 1.0 / (1.0 + jnp.exp(-v))


def grid_masks(n):
    i = lax.broadcasted_iota(jnp.int32, (n, n), 0)
    j = lax.broadcasted_iota(jnp.int32, (n, n), 1)
    return i, j


def unit_inverses(lowers, i, j):
    n = lowers[0].shape[0]
    level = jnp.where(i > j, i ^ j, 0)
    eye = jnp.where(i == j, 1.0, 0.0).astype(F32)
    highs = [a.astype(BF16) for a in lowers]
    lows = [(a - h.astype(F32)).astype(BF16) for a, h in zip(lowers, highs)]
    inverses = [eye - jnp.where(level == 1, a, 0.0) for a in lowers]
    size = 2
    while size < n:
        corner = (level >= size) & (level < 2 * size)
        lefts = [t.astype(BF16) for t in inverses]
        inner = [dot1(jnp.where(corner, h, jnp.zeros_like(h)), t) for h, t in zip(highs, lefts)]
        inverses = [t - dot1(b, c) for t, b, c in zip(inverses, lefts, inner)]
        size *= 2
    parts = [split(t) for t in inverses]
    rests = [
        eye - t - (dot1(h, th) + (dot1(h, tl) + dot1(lo, th)))
        for t, h, lo, (th, tl) in zip(inverses, highs, lows, parts)
    ]
    return [t + dot1(th, r) for t, (th, _), r in zip(inverses, parts, rests)]


def conv_of(ext, taps, rows):
    total = taps[0:1, :] * ext[HALO - 3 : HALO - 3 + rows]
    for i in range(1, CONV):
        total = total + taps[i : i + 1, :] * ext[HALO - 3 + i : HALO - 3 + i + rows]
    return total


def block_moves(places, me_ref, parts, grid):
    nz, n, _ = grid
    core, my_y, my_x, my_z = (me_ref[i] for i in range(4))
    moves = []
    for (number, base, k), part in zip(places, parts):
        late = lax.rem(jnp.where(core == 0, my_y, my_x) + (n - k), n)
        for i in range(part.shape[0]):
            to_y = jnp.where(core == 0, late, i)
            to_x = jnp.where(core == 0, i, late)
            for j in range(part.shape[1]):
                to_z = lax.rem(my_z + (nz - base - j), nz)
                moves.append((part.at[i, j], (to_z, to_y, to_x)))
    return moves


def place_kernel(places, cuts, me_ref, *refs):
    parts, outs, sem = refs[: len(places)], refs[len(places) : -1], refs[-1]
    copies = []
    for part, to in block_moves(places, me_ref, parts, outs[0].shape[:3]):
        for (low, high), out in zip(cuts, outs):
            copies.append(
                pltpu.make_async_copy(
                    part.at[:, pl.ds(low, high - low)], out.at[to], sem.at[len(copies)]
                )
            )
            copies[-1].start()
    for copy in copies:
        copy.wait()


def first_kernel(half, places, me_ref, *refs):
    parts, refs = refs[: len(places)], refs[len(places) :]
    if half == 0:
        x_ref, g_ref, beta_ref, cv_ref, bias_ref = refs[:5]
        n_ref, w_ref, pre_ref, qkv_ref, t_ref, wu_ref, pd_ref, b_ref, sem = refs[5:]
    else:
        n_ref, beta_ref, cv_ref, bias_ref = refs[:4]
        w_ref, pre_ref, qkv_ref, t_ref, wu_ref, pd_ref, b_ref, sem = refs[-8:]
    rows = qkv_ref.shape[1] // 2
    frame = rows + HALO
    copies = []
    columns_of = pl.ds(half * 768, 768)
    for part, to in block_moves(places, me_ref, parts, w_ref.shape[:3]):
        copies.append(
            pltpu.make_async_copy(
                part.at[:, columns_of], w_ref.at[to], sem.at[len(copies)]
            )
        )
        copies[-1].start()
    if half == 0:
        x = x_ref[...].astype(F32)
        scale = lax.rsqrt(jnp.mean(x * x, axis=-1, keepdims=True) + EPS)
        n_ref[...] = (x * scale * g_ref[...]).astype(BF16)
    normed = n_ref[...]
    for copy in copies:
        copy.wait()
    pre_ref[0] = dot1(normed, w_ref[...].reshape(D, 768)).astype(BF16)
    linear = dot1(normed, beta_ref[0])
    i, j = grid_masks(rows)
    keys, rights, lowers = [], [], []
    for q in range(2):
        rate = sigmoid(linear[q * frame + HALO : (q + 1) * frame] + bias_ref[0, q : q + 1, :])
        b_ref[0, q * rows : (q + 1) * rows, :] = rate
        ext = pre_ref[0, q * frame : (q + 1) * frame, :].astype(F32)
        conv = conv_of(ext, cv_ref[0], rows)
        act = conv * sigmoid(conv)
        for h in range(2):
            place = pl.ds(q * rows, rows)
            parts = []
            for kind in range(3):
                lane = (kind * 2 + h) * DK
                one = act[:, lane : lane + DK]
                if kind < 2:
                    one = one * lax.rsqrt(jnp.sum(one * one, axis=-1, keepdims=True) + EPS)
                if kind == 0:
                    one = one * DK ** (-0.5)
                one = one.astype(BF16)
                qkv_ref[0, place, lane : lane + DK] = one
                parts.append(one)
            key, value = parts[1], parts[2]
            col = rate[:, h : h + 1]
            keys.append(key)
            rights.append(jnp.concatenate([key, value], axis=1).astype(F32) * col)
            lowers.append(jnp.where(i > j, dot1(key, key, NT) * col, 0.0))
    inverses = unit_inverses(lowers, i, j)
    boths = [dot3(t, r) for t, r in zip(inverses, rights)]
    for p in range(4):
        t_ref[0, p] = inverses[p].astype(BF16)
        wu_ref[0, p] = boths[p].astype(BF16)
    for p in range(4):
        pd_ref[0, p] = dot1(keys[p], boths[p], TN).astype(BF16)


def state_kernel(pd_ref, s_ref):
    count = pd_ref.shape[0]
    state = jnp.zeros((DK, DK), F32)
    for s in range(count):
        s_ref[s] = state.astype(BF16)
        if s + 1 < count:
            high, low = split(state)
            move = pd_ref[s, :, :DK]
            state = state - (dot1(move, high) + dot1(move, low)) + pd_ref[s, :, DK:].astype(F32)


def adjoint_kernel(pd_ref, g_ref, l_ref):
    count = pd_ref.shape[0]
    adjoint = jnp.zeros((DK, DK), F32)
    for s in range(count - 1, -1, -1):
        l_ref[s] = adjoint.astype(BF16)
        if s > 0:
            high, low = split(adjoint)
            move = pd_ref[s, :, :DK]
            adjoint = (
                adjoint - (dot1(move, high, TN) + dot1(move, low, TN)) + g_ref[s].astype(F32)
            )


def pair_places(rows):
    return [
        (q * 2 + h, pl.ds(q * rows, rows), pl.ds(h * DK, DK), h) for q in range(2) for h in range(2)
    ]


def kind_lanes(kind, h):
    return pl.ds((kind * 2 + h) * DK, DK)


def second_kernel(qkv_ref, wu_ref, s_ref, hg_ref, f_ref, m_ref, h_ref):
    rows = qkv_ref.shape[1] // 2
    i, j = grid_masks(rows)
    pairs = pair_places(rows)
    queries = [qkv_ref[0, at, kind_lanes(0, h)] for _, at, _, h in pairs]
    keys = [qkv_ref[0, at, kind_lanes(1, h)] for _, at, _, h in pairs]
    scores = [jnp.where(i >= j, dot1(a, b, NT), 0.0).astype(BF16) for a, b in zip(queries, keys)]
    freshes = [
        (wu_ref[0, p, :, DK:].astype(F32) - dot1(wu_ref[0, p, :, :DK], s_ref[p])).astype(BF16)
        for p, _, _, _ in pairs
    ]
    mixes = [
        dot1(queries[p], s_ref[p]) + dot1(scores[p], freshes[p]) for p, _, _, _ in pairs
    ]
    for p, at, lanes, _ in pairs:
        mixed = mixes[p]
        scale = lax.rsqrt(jnp.mean(mixed * mixed, axis=-1, keepdims=True) + EPS)
        f_ref[at, lanes] = freshes[p]
        m_ref[at, lanes] = mixed
        h_ref[at, lanes] = (mixed * scale * hg_ref[...]).astype(BF16)


def third_kernel(qkv_ref, wu_ref, s_ref, f_ref, m_ref, dh_ref, hg_ref, sg_ref, gf_ref, gq_ref, gk_ref, ghg_ref):
    rows = qkv_ref.shape[1] // 2
    i, j = grid_masks(rows)
    gain = hg_ref[...]
    gain_grad = jnp.zeros((1, DK), F32)
    pairs = pair_places(rows)
    queries = [qkv_ref[0, at, kind_lanes(0, h)] for _, at, _, h in pairs]
    keys = [qkv_ref[0, at, kind_lanes(1, h)] for _, at, _, h in pairs]
    scores = [jnp.where(i >= j, dot1(a, b, NT), 0.0).astype(BF16) for a, b in zip(queries, keys)]
    grads = []
    for _, at, lanes, _ in pairs:
        mixed = m_ref[at, lanes]
        up = dh_ref[at, lanes].astype(F32)
        scale = lax.rsqrt(jnp.mean(mixed * mixed, axis=-1, keepdims=True) + EPS)
        unit = mixed * scale
        gain_grad = gain_grad + jnp.sum(up * unit, axis=0, keepdims=True)
        inner = up * gain
        grad = scale * (inner - unit * jnp.mean(inner * unit, axis=-1, keepdims=True))
        grads.append(grad.astype(BF16))
    ghg_ref[0] = jnp.broadcast_to(gain_grad, ghg_ref.shape[1:])
    fresh_grads = [dot1(a, g, TN) for a, g in zip(scores, grads)]
    starts = [
        dot1(queries[p], grads[p], TN) - dot1(wu_ref[0, p, :, :DK], fresh_grads[p], TN)
        for p in range(4)
    ]
    score_grads = [
        jnp.where(i >= j, dot1(grads[p], f_ref[at, lanes], NT), 0.0).astype(BF16)
        for p, at, lanes, _ in pairs
    ]
    for p, at, lanes, _ in pairs:
        gf_ref[at, lanes] = fresh_grads[p]
        sg_ref[0, p] = starts[p].astype(BF16)
        gq_ref[at, lanes] = dot1(grads[p], s_ref[p], NT) + dot1(score_grads[p], keys[p])
        gk_ref[at, lanes] = dot1(score_grads[p], queries[p], TN)


def fourth_kernel(qkv_ref, pre_ref, cv_ref, b_ref, t_ref, wu_ref, s_ref, l_ref, f_ref, gf_ref, gq_ref, gk_ref, eg_ref, gc_ref, lg_ref, gb_ref):
    rows = qkv_ref.shape[1] // 2
    frame = rows + HALO
    i, j = grid_masks(rows)
    lane = lax.broadcasted_iota(jnp.int32, (rows, DK), 1)
    pairs = pair_places(rows)
    keys = [qkv_ref[0, at, kind_lanes(1, h)] for _, at, _, h in pairs]
    values = [qkv_ref[0, at, kind_lanes(2, h)] for _, at, _, h in pairs]
    cols = [b_ref[0, at, h : h + 1] for _, at, _, h in pairs]
    fresh_grads = [
        gf_ref[at, lanes] + dot1(keys[p], l_ref[p]) for p, at, lanes, _ in pairs
    ]
    lows = [g.astype(BF16) for g in fresh_grads]
    factor_grads = [
        jnp.concatenate([-dot1(lows[p], s_ref[p], NT).astype(BF16), lows[p]], axis=1)
        for p in range(4)
    ]
    solved = [dot1(t_ref[0, p], factor_grads[p], TN) for p in range(4)]
    inners = [dot1(k, k, NT) for k in keys]
    system_grads = [
        jnp.where(i > j, -dot1(solved[p], wu_ref[0, p], NT), 0.0) for p in range(4)
    ]
    inner_grads = [(g * c).astype(BF16) for g, c in zip(system_grads, cols)]
    key_grads = [
        gk_ref[at, lanes]
        + dot1(f_ref[at, lanes], l_ref[p], NT)
        + cols[p] * solved[p][:, :DK]
        + dot1(inner_grads[p], keys[p])
        + dot1(inner_grads[p], keys[p], TN)
        for p, at, lanes, _ in pairs
    ]
    rate_grads = [
        (
            jnp.sum(
                solved[p][:, :DK] * keys[p].astype(F32) + solved[p][:, DK:] * values[p].astype(F32),
                axis=-1,
                keepdims=True,
            )
            + jnp.sum(system_grads[p] * inners[p], axis=-1, keepdims=True)
        )
        * cols[p]
        * (1.0 - cols[p])
        for p in range(4)
    ]
    for q in range(2):
        place = pl.ds(q * rows, rows)
        logit = jnp.where(
            lane == 0, rate_grads[2 * q], jnp.where(lane == 1, rate_grads[2 * q + 1], 0.0)
        )
        lg_ref[0, place, :] = logit.astype(BF16)
        gb_ref[0, q : q + 1, :] = jnp.sum(logit, axis=0, keepdims=True)
    zero = jnp.zeros((HALO, DK), F32)
    for kind in range(3):
        for h in range(2):
            at = kind_lanes(kind, h)
            tap = cv_ref[0, :, at]
            conv_grad = [jnp.zeros((1, DK), F32) for _ in range(CONV)]
            for q in range(2):
                p = q * 2 + h
                ext = pre_ref[0, q * frame : (q + 1) * frame, at].astype(F32)
                views = [ext[HALO - 3 + t : HALO - 3 + t + rows] for t in range(CONV)]
                conv = tap[0:1, :] * views[0]
                for t in range(1, CONV):
                    conv = conv + tap[t : t + 1, :] * views[t]
                sig = sigmoid(conv)
                act = conv * sig
                if kind == 0:
                    grad = gq_ref[q * rows : (q + 1) * rows, h * DK : (h + 1) * DK] * DK ** (-0.5)
                elif kind == 1:
                    grad = key_grads[p]
                else:
                    grad = cols[p] * solved[p][:, DK:]
                if kind < 2:
                    scale = lax.rsqrt(jnp.sum(act * act, axis=-1, keepdims=True) + EPS)
                    unit = act * scale
                    grad = scale * (grad - unit * jnp.sum(grad * unit, axis=-1, keepdims=True))
                grad = grad * (sig * (1.0 + conv * (1.0 - sig)))
                wide = jnp.concatenate([zero, grad, zero], axis=0)
                total = tap[0:1, :] * wide[3 : 3 + frame]
                for t in range(1, CONV):
                    total = total + tap[t : t + 1, :] * wide[3 - t : 3 - t + frame]
                eg_ref[0, q * frame : (q + 1) * frame, at] = total.astype(BF16)
                for t in range(CONV):
                    conv_grad[t] = conv_grad[t] + jnp.sum(grad * views[t], axis=0, keepdims=True)
            for t in range(CONV):
                gc_ref[0, t : t + 1, at] = conv_grad[t]


def lead(*shape):
    return pl.BlockSpec((1,) + shape, lambda p: (p,) + (0,) * len(shape))


def at_half(half, *shape):
    return pl.BlockSpec((1,) + shape, lambda p: (half,) + (0,) * len(shape))


def whole(*shape):
    return pl.BlockSpec(shape, lambda p: (0,) * len(shape))


def columns(rows, cols):
    return pl.BlockSpec((rows, cols), lambda p: (0, p))


def quarter():
    return pl.BlockSpec((4, DK, DK), lambda p: (p, 0, 0))


def cost(microseconds):
    return pl.CostEstimate(
        flops=int(microseconds * 1.15e9), bytes_accessed=0, transcendentals=0
    )


def on_core(kernel, outs, in_specs, out_specs, name, microseconds):
    return pl.pallas_call(
        kernel,
        out_shape=outs,
        grid=(2,),
        in_specs=in_specs,
        out_specs=out_specs,
        compiler_params=pltpu.CompilerParams(
            vmem_limit_bytes=VMEM_LIMIT, dimension_semantics=("arbitrary",)
        ),
        cost_estimate=cost(microseconds),
        name=name,
    )


def sds(shape, kind):
    return jax.ShapeDtypeStruct(shape, kind)


def all_ranges(a):
    if lax.axis_size("z") * lax.axis_size("y") == a.shape[0]:
        return lax.all_to_all(a, SEQ, 0, 0, tiled=True)
    return lax.all_gather(a, SEQ)


def scan_states(every):
    count = lax.axis_size("z") * lax.axis_size("y")
    if every.ndim == 3:
        return pl.pallas_call(
            state_kernel,
            out_shape=sds((count, DK, DK), BF16),
            cost_estimate=cost(3),
            name="state_scan",
        )(every)

    def step(s, state):
        one = lax.dynamic_index_in_dim(every, s, 0, False).astype(F32)
        moved = jnp.einsum(
            "pij,pjk->pik", one[:, :, :DK], state, precision=lax.Precision.HIGHEST
        )
        return state - moved + one[:, :, DK:]

    start = jnp.zeros((every.shape[1], DK, DK), F32)
    return lax.fori_loop(0, lax.axis_index(SEQ), step, start).astype(BF16)


def scan_adjoints(every, grads):
    count = lax.axis_size("z") * lax.axis_size("y")
    if every.ndim == 3:
        return pl.pallas_call(
            adjoint_kernel,
            out_shape=sds((count, DK, DK), BF16),
            cost_estimate=cost(3),
            name="adjoint_scan",
        )(every, grads)

    def step(k, adjoint):
        s = count - 1 - k
        one = lax.dynamic_index_in_dim(every, s, 0, False).astype(F32)
        moved = jnp.einsum(
            "pji,pjk->pik", one[:, :, :DK], adjoint, precision=lax.Precision.HIGHEST
        )
        return adjoint - moved + lax.dynamic_index_in_dim(grads, s, 0, False).astype(F32)

    start = jnp.zeros((every.shape[1], DK, DK), F32)
    steps = count - 1 - lax.axis_index(SEQ)
    return lax.fori_loop(0, steps, step, start).astype(BF16)


def own_range(a):
    if lax.axis_size("z") * lax.axis_size("y") == H:
        return lax.all_to_all(a, SEQ, 0, 0, tiled=True)
    return a


def shards(
    inputs,
    domain_ids,
    norm1_gain,
    w_qkv,
    w_beta,
    conv_weight,
    domain_bias,
    head_gain,
    w_out,
    norm2_gain,
    w_gate_up,
    w_down,
    cotangent,
):
    core = lax.axis_index("core")
    nz, ny, nx = (lax.axis_size(a) for a in ("z", "y", "x"))
    z, y, x = (lax.axis_index(a) for a in ("z", "y", "x"))
    chips = nz * ny * nx
    seq_devices = nz * ny
    rows = inputs.shape[1]
    frame = rows + HALO
    tall = 2 * rows
    drows = w_qkv.shape[0]
    both_rows = 2 * drows
    frows = w_down.shape[0]
    grows = conv_weight.shape[0]
    first = core == 0
    half = H // 2
    fence = lax.optimization_barrier

    q_mine, q_other = core_pick(
        w_qkv.reshape(drows, 3, 2, 2, 256).transpose(2, 0, 3, 1, 4).reshape(2, drows, 1536), core
    )
    q_got = swap(q_other)
    small = jnp.concatenate(
        [norm1_gain, norm2_gain, w_beta.reshape(-1), conv_weight.reshape(-1)]
    )
    n_small = small.shape[0]
    small = jnp.pad(small, (0, 768 - n_small)).reshape(1, 768)
    small_got = swap(small)
    x_own = inputs.reshape(rows, D)
    halo = lax.ppermute(
        x_own[rows - HALO :], SEQ, [(i, i + 1) for i in range(seq_devices - 1)]
    )
    small = jnp.concatenate(
        [jnp.where(first, small, small_got), jnp.where(first, small_got, small)], axis=0
    )
    q_part = chip_rows(q_mine, q_got, core)
    q_part, small, halo, x_own, w_gate_up, w_out, w_down, cotangent = fence(
        (q_part, small, halo, x_own, w_gate_up, w_out, w_down, cotangent)
    )

    q_near = [q_part, turned(q_part, "z", 1)]
    out_cols = w_out.reshape(drows, 2, 2, 256).transpose(1, 2, 0, 3)
    gu_cols = (
        w_gate_up.reshape(drows, 2, chips, 2, frows)
        .transpose(3, 1, 0, 2, 4)
        .reshape(2, 2, drows, FF // 2)
    )
    wide_cols = jnp.concatenate(
        [gu_cols[:, 0], gu_cols[:, 1], out_cols[:, 0], out_cols[:, 1]], axis=-1
    )
    wide_mine, wide_other = core_pick(wide_cols, core)
    wide_part = chip_rows(wide_mine, swap(wide_other), core)
    choose = (domain_ids[0] == jnp.arange(NDOM, dtype=jnp.int32)).astype(BF16)
    bias_own = jnp.sum(domain_bias.astype(F32) * choose.astype(F32)[:, None], axis=0)
    extra = jnp.pad(jnp.concatenate([bias_own.astype(BF16), choose]), (0, D - H - NDOM))
    extra = jnp.pad(extra.reshape(1, D), ((0, HALO - 1), (0, 0)))
    frame_own = jnp.concatenate([halo, x_own, extra], axis=0)
    frame_other = swap(frame_own)
    g_own = cotangent.reshape(rows, D)
    g_other = swap(g_own)
    smalls = plane_fetched(small)
    q_near, smalls, wide_part = fence((q_near, smalls, wide_part))
    smalls = plane_stack(smalls)
    q_rest = [turned(q_near[0], "z", k) for k in range(nz - 1, max(nz - 2, 1), -1)]
    q_u = cross_fetched(jnp.stack(q_near), True)
    q_near, q_rest, q_u, smalls = fence((q_near, q_rest, q_u, smalls))
    smalls = fetched(smalls, "z")
    q_rest = [turned(q_near[0], "z", k) for k in range(2, nz - 1)] + q_rest
    q_u = cross_fetched(cross_stack(q_u), False)
    q_rest, q_u, smalls, frame_own, frame_other, g_own, g_other, wide_part, w_down = fence(
        (q_rest, q_u, smalls, frame_own, frame_other, g_own, g_other, wide_part, w_down)
    )

    q_v = cross_fetched(jnp.stack(q_rest), True)
    smalls = jnp.stack(in_place(smalls, z)).reshape(2 * chips, 768)[:, :n_small]
    gain_one = smalls[:, :drows].reshape(1, D).astype(F32)
    gain_two = smalls[:, drows : 2 * drows].reshape(1, D).astype(F32)
    full_beta = smalls[:, 2 * drows : 2 * drows + drows * H].reshape(D, 2, half)
    full_conv = smalls[:, 2 * drows + drows * H :].reshape(3, 2, 2, 256, CONV)
    beta_mine = lax.dynamic_index_in_dim(full_beta, core, 1, False)
    conv_mine = (
        lax.dynamic_index_in_dim(full_conv, core, 1, False)
        .transpose(1, 3, 0, 2)
        .reshape(2, CONV, 768)
        .astype(F32)
    )
    beta_pairs = jnp.pad(
        beta_mine.reshape(D, 2, 2).transpose(1, 0, 2), ((0, 0), (0, 0), (0, DK - 2))
    )
    ends = sorted({1, nz - 1})
    wide_near = [wide_part, turned(wide_part, "z", 1)]
    q_v, wide_near, w_down, gain_one, gain_two, beta_pairs, conv_mine = fence(
        (q_v, wide_near, w_down, gain_one, gain_two, beta_pairs, conv_mine)
    )

    q_v = cross_fetched(cross_stack(q_v), False)
    wide_rest = [turned(wide_near[0], "z", k) for k in ends[1:]]
    x_frames = jnp.concatenate([frame_own[:frame], frame_other[:frame]], axis=0)
    bias_both = jnp.stack([frame_own[frame, :H], frame_other[frame, :H]]).astype(F32)
    choose_both = jnp.stack(
        [frame_own[frame, H : H + NDOM], frame_other[frame, H : H + NDOM]]
    ).astype(F32)
    bias_mine = lax.dynamic_index_in_dim(bias_both.reshape(2, 2, half), core, 1, False)
    bias_pairs = jnp.pad(
        bias_mine.reshape(2, 2, 2).transpose(1, 0, 2), ((0, 0), (0, 0), (0, DK - 2))
    )
    x_both = jnp.concatenate(
        [frame_own[HALO:frame], frame_other[HALO:frame]], axis=0
    ).astype(F32)
    g_both = jnp.concatenate([g_own, g_other], axis=0)
    (
        q_u,
        q_v,
        wide_near,
        wide_rest,
        w_down,
        gain_one,
        gain_two,
        beta_pairs,
        conv_mine,
        bias_pairs,
        x_frames,
        x_both,
        g_both,
    ) = fence(
        (
            q_u,
            q_v,
            wide_near,
            wide_rest,
            w_down,
            gain_one,
            gain_two,
            beta_pairs,
            conv_mine,
            bias_pairs,
            x_frames,
            x_both,
            g_both,
        )
    )

    q_parts, q_places = q_u + q_v, spots((q_u, q_v))
    blocks = chips
    if both_rows % 16 == 0:
        w_shape = sds((nz, ny, nx, both_rows, 768), BF16)
    else:
        w_shape = sds((1, 1, 1, D, 768), BF16)
        q_parts, q_places, blocks = [assembled((q_u, q_v)).reshape(1, 1, D, 1536)], [(0, 0, 0)], 1
    place = jnp.stack([core, y, x, z]).astype(jnp.int32)
    kept = (
        sds((2, 2 * frame, 768), BF16),
        sds((2, tall, 768), BF16),
        sds((2, 4, rows, rows), BF16),
        sds((2, 4, rows, 2 * DK), BF16),
        sds((2, 4, DK, 2 * DK), BF16),
        sds((2, tall, DK), F32),
    )
    anywhere = pl.BlockSpec(memory_space=pl.ANY)

    def local(number, parts, ins, in_specs, outs, out_specs, held):
        fixed = [at_half(number, D, DK), at_half(number, CONV, 768), at_half(number, 2, DK)]
        first_held = 1 + len(parts) + len(ins) + 3
        return pl.pallas_call(
            functools.partial(first_kernel, number, q_places),
            out_shape=outs + (w_shape,) + kept,
            grid=(1,),
            in_specs=[pl.BlockSpec(memory_space=pltpu.SMEM)]
            + [anywhere] * len(parts)
            + in_specs
            + fixed
            + [anywhere] * len(held),
            out_specs=out_specs
            + (whole(*w_shape.shape),)
            + tuple(at_half(number, *k.shape[1:]) for k in kept),
            scratch_shapes=[pltpu.SemaphoreType.DMA((blocks,))],
            input_output_aliases={
                first_held + k: len(outs) + 1 + k for k in range(len(held))
            },
            compiler_params=pltpu.CompilerParams(vmem_limit_bytes=VMEM_LIMIT),
            cost_estimate=cost(10),
            name="delta_local",
        )(place, *parts, *ins, beta_pairs, conv_mine, bias_pairs, *held)

    wide_rest = [turned(wide_near[0], "z", k) for k in range(2, nz - 1)] + wide_rest
    wide_u = cross_fetched(jnp.stack(wide_near), True)
    normed, w_q_one, *held = local(
        0,
        q_parts,
        (x_frames, gain_one),
        [whole(2 * frame, D), whole(1, D)],
        (sds((2 * frame, D), BF16),),
        (whole(2 * frame, D),),
        (),
    )
    normed, w_q_one, held, wide_rest, wide_u, q_parts, w_down = fence(
        (normed, w_q_one, held, wide_rest, wide_u, q_parts, w_down)
    )

    wide_rest, wide_two = jnp.stack(wide_rest), cross_stack(wide_u)
    wide_v = cross_fetched(wide_rest, True)
    wide_u = cross_fetched(wide_two, False)
    down_z = fetched(w_down, "z")
    w_q_two, *held = local(
        1,
        q_parts,
        (after(normed, wide_rest, wide_two),),
        [whole(2 * frame, D)],
        (),
        (),
        tuple(held),
    )
    pre, qkv, inverse, factors, pd, rates = held
    w_q_one = w_q_one.reshape(D, 768)
    w_q_two = w_q_two.reshape(D, 768)
    (
        normed,
        w_q_one,
        w_q_two,
        pre,
        qkv,
        inverse,
        factors,
        pd,
        rates,
        down_z,
        wide_v,
    ) = fence(
        (
            normed,
            w_q_one,
            w_q_two,
            pre,
            qkv,
            inverse,
            factors,
            pd,
            rates,
            down_z,
            wide_v,
        )
    )

    every = all_ranges(pd.reshape(H, DK, 2 * DK))
    down_stack = jnp.stack(in_place(down_z, z))
    wide_v = cross_fetched(cross_stack(wide_v), False)
    every, wide_u, down_stack = fence((every, wide_u, down_stack))

    states = scan_states(every)
    states = own_range(states)
    down_parts = cross_fetched(after(down_stack, states), True)
    gain_head = head_gain.astype(F32).reshape(1, DK)
    fresh, mixed, heads_mine = on_core(
        second_kernel,
        (sds((tall, 512), BF16), sds((tall, 512), F32), sds((tall, 512), BF16)),
        [lead(tall, 768), lead(4, rows, 2 * DK), quarter(), whole(1, DK)],
        (columns(tall, 256), columns(tall, 256), columns(tall, 256)),
        "delta_mix",
        2,
    )(qkv, factors, states, gain_head)
    heads_got = swap(heads_mine)
    wide_v, states, fresh, mixed, heads_mine, heads_got = fence(
        (wide_v, states, fresh, mixed, heads_mine, heads_got)
    )

    down_parts = cross_fetched(cross_stack(down_parts), False)
    groups = (wide_u, wide_v)

    def placed(cuts, parts):
        return pl.pallas_call(
            functools.partial(place_kernel, spots(groups), cuts),
            out_shape=[sds((nz, ny, nx, both_rows, hi - lo), BF16) for lo, hi in cuts],
            in_specs=[pl.BlockSpec(memory_space=pltpu.SMEM)] + [anywhere] * len(parts),
            out_specs=[pl.BlockSpec(memory_space=pltpu.VMEM)] * len(cuts),
            scratch_shapes=[pltpu.SemaphoreType.DMA((chips * len(cuts),))],
            compiler_params=pltpu.CompilerParams(vmem_limit_bytes=VMEM_LIMIT),
            cost_estimate=cost(3),
            name="placed",
        )(place, *parts)

    out_cuts, gu_cuts = ((FF, FF + D // 2),), ((0, FF // 2), (FF // 2, FF))
    if both_rows % 16 == 0:
        parts = wide_u + wide_v
        (out_mine,) = placed(out_cuts, parts)
        w_gate, w_up = placed(gu_cuts, after(parts, out_mine))
    else:
        wide = assembled(groups)
        out_mine, w_gate, w_up = (wide[..., lo:hi] for lo, hi in out_cuts + gu_cuts)
    out_mine, w_gate, w_up = (a.reshape(D, -1) for a in (out_mine, w_gate, w_up))
    out_got = swap(out_mine)
    full_out = jnp.concatenate(
        [jnp.where(first, out_mine, out_got), jnp.where(first, out_got, out_mine)], axis=1
    )
    heads_got = jnp.concatenate([heads_got[rows:], heads_got[:rows]], axis=0)
    heads = jnp.concatenate(
        [jnp.where(first, heads_mine, heads_got), jnp.where(first, heads_got, heads_mine)], axis=1
    )
    middle = x_both + jnp.dot(heads, full_out, preferred_element_type=F32)
    scale_two = lax.rsqrt(jnp.mean(middle * middle, axis=-1, keepdims=True) + EPS)
    unit_two = middle * scale_two
    normed_two = (unit_two * gain_two).astype(BF16)
    gate = jnp.dot(normed_two, w_gate, preferred_element_type=F32)
    up = jnp.dot(normed_two, w_up, preferred_element_type=F32)
    sig = jax.nn.sigmoid(gate)
    hidden = (gate * sig * up).astype(BF16)
    grad_down = jnp.einsum("nf,nd->fd", hidden, g_both, preferred_element_type=F32).astype(BF16)
    down_shares = late_shares(grid_of(grad_down))
    down_stage = cross_sent(down_shares, False)
    w_down_mine = cross_end(after(down_parts, down_shares)).reshape(chips * frows, D)
    hidden_grad = jnp.einsum("nd,fd->nf", g_both, w_down_mine, preferred_element_type=F32)
    up_grad = (hidden_grad * gate * sig).astype(BF16)
    gate_grad = (hidden_grad * up * sig * (1.0 + gate * (1.0 - sig))).astype(BF16)
    up_grad, gate_grad = fence((up_grad, gate_grad))

    grad_gate = jnp.einsum("nd,nf->df", normed_two, gate_grad, preferred_element_type=F32)
    gate_shares = late_shares(grid_of(grad_gate.astype(BF16)))
    gate_stage = cross_sent(gate_shares, False)
    normed_two_part = jnp.einsum(
        "nf,df->nd", after(gate_grad, gate_shares), w_gate, preferred_element_type=F32
    ) + jnp.einsum("nf,df->nd", up_grad, w_up, preferred_element_type=F32)
    part_low, down_stage = fence((normed_two_part.astype(BF16), down_stage))
    part_got = swap(part_low)
    grad_up = jnp.einsum(
        "nd,nf->df", after(normed_two, part_low), up_grad, preferred_element_type=F32
    ).astype(BF16)
    up_shares = late_shares(grid_of(grad_up))
    up_stage = cross_sent(up_shares, False)
    part_got = after(part_got, up_shares)
    part_got = jnp.concatenate([part_got[rows:], part_got[:rows]], axis=0)
    normed_two_grad = normed_two_part + part_got.astype(F32)
    grad_norm2 = jnp.sum(normed_two_grad[:rows] * unit_two[:rows], axis=0)
    inner = normed_two_grad * gain_two
    middle_grad = g_both.astype(F32) + scale_two * (
        inner - unit_two * jnp.mean(inner * unit_two, axis=-1, keepdims=True)
    )
    middle_low = middle_grad.astype(BF16)
    out_rows = lax.dynamic_slice_in_dim(full_out, core * 512, 512, 0)
    heads_grad = jnp.einsum("ne,de->nd", middle_low, out_rows, preferred_element_type=F32)
    start_grad, fresh_grad, query_grad, key_grad, gain_part = on_core(
        third_kernel,
        (
            sds((2, 4, DK, DK), BF16),
            sds((tall, 512), F32),
            sds((tall, 512), F32),
            sds((tall, 512), F32),
            sds((2, 8, DK), F32),
        ),
        [
            lead(tall, 768),
            lead(4, rows, 2 * DK),
            quarter(),
            columns(tall, 256),
            columns(tall, 256),
            columns(tall, 256),
            whole(1, DK),
        ],
        (
            lead(4, DK, DK),
            columns(tall, 256),
            columns(tall, 256),
            columns(tall, 256),
            lead(8, DK),
        ),
        "delta_back_local",
        5,
    )(qkv, factors, states, fresh, mixed, heads_grad, gain_head)
    (
        start_grad,
        fresh_grad,
        query_grad,
        key_grad,
        gain_part,
        middle_low,
        hidden,
    ) = fence(
        (
            start_grad,
            fresh_grad,
            query_grad,
            key_grad,
            gain_part,
            middle_low,
            hidden,
        )
    )

    start_grads = all_ranges(start_grad.reshape(H, DK, DK))
    low_cols = lax.dynamic_slice_in_dim(middle_low, core * 512, 512, 1)
    grad_out = jnp.einsum("nd,ne->de", heads, low_cols, preferred_element_type=F32)
    out_shares = late_shares(grid_of(grad_out.astype(BF16)))
    out_stage = cross_sent(out_shares, False)
    adjoints = scan_adjoints(every, after(start_grads, out_shares))
    down_shares = early_shares(after(down_stage, adjoints))
    down_stage = cross_sent(down_shares, True)
    gate_shares = early_shares(after(gate_stage, down_shares))
    gate_stage = cross_sent(gate_shares, True)
    up_shares = [
        jnp.concatenate(cut, axis=-1)
        for cut in zip(*(early_shares(stage) for stage in after((up_stage, out_stage), adjoints)))
    ]
    up_stage = cross_sent(up_shares, True)
    down_part = jnp.dot(after(hidden, adjoints), w_down_mine, preferred_element_type=F32)
    output = (middle[:rows] + down_part[:rows]) + swap(down_part[rows:].astype(BF16)).astype(F32)
    output = output.astype(BF16).reshape(1, rows, D)
    adjoints = own_range(adjoints)
    down_shares = shares(added(*after(down_stage, gate_shares)).astype(BF16), "z", 0)
    down_stage = sent(down_shares, "z")
    adjoints = after(adjoints, up_shares, down_shares, output)
    ext_grad, conv_part, logit_low, bias_part = on_core(
        fourth_kernel,
        (
            sds((2, 2 * frame, 768), BF16),
            sds((2, CONV, 768), F32),
            sds((2, tall, DK), BF16),
            sds((2, 2, DK), F32),
        ),
        [
            lead(tall, 768),
            lead(2 * frame, 768),
            lead(CONV, 768),
            lead(tall, DK),
            lead(4, rows, rows),
            lead(4, rows, 2 * DK),
            quarter(),
            quarter(),
            columns(tall, 256),
            columns(tall, 256),
            columns(tall, 256),
            columns(tall, 256),
        ],
        (lead(2 * frame, 768), lead(CONV, 768), lead(tall, DK), lead(2, DK)),
        "delta_back",
        15,
    )(qkv, pre, conv_mine, rates, inverse, factors, states, adjoints, fresh, fresh_grad, query_grad, key_grad)
    ext_grad, conv_part, logit_low, bias_part, gate_stage, up_stage, down_stage = fence(
        (ext_grad, conv_part, logit_low, bias_part, gate_stage, up_stage, down_stage)
    )

    ext_frames = ext_grad.reshape(2, 2, frame, 768)
    grad_q = [
        jnp.einsum("nd,nf->df", normed, e, preferred_element_type=F32).astype(BF16)
        for e in (ext_grad[0], ext_grad[1])
    ]
    q_shares = [
        jnp.concatenate(cut, axis=-1) for cut in zip(*(late_shares(grid_of(g)) for g in grad_q))
    ]
    ext_frames, gate_stage, up_stage, q_shares = fence(
        (ext_frames, gate_stage, up_stage, q_shares)
    )
    q_stage = cross_sent(q_shares, False)
    sent_back = lax.ppermute(
        ext_frames[:, :, :HALO], SEQ, [(i + 1, i) for i in range(seq_devices - 1)]
    )
    wide_part = jnp.concatenate([added(*gate_stage), added(*up_stage)], axis=-1).astype(BF16)
    wide_stage = sent(shares(wide_part, "z", 0), "z")
    tail = ext_frames[:, :, frame - HALO :].astype(F32) + sent_back.astype(F32)
    pre_low = jnp.concatenate(
        [ext_frames[:, :, HALO : frame - HALO], tail.astype(BF16)], axis=2
    ).reshape(2, tall, 768)
    normed_part = (
        jnp.einsum("nf,df->nd", pre_low[0], w_q_one, preferred_element_type=F32)
        + jnp.einsum("nf,df->nd", pre_low[1], w_q_two, preferred_element_type=F32)
        + jnp.einsum("pnh,pdh->nd", logit_low, beta_pairs, preferred_element_type=F32)
    )
    normed_grad = normed_part[:rows] + swap(normed_part[rows:].astype(BF16)).astype(F32)
    q_stage, normed_grad, normed, conv_part, logit_low, x_both = fence(
        (q_stage, normed_grad, normed, conv_part, logit_low, x_both)
    )

    q_shares, normed_grad, x_both = fence((early_shares(q_stage), normed_grad, x_both))
    q_stage = cross_sent(q_shares, True)
    x32 = x_both[:rows]
    scale_one = lax.rsqrt(jnp.mean(x32 * x32, axis=-1, keepdims=True) + EPS)
    unit_one = x32 * scale_one
    grad_norm1 = jnp.sum(normed_grad * unit_one, axis=0)
    inner_one = normed_grad * gain_one
    grad_input = middle_grad[:rows] + scale_one * (
        inner_one - unit_one * jnp.mean(inner_one * unit_one, axis=-1, keepdims=True)
    )
    grad_input = grad_input.reshape(1, rows, D)
    normed_tokens = normed.reshape(2, frame, D)[:, HALO:].reshape(tall, D)
    grad_beta = jnp.einsum(
        "nd,pnh->dph", normed_tokens, logit_low[:, :, :2], preferred_element_type=F32
    ).reshape(D, half)
    beta_full = jnp.where(
        first,
        jnp.pad(grad_beta, ((0, 0), (0, half))),
        jnp.pad(grad_beta, ((0, 0), (half, 0))),
    )
    conv_cols = conv_part.reshape(2, CONV, 3, 256).transpose(2, 0, 3, 1).reshape(3, 512, CONV)
    conv_full = jnp.where(
        first,
        jnp.pad(conv_cols, ((0, 0), (0, 512), (0, 0))),
        jnp.pad(conv_cols, ((0, 0), (512, 0), (0, 0))),
    )
    bias_heads = bias_part[:, :, :2].transpose(1, 0, 2).reshape(2, half)
    bias_heads = jnp.where(
        first,
        jnp.pad(bias_heads, ((0, 0), (0, half))),
        jnp.pad(bias_heads, ((0, 0), (half, 0))),
    )
    bias_grad = jnp.sum(choose_both[:, :, None] * bias_heads[:, None, :], axis=0)
    shared = jnp.concatenate([bias_grad.reshape(-1), gain_part[0, 0] + gain_part[1, 0]])
    shared = jnp.broadcast_to(shared, (2 * chips, shared.shape[0]))
    pack = jnp.concatenate(
        [
            grad_norm2.reshape(2 * chips, drows),
            beta_full.reshape(2 * chips, drows * H),
            conv_full.reshape(2 * chips, grows * CONV),
            shared,
        ],
        axis=1,
    )
    pack = jnp.pad(pack, ((0, 0), (0, -pack.shape[1] % DK)))
    norm_rows = jnp.pad(grad_norm1.reshape(2 * chips, drows), ((0, 0), (0, DK - drows)))
    pack = jnp.concatenate([norm_rows, pack], axis=1).reshape(chips, 2, -1)
    pack_own = lax.dynamic_index_in_dim(pack, core, 1, False)
    pack_got = swap(lax.dynamic_index_in_dim(pack, 1 - core, 1, False))
    pack = plane_shares((pack_own + pack_got).reshape(nz, ny, nx, -1))
    q_stage, pack, grad_input = fence((q_stage, pack, grad_input))

    q_shares = fence(shares(added(*q_stage).astype(BF16), "z", 0))
    q_stage = sent(q_shares, "z")
    pack = plane_sum(pack)
    own_down = added(*after(down_stage, q_shares))
    wide_own = own_rows(added(*after(wide_stage, q_shares)), core)
    own_gu = (
        wide_own[..., :FF]
        .reshape(2, drows, 2, chips, frows)
        .transpose(1, 2, 3, 0, 4)
        .reshape(drows, 2 * FF)
    )
    own_out = wide_own[..., FF:].transpose(1, 0, 2).reshape(drows, D)
    mine = z_sum(pack)
    q_stage, mine, own_gu, own_down, own_out = fence((q_stage, mine, own_gu, own_down, own_out))

    q_own = own_rows(added(*q_stage), core)
    own_qkv = (
        q_own.reshape(2, drows, 2, 3, 256).transpose(1, 3, 0, 2, 4).reshape(drows, 3 * D)
    )
    own_g1 = mine[:drows]
    at = DK
    own_g2 = mine[at : at + drows]
    at += drows
    own_beta = mine[at : at + drows * H].reshape(drows, H)
    at += drows * H
    own_conv = mine[at : at + grows * CONV].reshape(grows, CONV)
    at += grows * CONV
    bias_total = mine[at : at + NDOM * H].reshape(NDOM, H)
    at += NDOM * H
    gain_total = mine[at : at + DK]
    return (
        output,
        grad_input,
        own_g1,
        own_qkv,
        own_beta,
        own_conv,
        bias_total,
        gain_total,
        own_out,
        own_g2,
        own_gu,
        own_down,
    )


def solution(mesh):
    seq, batch = mesh.shape["seq"], mesh.shape["batch"]
    plane = batch // 2
    fine = Mesh(mesh.devices.reshape(seq // plane, plane, plane, 2), ALL)
    tokens = P(("x", "core"), ("z", "y"), None)
    rows = P(ALL, None)
    vector = P(ALL)
    return jax.shard_map(
        shards,
        mesh=fine,
        in_specs=(
            tokens,
            P(("x", "core")),
            vector,
            rows,
            rows,
            rows,
            P(),
            P(),
            rows,
            vector,
            rows,
            rows,
            tokens,
        ),
        out_specs=(
            tokens,
            tokens,
            vector,
            rows,
            rows,
            rows,
            P(),
            P(),
            rows,
            vector,
            rows,
            rows,
        ),
        check_vma=False,
    )
```

```python
import functools

import jax
import jax.numpy as jnp
from jax import lax
from jax.experimental import pallas as pl
from jax.experimental.pallas import tpu as pltpu
from jax.sharding import Mesh
from jax.sharding import PartitionSpec as P

D = 1024
H = 8
DK = 128
FF = 2816
CONV = 4
NDOM = 4
EPS = 1e-06
HALO = 16
F32 = jnp.float32
BF16 = jnp.bfloat16
SEQ = ("z", "y")
ALL = ("z", "y", "x", "core")
VMEM_LIMIT = 60 * 1024 * 1024


def swap(a):
    return lax.ppermute(a, "core", [(0, 1), (1, 0)])


def turned(a, axis, by):
    n = lax.axis_size(axis)
    return lax.ppermute(a, axis, [(i, (i + by) % n) for i in range(n)])


def after(a, *others):
    return lax.optimization_barrier((a, others))[0]


def in_place(parts, me):
    n = len(parts)
    if n == 2:
        first = me == 0
        return [jnp.where(first, *parts), jnp.where(first, *parts[::-1])]
    if n <= 4:
        return [lax.select_n((me - i) % n, *parts) for i in range(n)]
    back = parts[:0:-1] + parts[:1]
    wide = jnp.stack(back + back)
    return list(lax.dynamic_slice_in_dim(wide, n - 1 - me, n, axis=0))


def fetched(a, axis):
    return [a] + [turned(a, axis, k) for k in range(1, lax.axis_size(axis))]


def gather_axis(a, axis, dim):
    if lax.axis_size(axis) == 1:
        return jnp.expand_dims(a, dim)
    return jnp.stack(in_place(fetched(a, axis), lax.axis_index(axis)), axis=dim)


def shares(a, axis, dim):
    n, me = lax.axis_size(axis), lax.axis_index(axis)
    return [lax.dynamic_index_in_dim(a, (me + k) % n, dim, False) for k in range(n)]


def sent(parts, axis):
    return parts[0], [turned(a, axis, k) for k, a in enumerate(parts) if k]


def sends(a, axis, dim):
    return sent(shares(a, axis, dim), axis)


def added(own, got):
    total = own.astype(F32)
    for part in got:
        total = total + part.astype(F32)
    return total


def crossed(a, early, by):
    n = lax.axis_size("x")
    pairs = []
    for y in range(n):
        for x in range(n):
            for core in range(2):
                along_x = (core == 0) == early
                to_x = (x + by) % n if along_x else x
                to_y = y if along_x else (y + by) % n
                pairs.append(((y * n + x) * 2 + core, (to_y * n + to_x) * 2 + core))
    return lax.ppermute(a, ("y", "x", "core"), pairs)


def cross_place(early):
    along_x = (lax.axis_index("core") == 0) == early
    return jnp.where(along_x, lax.axis_index("x"), lax.axis_index("y"))


def cross_fetched(a, early):
    return [a] + [crossed(a, early, k) for k in range(1, lax.axis_size("x"))]


def cross_stack(parts):
    return jnp.stack(in_place(parts, cross_place(True)))


def cross_end(parts):
    every = jnp.stack(in_place(parts, cross_place(False)))
    first = lax.axis_index("core") == 0
    return jnp.where(first, every, jnp.swapaxes(every, 0, 1)).transpose(2, 0, 1, 3, 4)


def assembled(groups):
    first = lax.axis_index("core") == 0
    far = []
    for parts in groups:
        every = jnp.stack(in_place(parts, cross_place(False)))
        grid = jnp.where(first, every, jnp.swapaxes(every, 0, 1))
        far += [grid[:, :, j] for j in range(grid.shape[2])]
    return jnp.stack(in_place(far, lax.axis_index("z")))


def spots(groups):
    out, base = [], 0
    for parts in groups:
        for k, part in enumerate(parts):
            out.append((len(out), base, k))
        base += parts[0].shape[1]
    return out


def grid_of(a):
    nz, ny, nx = (lax.axis_size(axis) for axis in ("z", "y", "x"))
    return a.reshape(nz, ny, nx, -1, a.shape[-1])


def late_shares(a):
    n = lax.axis_size("x")
    first = lax.axis_index("core") == 0
    y, x = lax.axis_index("y"), lax.axis_index("x")
    return [
        jnp.where(
            first,
            lax.dynamic_index_in_dim(a, (y + k) % n, 1, False),
            lax.dynamic_index_in_dim(a, (x + k) % n, 2, False),
        )
        for k in range(n)
    ]


def early_shares(stage):
    total = added(*stage).astype(BF16)
    n, me = lax.axis_size("x"), cross_place(True)
    return [lax.dynamic_index_in_dim(total, (me + k) % n, 1, False) for k in range(n)]


def cross_sent(parts, early):
    return parts[0], [crossed(a, early, k) for k, a in enumerate(parts) if k]


def core_pick(a, core):
    return (
        lax.dynamic_index_in_dim(a, core, 0, False),
        lax.dynamic_index_in_dim(a, 1 - core, 0, False),
    )


def chip_rows(mine, got, core):
    first = core == 0
    return jnp.concatenate(
        [jnp.where(first, mine, got), jnp.where(first, got, mine)], axis=-2
    )


def own_rows(total, core):
    mine, other = core_pick(total.reshape(2, -1, total.shape[-1]), core)
    got = swap(other)
    first = core == 0
    return jnp.stack([jnp.where(first, mine, got), jnp.where(first, got, mine)], axis=0)


def z_sum(a):
    parts = in_place([p if k == 0 else turned(p, "z", k) for k, p in enumerate(shares(a, "z", 0))], lax.axis_index("z"))
    total = parts[0]
    for part in parts[1:]:
        total = total + part
    return total


def plane_step(a, k):
    n = lax.axis_size("x")
    ky, kx = divmod(k, n)
    pairs = [(j * n + i, (j + ky) % n * n + (i + kx) % n) for j in range(n) for i in range(n)]
    return lax.ppermute(a, ("y", "x"), pairs)


def plane_fetched(a):
    return [a] + [plane_step(a, k) for k in range(1, lax.axis_size("x") ** 2)]


def plane_order(parts):
    n = lax.axis_size("x")
    rows_of = [in_place(parts[k * n : (k + 1) * n], lax.axis_index("x")) for k in range(n)]
    columns_of = [in_place([r[i] for r in rows_of], lax.axis_index("y")) for i in range(n)]
    return [[columns_of[i][j] for i in range(n)] for j in range(n)]


def plane_stack(parts):
    return jnp.stack([jnp.stack(row) for row in plane_order(parts)])


def plane_shares(a):
    n = lax.axis_size("x")
    y, x = lax.axis_index("y"), lax.axis_index("x")
    out = []
    for k in range(n * n):
        ky, kx = divmod(k, n)
        one = lax.dynamic_index_in_dim(a, (y + ky) % n, 1, False)
        out.append(lax.dynamic_index_in_dim(one, (x + kx) % n, 1, False))
    return out


def plane_sum(shares):
    parts = [a if k == 0 else plane_step(a, k) for k, a in enumerate(shares)]
    total = None
    for row in plane_order(parts):
        for part in row:
            total = part if total is None else total + part
    return total


def dot1(a, b, dims=((1,), (0,))):
    return lax.dot_general(
        a.astype(BF16), b.astype(BF16), (dims, ((), ())), preferred_element_type=F32
    )


TN = ((0,), (0,))
NT = ((1,), (1,))


def split(a):
    high = a.astype(BF16)
    return high, (a - high.astype(F32)).astype(BF16)


def dot3(a, b):
    ah, al = split(a)
    bh, bl = split(b)
    return dot1(ah, bh) + (dot1(ah, bl) + dot1(al, bh))


def sigmoid(v):
    return 1.0 / (1.0 + jnp.exp(-v))


def grid_masks(n):
    i = lax.broadcasted_iota(jnp.int32, (n, n), 0)
    j = lax.broadcasted_iota(jnp.int32, (n, n), 1)
    return i, j


def unit_inverses(lowers, i, j):
    n = lowers[0].shape[0]
    level = jnp.where(i > j, i ^ j, 0)
    eye = jnp.where(i == j, 1.0, 0.0).astype(F32)
    highs = [a.astype(BF16) for a in lowers]
    lows = [(a - h.astype(F32)).astype(BF16) for a, h in zip(lowers, highs)]
    inverses = [eye - jnp.where(level == 1, a, 0.0) for a in lowers]
    size = 2
    while size < n:
        corner = (level >= size) & (level < 2 * size)
        lefts = [t.astype(BF16) for t in inverses]
        inner = [dot1(jnp.where(corner, h, jnp.zeros_like(h)), t) for h, t in zip(highs, lefts)]
        inverses = [t - dot1(b, c) for t, b, c in zip(inverses, lefts, inner)]
        size *= 2
    parts = [split(t) for t in inverses]
    rests = [
        eye - t - (dot1(h, th) + (dot1(h, tl) + dot1(lo, th)))
        for t, h, lo, (th, tl) in zip(inverses, highs, lows, parts)
    ]
    return [t + dot1(th, r) for t, (th, _), r in zip(inverses, parts, rests)]


def conv_of(ext, taps, rows):
    total = taps[0:1, :] * ext[HALO - 3 : HALO - 3 + rows]
    for i in range(1, CONV):
        total = total + taps[i : i + 1, :] * ext[HALO - 3 + i : HALO - 3 + i + rows]
    return total


def block_moves(places, me_ref, parts, grid):
    nz, n, _ = grid
    core, my_y, my_x, my_z = (me_ref[i] for i in range(4))
    moves = []
    for (number, base, k), part in zip(places, parts):
        late = lax.rem(jnp.where(core == 0, my_y, my_x) + (n - k), n)
        for i in range(part.shape[0]):
            to_y = jnp.where(core == 0, late, i)
            to_x = jnp.where(core == 0, i, late)
            for j in range(part.shape[1]):
                to_z = lax.rem(my_z + (nz - base - j), nz)
                moves.append((part.at[i, j], (to_z, to_y, to_x)))
    return moves


def place_kernel(places, cuts, grid, me_ref, *refs):
    parts, outs, sem = refs[: len(places)], refs[-1 - len(cuts) : -1], refs[-1]
    copies = []
    for part, to in block_moves(places, me_ref, parts, grid):
        for (low, high), out in zip(cuts, outs):
            copies.append(
                pltpu.make_async_copy(
                    part.at[:, pl.ds(low, high - low)], out.at[to], sem.at[len(copies)]
                )
            )
            copies[-1].start()
    for copy in copies:
        copy.wait()


def first_kernel(half, places, me_ref, *refs):
    parts, refs = refs[: len(places)], refs[len(places) :]
    if half == 0:
        x_ref, g_ref, beta_ref, cv_ref, bias_ref = refs[:5]
        n_ref, w_ref, pre_ref, qkv_ref, t_ref, wu_ref, pd_ref, b_ref, sem = refs[5:]
    else:
        n_ref, beta_ref, cv_ref, bias_ref = refs[:4]
        w_ref, pre_ref, qkv_ref, t_ref, wu_ref, pd_ref, b_ref, sem = refs[-8:]
    rows = qkv_ref.shape[1] // 2
    frame = rows + HALO
    copies = []
    columns_of = pl.ds(half * 768, 768)
    for part, to in block_moves(places, me_ref, parts, w_ref.shape[:3]):
        copies.append(
            pltpu.make_async_copy(
                part.at[:, columns_of], w_ref.at[to], sem.at[len(copies)]
            )
        )
        copies[-1].start()
    if half == 0:
        x = x_ref[...].astype(F32)
        scale = lax.rsqrt(jnp.mean(x * x, axis=-1, keepdims=True) + EPS)
        n_ref[...] = (x * scale * g_ref[...]).astype(BF16)
    normed = n_ref[...]
    for copy in copies:
        copy.wait()
    pre_ref[0] = dot1(normed, w_ref[...].reshape(D, 768)).astype(BF16)
    linear = dot1(normed, beta_ref[0])
    i, j = grid_masks(rows)
    keys, rights, lowers = [], [], []
    for q in range(2):
        rate = sigmoid(linear[q * frame + HALO : (q + 1) * frame] + bias_ref[0, q : q + 1, :])
        b_ref[0, q * rows : (q + 1) * rows, :] = rate
        ext = pre_ref[0, q * frame : (q + 1) * frame, :].astype(F32)
        conv = conv_of(ext, cv_ref[0], rows)
        act = conv * sigmoid(conv)
        for h in range(2):
            place = pl.ds(q * rows, rows)
            parts = []
            for kind in range(3):
                lane = (kind * 2 + h) * DK
                one = act[:, lane : lane + DK]
                if kind < 2:
                    one = one * lax.rsqrt(jnp.sum(one * one, axis=-1, keepdims=True) + EPS)
                if kind == 0:
                    one = one * DK ** (-0.5)
                one = one.astype(BF16)
                qkv_ref[0, place, lane : lane + DK] = one
                parts.append(one)
            key, value = parts[1], parts[2]
            col = rate[:, h : h + 1]
            keys.append(key)
            rights.append(jnp.concatenate([key, value], axis=1).astype(F32) * col)
            lowers.append(jnp.where(i > j, dot1(key, key, NT) * col, 0.0))
    inverses = unit_inverses(lowers, i, j)
    boths = [dot3(t, r) for t, r in zip(inverses, rights)]
    for p in range(4):
        t_ref[0, p] = inverses[p].astype(BF16)
        wu_ref[0, p] = boths[p].astype(BF16)
    for p in range(4):
        pd_ref[0, p] = dot1(keys[p], boths[p], TN).astype(BF16)


def state_kernel(pd_ref, s_ref):
    count = pd_ref.shape[0]
    state = jnp.zeros((DK, DK), F32)
    for s in range(count):
        s_ref[s] = state.astype(BF16)
        if s + 1 < count:
            high, low = split(state)
            move = pd_ref[s, :, :DK]
            state = state - (dot1(move, high) + dot1(move, low)) + pd_ref[s, :, DK:].astype(F32)


def adjoint_kernel(pd_ref, g_ref, l_ref):
    count = pd_ref.shape[0]
    adjoint = jnp.zeros((DK, DK), F32)
    for s in range(count - 1, -1, -1):
        l_ref[s] = adjoint.astype(BF16)
        if s > 0:
            high, low = split(adjoint)
            move = pd_ref[s, :, :DK]
            adjoint = (
                adjoint - (dot1(move, high, TN) + dot1(move, low, TN)) + g_ref[s].astype(F32)
            )


def pair_places(rows):
    return [
        (q * 2 + h, pl.ds(q * rows, rows), pl.ds(h * DK, DK), h) for q in range(2) for h in range(2)
    ]


def kind_lanes(kind, h):
    return pl.ds((kind * 2 + h) * DK, DK)


def second_kernel(qkv_ref, wu_ref, s_ref, hg_ref, f_ref, m_ref, h_ref):
    rows = qkv_ref.shape[1] // 2
    i, j = grid_masks(rows)
    pairs = pair_places(rows)
    queries = [qkv_ref[0, at, kind_lanes(0, h)] for _, at, _, h in pairs]
    keys = [qkv_ref[0, at, kind_lanes(1, h)] for _, at, _, h in pairs]
    scores = [jnp.where(i >= j, dot1(a, b, NT), 0.0).astype(BF16) for a, b in zip(queries, keys)]
    freshes = [
        (wu_ref[0, p, :, DK:].astype(F32) - dot1(wu_ref[0, p, :, :DK], s_ref[p])).astype(BF16)
        for p, _, _, _ in pairs
    ]
    mixes = [
        dot1(queries[p], s_ref[p]) + dot1(scores[p], freshes[p]) for p, _, _, _ in pairs
    ]
    for p, at, lanes, _ in pairs:
        mixed = mixes[p]
        scale = lax.rsqrt(jnp.mean(mixed * mixed, axis=-1, keepdims=True) + EPS)
        f_ref[at, lanes] = freshes[p]
        m_ref[at, lanes] = mixed
        h_ref[at, lanes] = (mixed * scale * hg_ref[...]).astype(BF16)


def third_kernel(qkv_ref, wu_ref, s_ref, f_ref, m_ref, dh_ref, hg_ref, sg_ref, gf_ref, gq_ref, gk_ref, ghg_ref):
    rows = qkv_ref.shape[1] // 2
    i, j = grid_masks(rows)
    gain = hg_ref[...]
    gain_grad = jnp.zeros((1, DK), F32)
    pairs = pair_places(rows)
    queries = [qkv_ref[0, at, kind_lanes(0, h)] for _, at, _, h in pairs]
    keys = [qkv_ref[0, at, kind_lanes(1, h)] for _, at, _, h in pairs]
    scores = [jnp.where(i >= j, dot1(a, b, NT), 0.0).astype(BF16) for a, b in zip(queries, keys)]
    grads = []
    for _, at, lanes, _ in pairs:
        mixed = m_ref[at, lanes]
        up = dh_ref[at, lanes].astype(F32)
        scale = lax.rsqrt(jnp.mean(mixed * mixed, axis=-1, keepdims=True) + EPS)
        unit = mixed * scale
        gain_grad = gain_grad + jnp.sum(up * unit, axis=0, keepdims=True)
        inner = up * gain
        grad = scale * (inner - unit * jnp.mean(inner * unit, axis=-1, keepdims=True))
        grads.append(grad.astype(BF16))
    ghg_ref[0] = jnp.broadcast_to(gain_grad, ghg_ref.shape[1:])
    fresh_grads = [dot1(a, g, TN) for a, g in zip(scores, grads)]
    starts = [
        dot1(queries[p], grads[p], TN) - dot1(wu_ref[0, p, :, :DK], fresh_grads[p], TN)
        for p in range(4)
    ]
    score_grads = [
        jnp.where(i >= j, dot1(grads[p], f_ref[at, lanes], NT), 0.0).astype(BF16)
        for p, at, lanes, _ in pairs
    ]
    for p, at, lanes, _ in pairs:
        gf_ref[at, lanes] = fresh_grads[p]
        sg_ref[0, p] = starts[p].astype(BF16)
        gq_ref[at, lanes] = dot1(grads[p], s_ref[p], NT) + dot1(score_grads[p], keys[p])
        gk_ref[at, lanes] = dot1(score_grads[p], queries[p], TN)


def fourth_kernel(qkv_ref, pre_ref, cv_ref, b_ref, t_ref, wu_ref, s_ref, l_ref, f_ref, gf_ref, gq_ref, gk_ref, eg_ref, gc_ref, lg_ref, gb_ref):
    rows = qkv_ref.shape[1] // 2
    frame = rows + HALO
    i, j = grid_masks(rows)
    lane = lax.broadcasted_iota(jnp.int32, (rows, DK), 1)
    pairs = pair_places(rows)
    keys = [qkv_ref[0, at, kind_lanes(1, h)] for _, at, _, h in pairs]
    values = [qkv_ref[0, at, kind_lanes(2, h)] for _, at, _, h in pairs]
    cols = [b_ref[0, at, h : h + 1] for _, at, _, h in pairs]
    fresh_grads = [
        gf_ref[at, lanes] + dot1(keys[p], l_ref[p]) for p, at, lanes, _ in pairs
    ]
    lows = [g.astype(BF16) for g in fresh_grads]
    factor_grads = [
        jnp.concatenate([-dot1(lows[p], s_ref[p], NT).astype(BF16), lows[p]], axis=1)
        for p in range(4)
    ]
    solved = [dot1(t_ref[0, p], factor_grads[p], TN) for p in range(4)]
    inners = [dot1(k, k, NT) for k in keys]
    system_grads = [
        jnp.where(i > j, -dot1(solved[p], wu_ref[0, p], NT), 0.0) for p in range(4)
    ]
    inner_grads = [(g * c).astype(BF16) for g, c in zip(system_grads, cols)]
    key_grads = [
        gk_ref[at, lanes]
        + dot1(f_ref[at, lanes], l_ref[p], NT)
        + cols[p] * solved[p][:, :DK]
        + dot1(inner_grads[p], keys[p])
        + dot1(inner_grads[p], keys[p], TN)
        for p, at, lanes, _ in pairs
    ]
    rate_grads = [
        (
            jnp.sum(
                solved[p][:, :DK] * keys[p].astype(F32) + solved[p][:, DK:] * values[p].astype(F32),
                axis=-1,
                keepdims=True,
            )
            + jnp.sum(system_grads[p] * inners[p], axis=-1, keepdims=True)
        )
        * cols[p]
        * (1.0 - cols[p])
        for p in range(4)
    ]
    for q in range(2):
        place = pl.ds(q * rows, rows)
        logit = jnp.where(
            lane == 0, rate_grads[2 * q], jnp.where(lane == 1, rate_grads[2 * q + 1], 0.0)
        )
        lg_ref[0, place, :] = logit.astype(BF16)
        gb_ref[0, q : q + 1, :] = jnp.sum(logit, axis=0, keepdims=True)
    zero = jnp.zeros((HALO, DK), F32)
    for kind in range(3):
        for h in range(2):
            at = kind_lanes(kind, h)
            tap = cv_ref[0, :, at]
            conv_grad = [jnp.zeros((1, DK), F32) for _ in range(CONV)]
            for q in range(2):
                p = q * 2 + h
                ext = pre_ref[0, q * frame : (q + 1) * frame, at].astype(F32)
                views = [ext[HALO - 3 + t : HALO - 3 + t + rows] for t in range(CONV)]
                conv = tap[0:1, :] * views[0]
                for t in range(1, CONV):
                    conv = conv + tap[t : t + 1, :] * views[t]
                sig = sigmoid(conv)
                act = conv * sig
                if kind == 0:
                    grad = gq_ref[q * rows : (q + 1) * rows, h * DK : (h + 1) * DK] * DK ** (-0.5)
                elif kind == 1:
                    grad = key_grads[p]
                else:
                    grad = cols[p] * solved[p][:, DK:]
                if kind < 2:
                    scale = lax.rsqrt(jnp.sum(act * act, axis=-1, keepdims=True) + EPS)
                    unit = act * scale
                    grad = scale * (grad - unit * jnp.sum(grad * unit, axis=-1, keepdims=True))
                grad = grad * (sig * (1.0 + conv * (1.0 - sig)))
                wide = jnp.concatenate([zero, grad, zero], axis=0)
                total = tap[0:1, :] * wide[3 : 3 + frame]
                for t in range(1, CONV):
                    total = total + tap[t : t + 1, :] * wide[3 - t : 3 - t + frame]
                eg_ref[0, q * frame : (q + 1) * frame, at] = total.astype(BF16)
                for t in range(CONV):
                    conv_grad[t] = conv_grad[t] + jnp.sum(grad * views[t], axis=0, keepdims=True)
            for t in range(CONV):
                gc_ref[0, t : t + 1, at] = conv_grad[t]


def lead(*shape):
    return pl.BlockSpec((1,) + shape, lambda p: (p,) + (0,) * len(shape))


def at_half(half, *shape):
    return pl.BlockSpec((1,) + shape, lambda p: (half,) + (0,) * len(shape))


def whole(*shape):
    return pl.BlockSpec(shape, lambda p: (0,) * len(shape))


def columns(rows, cols):
    return pl.BlockSpec((rows, cols), lambda p: (0, p))


def quarter():
    return pl.BlockSpec((4, DK, DK), lambda p: (p, 0, 0))


def cost(microseconds):
    return pl.CostEstimate(
        flops=int(microseconds * 1.15e9), bytes_accessed=0, transcendentals=0
    )


def on_core(kernel, outs, in_specs, out_specs, name, microseconds):
    return pl.pallas_call(
        kernel,
        out_shape=outs,
        grid=(2,),
        in_specs=in_specs,
        out_specs=out_specs,
        compiler_params=pltpu.CompilerParams(
            vmem_limit_bytes=VMEM_LIMIT, dimension_semantics=("arbitrary",)
        ),
        cost_estimate=cost(microseconds),
        name=name,
    )


def sds(shape, kind):
    return jax.ShapeDtypeStruct(shape, kind)


def all_ranges(a):
    if lax.axis_size("z") * lax.axis_size("y") == a.shape[0]:
        return lax.all_to_all(a, SEQ, 0, 0, tiled=True)
    return lax.all_gather(a, SEQ)


def scan_states(every):
    count = lax.axis_size("z") * lax.axis_size("y")
    if every.ndim == 3:
        return pl.pallas_call(
            state_kernel,
            out_shape=sds((count, DK, DK), BF16),
            cost_estimate=cost(3),
            name="state_scan",
        )(every)

    def step(s, state):
        one = lax.dynamic_index_in_dim(every, s, 0, False).astype(F32)
        moved = jnp.einsum(
            "pij,pjk->pik", one[:, :, :DK], state, precision=lax.Precision.HIGHEST
        )
        return state - moved + one[:, :, DK:]

    start = jnp.zeros((every.shape[1], DK, DK), F32)
    return lax.fori_loop(0, lax.axis_index(SEQ), step, start).astype(BF16)


def scan_adjoints(every, grads):
    count = lax.axis_size("z") * lax.axis_size("y")
    if every.ndim == 3:
        return pl.pallas_call(
            adjoint_kernel,
            out_shape=sds((count, DK, DK), BF16),
            cost_estimate=cost(3),
            name="adjoint_scan",
        )(every, grads)

    def step(k, adjoint):
        s = count - 1 - k
        one = lax.dynamic_index_in_dim(every, s, 0, False).astype(F32)
        moved = jnp.einsum(
            "pji,pjk->pik", one[:, :, :DK], adjoint, precision=lax.Precision.HIGHEST
        )
        return adjoint - moved + lax.dynamic_index_in_dim(grads, s, 0, False).astype(F32)

    start = jnp.zeros((every.shape[1], DK, DK), F32)
    steps = count - 1 - lax.axis_index(SEQ)
    return lax.fori_loop(0, steps, step, start).astype(BF16)


def own_range(a):
    if lax.axis_size("z") * lax.axis_size("y") == H:
        return lax.all_to_all(a, SEQ, 0, 0, tiled=True)
    return a


def shards(
    inputs,
    domain_ids,
    norm1_gain,
    w_qkv,
    w_beta,
    conv_weight,
    domain_bias,
    head_gain,
    w_out,
    norm2_gain,
    w_gate_up,
    w_down,
    cotangent,
):
    core = lax.axis_index("core")
    nz, ny, nx = (lax.axis_size(a) for a in ("z", "y", "x"))
    z, y, x = (lax.axis_index(a) for a in ("z", "y", "x"))
    chips = nz * ny * nx
    seq_devices = nz * ny
    rows = inputs.shape[1]
    frame = rows + HALO
    tall = 2 * rows
    drows = w_qkv.shape[0]
    both_rows = 2 * drows
    frows = w_down.shape[0]
    grows = conv_weight.shape[0]
    first = core == 0
    half = H // 2
    fence = lax.optimization_barrier

    q_mine, q_other = core_pick(
        w_qkv.reshape(drows, 3, 2, 2, 256).transpose(2, 0, 3, 1, 4).reshape(2, drows, 1536), core
    )
    q_got = swap(q_other)
    small = jnp.concatenate(
        [norm1_gain, norm2_gain, w_beta.reshape(-1), conv_weight.reshape(-1)]
    )
    n_small = small.shape[0]
    small = jnp.pad(small, (0, 768 - n_small)).reshape(1, 768)
    small_got = swap(small)
    x_own = inputs.reshape(rows, D)
    small = jnp.concatenate(
        [jnp.where(first, small, small_got), jnp.where(first, small_got, small)], axis=1
    )
    small = jnp.pad(small, ((0, 7), (0, 0)))
    q_part = jnp.concatenate([chip_rows(q_mine, q_got, core), small], axis=0)
    q_part, x_own, w_gate_up, w_out, w_down, cotangent = fence(
        (q_part, x_own, w_gate_up, w_out, w_down, cotangent)
    )

    q_far = fetched(q_part, "z")
    out_cols = w_out.reshape(drows, 2, 2, 256).transpose(1, 2, 0, 3)
    gu_cols = (
        w_gate_up.reshape(drows, 2, chips, 2, frows)
        .transpose(3, 1, 0, 2, 4)
        .reshape(2, 2, drows, FF // 2)
    )
    wide_cols = jnp.concatenate(
        [gu_cols[:, 0], gu_cols[:, 1], out_cols[:, 0], out_cols[:, 1]], axis=-1
    )
    wide_mine, wide_other = core_pick(wide_cols, core)
    wide_part = chip_rows(wide_mine, swap(wide_other), core)
    q_far, x_own, cotangent, wide_part, w_down = fence(
        (q_far, x_own, cotangent, wide_part, w_down)
    )
    halo = lax.ppermute(
        x_own[rows - HALO :], SEQ, [(i, i + 1) for i in range(seq_devices - 1)]
    )
    choose = (domain_ids[0] == jnp.arange(NDOM, dtype=jnp.int32)).astype(BF16)
    bias_own = jnp.sum(domain_bias.astype(F32) * choose.astype(F32)[:, None], axis=0)
    extra = jnp.pad(jnp.concatenate([bias_own.astype(BF16), choose]), (0, D - H - NDOM))
    extra = jnp.pad(extra.reshape(1, D), ((0, HALO - 1), (0, 0)))
    frame_own = jnp.concatenate([halo, x_own, extra], axis=0)
    frame_other = swap(frame_own)
    g_own = cotangent.reshape(rows, D)
    g_other = swap(g_own)

    q_parts = cross_fetched(jnp.stack([a[:both_rows] for a in q_far]), True)
    smalls = jnp.stack(in_place([a[both_rows].reshape(2, 768) for a in q_far], z))
    smalls = plane_fetched(smalls)
    ends = sorted({1, nz - 1})
    wide_near = [wide_part, turned(wide_part, "z", 1)]
    q_parts, wide_near, w_down, smalls = fence((q_parts, wide_near, w_down, smalls))
    smalls = plane_stack(smalls).transpose(2, 0, 1, 3, 4).reshape(2 * chips, 768)[:, :n_small]
    gain_one = smalls[:, :drows].reshape(1, D).astype(F32)
    gain_two = smalls[:, drows : 2 * drows].reshape(1, D).astype(F32)
    full_beta = smalls[:, 2 * drows : 2 * drows + drows * H].reshape(D, 2, half)
    full_conv = smalls[:, 2 * drows + drows * H :].reshape(3, 2, 2, 256, CONV)
    beta_mine = lax.dynamic_index_in_dim(full_beta, core, 1, False)
    conv_mine = (
        lax.dynamic_index_in_dim(full_conv, core, 1, False)
        .transpose(1, 3, 0, 2)
        .reshape(2, CONV, 768)
        .astype(F32)
    )
    beta_pairs = jnp.pad(
        beta_mine.reshape(D, 2, 2).transpose(1, 0, 2), ((0, 0), (0, 0), (0, DK - 2))
    )

    q_parts = cross_fetched(cross_stack(q_parts), False)
    wide_rest = [turned(wide_near[0], "z", k) for k in ends[1:]]
    x_frames = jnp.concatenate([frame_own[:frame], frame_other[:frame]], axis=0)
    bias_both = jnp.stack([frame_own[frame, :H], frame_other[frame, :H]]).astype(F32)
    choose_both = jnp.stack(
        [frame_own[frame, H : H + NDOM], frame_other[frame, H : H + NDOM]]
    ).astype(F32)
    bias_mine = lax.dynamic_index_in_dim(bias_both.reshape(2, 2, half), core, 1, False)
    bias_pairs = jnp.pad(
        bias_mine.reshape(2, 2, 2).transpose(1, 0, 2), ((0, 0), (0, 0), (0, DK - 2))
    )
    x_both = jnp.concatenate(
        [frame_own[HALO:frame], frame_other[HALO:frame]], axis=0
    ).astype(F32)
    g_both = jnp.concatenate([g_own, g_other], axis=0)
    (
        q_parts,
        wide_near,
        wide_rest,
        w_down,
        gain_one,
        gain_two,
        beta_pairs,
        conv_mine,
        bias_pairs,
        x_frames,
        x_both,
        g_both,
    ) = fence(
        (
            q_parts,
            wide_near,
            wide_rest,
            w_down,
            gain_one,
            gain_two,
            beta_pairs,
            conv_mine,
            bias_pairs,
            x_frames,
            x_both,
            g_both,
        )
    )

    q_places = spots((q_parts,))
    blocks = chips
    if both_rows % 16 == 0:
        w_shape = sds((nz, ny, nx, both_rows, 768), BF16)
    else:
        w_shape = sds((1, 1, 1, D, 768), BF16)
        q_parts, q_places, blocks = [assembled((q_parts,)).reshape(1, 1, D, 1536)], [(0, 0, 0)], 1
    place = jnp.stack([core, y, x, z]).astype(jnp.int32)
    kept = (
        sds((2, 2 * frame, 768), BF16),
        sds((2, tall, 768), BF16),
        sds((2, 4, rows, rows), BF16),
        sds((2, 4, rows, 2 * DK), BF16),
        sds((2, 4, DK, 2 * DK), BF16),
        sds((2, tall, DK), F32),
    )
    anywhere = pl.BlockSpec(memory_space=pl.ANY)

    def local(number, parts, ins, in_specs, outs, out_specs, held):
        fixed = [at_half(number, D, DK), at_half(number, CONV, 768), at_half(number, 2, DK)]
        first_held = 1 + len(parts) + len(ins) + 3
        return pl.pallas_call(
            functools.partial(first_kernel, number, q_places),
            out_shape=outs + (w_shape,) + kept,
            grid=(1,),
            in_specs=[pl.BlockSpec(memory_space=pltpu.SMEM)]
            + [anywhere] * len(parts)
            + in_specs
            + fixed
            + [anywhere] * len(held),
            out_specs=out_specs
            + (whole(*w_shape.shape),)
            + tuple(at_half(number, *k.shape[1:]) for k in kept),
            scratch_shapes=[pltpu.SemaphoreType.DMA((blocks,))],
            input_output_aliases={
                first_held + k: len(outs) + 1 + k for k in range(len(held))
            },
            compiler_params=pltpu.CompilerParams(vmem_limit_bytes=VMEM_LIMIT),
            cost_estimate=cost(10),
            name="delta_local",
        )(place, *parts, *ins, beta_pairs, conv_mine, bias_pairs, *held)

    wide_rest = [turned(wide_near[0], "z", k) for k in range(2, nz - 1)] + wide_rest
    wide_u = cross_fetched(jnp.stack(wide_near), True)
    normed, w_q_one, *held = local(
        0,
        q_parts,
        (x_frames, gain_one),
        [whole(2 * frame, D), whole(1, D)],
        (sds((2 * frame, D), BF16),),
        (whole(2 * frame, D),),
        (),
    )
    normed, w_q_one, held, wide_rest, wide_u, q_parts, w_down = fence(
        (normed, w_q_one, held, wide_rest, wide_u, q_parts, w_down)
    )

    wide_rest, wide_two = jnp.stack(wide_rest), cross_stack(wide_u)
    wide_v = cross_fetched(wide_rest, True)
    wide_u = cross_fetched(wide_two, False)
    down_z = fetched(w_down, "z")
    w_q_two, *held = local(
        1,
        q_parts,
        (after(normed, wide_rest, wide_two),),
        [whole(2 * frame, D)],
        (),
        (),
        tuple(held),
    )
    pre, qkv, inverse, factors, pd, rates = held
    w_q_one = w_q_one.reshape(D, 768)
    w_q_two = w_q_two.reshape(D, 768)
    (
        normed,
        w_q_one,
        w_q_two,
        pre,
        qkv,
        inverse,
        factors,
        pd,
        rates,
        down_z,
        wide_v,
    ) = fence(
        (
            normed,
            w_q_one,
            w_q_two,
            pre,
            qkv,
            inverse,
            factors,
            pd,
            rates,
            down_z,
            wide_v,
        )
    )

    every = all_ranges(pd.reshape(H, DK, 2 * DK))
    down_stack = jnp.stack(in_place(down_z, z))
    wide_v = cross_fetched(cross_stack(wide_v), False)
    every, wide_u, down_stack = fence((every, wide_u, down_stack))

    states = scan_states(every)
    def placed(parts, places, held):
        return pl.pallas_call(
            functools.partial(place_kernel, places, cuts, (nz, ny, nx)),
            out_shape=[sds((nz, ny, nx, both_rows, hi - lo), BF16) for lo, hi in cuts],
            in_specs=[pl.BlockSpec(memory_space=pltpu.SMEM)]
            + [pl.BlockSpec(memory_space=pltpu.VMEM)] * len(parts)
            + [anywhere] * len(held),
            out_specs=[anywhere] * len(cuts),
            input_output_aliases={1 + len(parts) + k: k for k in range(len(held))},
            scratch_shapes=[
                pltpu.SemaphoreType.DMA(
                    (sum(p.shape[0] * p.shape[1] for p in parts) * len(cuts),)
                )
            ],
            compiler_params=pltpu.CompilerParams(vmem_limit_bytes=VMEM_LIMIT),
            cost_estimate=cost(3),
            name="placed",
        )(place, *parts, *held)

    cuts = ((FF, FF + D // 2), (0, FF // 2), (FF // 2, FF))
    wide_places = spots((wide_u, wide_v))
    wide = ()
    if both_rows % 16 == 0:
        wide = tuple(placed(after(wide_u, states), wide_places[: len(wide_u)], ()))
    states = after(own_range(states), wide)
    down_parts = cross_fetched(after(down_stack, wide), True)
    gain_head = head_gain.astype(F32).reshape(1, DK)
    fresh, mixed, heads_mine = on_core(
        second_kernel,
        (sds((tall, 512), BF16), sds((tall, 512), F32), sds((tall, 512), BF16)),
        [lead(tall, 768), lead(4, rows, 2 * DK), quarter(), whole(1, DK)],
        (columns(tall, 256), columns(tall, 256), columns(tall, 256)),
        "delta_mix",
        2,
    )(qkv, factors, states, gain_head)
    heads_got = swap(heads_mine)
    wide, wide_v, states, fresh, mixed, heads_mine, heads_got = fence(
        (wide, wide_v, states, fresh, mixed, heads_mine, heads_got)
    )

    down_parts = cross_fetched(cross_stack(down_parts), False)
    if both_rows % 16 == 0:
        out_mine, w_gate, w_up = placed(wide_v, wide_places[len(wide_u) :], wide)
    else:
        wide = assembled((wide_u, wide_v))
        out_mine, w_gate, w_up = (wide[..., lo:hi] for lo, hi in cuts)
    out_mine, w_gate, w_up = (a.reshape(D, -1) for a in (out_mine, w_gate, w_up))
    out_got = swap(out_mine)
    full_out = jnp.concatenate(
        [jnp.where(first, out_mine, out_got), jnp.where(first, out_got, out_mine)], axis=1
    )
    heads_got = jnp.concatenate([heads_got[rows:], heads_got[:rows]], axis=0)
    heads = jnp.concatenate(
        [jnp.where(first, heads_mine, heads_got), jnp.where(first, heads_got, heads_mine)], axis=1
    )
    middle = x_both + jnp.dot(heads, full_out, preferred_element_type=F32)
    scale_two = lax.rsqrt(jnp.mean(middle * middle, axis=-1, keepdims=True) + EPS)
    unit_two = middle * scale_two
    normed_two = (unit_two * gain_two).astype(BF16)
    gate = jnp.dot(normed_two, w_gate, preferred_element_type=F32)
    up = jnp.dot(normed_two, w_up, preferred_element_type=F32)
    sig = jax.nn.sigmoid(gate)
    hidden = (gate * sig * up).astype(BF16)
    grad_down = jnp.einsum("nf,nd->fd", hidden, g_both, preferred_element_type=F32).astype(BF16)
    down_shares = late_shares(grid_of(grad_down))
    down_stage = cross_sent(down_shares, False)
    w_down_mine = cross_end(after(down_parts, down_shares)).reshape(chips * frows, D)
    hidden_grad = jnp.einsum("nd,fd->nf", g_both, w_down_mine, preferred_element_type=F32)
    up_grad = (hidden_grad * gate * sig).astype(BF16)
    gate_grad = (hidden_grad * up * sig * (1.0 + gate * (1.0 - sig))).astype(BF16)
    up_grad, gate_grad = fence((up_grad, gate_grad))

    grad_gate = jnp.einsum("nd,nf->df", normed_two, gate_grad, preferred_element_type=F32)
    gate_shares = late_shares(grid_of(grad_gate.astype(BF16)))
    gate_stage = cross_sent(gate_shares, False)
    normed_two_part = jnp.einsum(
        "nf,df->nd", after(gate_grad, gate_shares), w_gate, preferred_element_type=F32
    ) + jnp.einsum("nf,df->nd", up_grad, w_up, preferred_element_type=F32)
    part_low = normed_two_part.astype(BF16)
    part_got, down_stage = fence((swap(part_low), down_stage))
    grad_up = jnp.einsum(
        "nd,nf->df", after(normed_two, part_low), up_grad, preferred_element_type=F32
    ).astype(BF16)
    up_shares = late_shares(grid_of(grad_up))
    up_stage = cross_sent(up_shares, False)
    part_got = after(part_got, up_shares)
    part_got = jnp.concatenate([part_got[rows:], part_got[:rows]], axis=0)
    normed_two_grad = normed_two_part + part_got.astype(F32)
    grad_norm2 = jnp.sum(normed_two_grad[:rows] * unit_two[:rows], axis=0)
    inner = normed_two_grad * gain_two
    middle_grad = g_both.astype(F32) + scale_two * (
        inner - unit_two * jnp.mean(inner * unit_two, axis=-1, keepdims=True)
    )
    middle_low = middle_grad.astype(BF16)
    out_rows = lax.dynamic_slice_in_dim(full_out, core * 512, 512, 0)
    heads_grad = jnp.einsum("ne,de->nd", middle_low, out_rows, preferred_element_type=F32)
    start_grad, fresh_grad, query_grad, key_grad, gain_part = on_core(
        third_kernel,
        (
            sds((2, 4, DK, DK), BF16),
            sds((tall, 512), F32),
            sds((tall, 512), F32),
            sds((tall, 512), F32),
            sds((2, 8, DK), F32),
        ),
        [
            lead(tall, 768),
            lead(4, rows, 2 * DK),
            quarter(),
            columns(tall, 256),
            columns(tall, 256),
            columns(tall, 256),
            whole(1, DK),
        ],
        (
            lead(4, DK, DK),
            columns(tall, 256),
            columns(tall, 256),
            columns(tall, 256),
            lead(8, DK),
        ),
        "delta_back_local",
        5,
    )(qkv, factors, states, fresh, mixed, heads_grad, gain_head)
    (
        start_grad,
        fresh_grad,
        query_grad,
        key_grad,
        gain_part,
        middle_low,
        hidden,
    ) = fence(
        (
            start_grad,
            fresh_grad,
            query_grad,
            key_grad,
            gain_part,
            middle_low,
            hidden,
        )
    )

    start_grads = all_ranges(start_grad.reshape(H, DK, DK))
    low_cols = lax.dynamic_slice_in_dim(middle_low, core * 512, 512, 1)
    grad_out = jnp.einsum("nd,ne->de", heads, low_cols, preferred_element_type=F32)
    out_shares = late_shares(grid_of(grad_out.astype(BF16)))
    out_stage = cross_sent(out_shares, False)
    adjoints = scan_adjoints(every, after(start_grads, out_shares))
    down_shares = early_shares(after(down_stage, adjoints))
    down_stage = cross_sent(down_shares, True)
    gate_shares = early_shares(after(gate_stage, down_shares))
    gate_stage = cross_sent(gate_shares, True)
    up_shares = [
        jnp.concatenate(cut, axis=-1)
        for cut in zip(*(early_shares(stage) for stage in after((up_stage, out_stage), adjoints)))
    ]
    up_stage = cross_sent(up_shares, True)
    down_part = jnp.dot(after(hidden, adjoints), w_down_mine, preferred_element_type=F32)
    output = (middle[:rows] + down_part[:rows]) + swap(down_part[rows:].astype(BF16)).astype(F32)
    output = output.astype(BF16).reshape(1, rows, D)
    adjoints = own_range(adjoints)
    down_shares = shares(added(*after(down_stage, gate_shares)).astype(BF16), "z", 0)
    down_stage = sent(down_shares, "z")
    adjoints = after(adjoints, up_shares, down_shares, output)
    ext_grad, conv_part, logit_low, bias_part = on_core(
        fourth_kernel,
        (
            sds((2, 2 * frame, 768), BF16),
            sds((2, CONV, 768), F32),
            sds((2, tall, DK), BF16),
            sds((2, 2, DK), F32),
        ),
        [
            lead(tall, 768),
            lead(2 * frame, 768),
            lead(CONV, 768),
            lead(tall, DK),
            lead(4, rows, rows),
            lead(4, rows, 2 * DK),
            quarter(),
            quarter(),
            columns(tall, 256),
            columns(tall, 256),
            columns(tall, 256),
            columns(tall, 256),
        ],
        (lead(2 * frame, 768), lead(CONV, 768), lead(tall, DK), lead(2, DK)),
        "delta_back",
        15,
    )(qkv, pre, conv_mine, rates, inverse, factors, states, adjoints, fresh, fresh_grad, query_grad, key_grad)
    ext_grad, conv_part, logit_low, bias_part, gate_stage, up_stage, down_stage = fence(
        (ext_grad, conv_part, logit_low, bias_part, gate_stage, up_stage, down_stage)
    )

    ext_frames = ext_grad.reshape(2, 2, frame, 768)
    grad_q = [
        jnp.einsum("nd,nf->df", normed, e, preferred_element_type=F32).astype(BF16)
        for e in (ext_grad[0], ext_grad[1])
    ]
    q_shares = [
        jnp.concatenate(cut, axis=-1) for cut in zip(*(late_shares(grid_of(g)) for g in grad_q))
    ]
    ext_frames, gate_stage, up_stage, q_shares = fence(
        (ext_frames, gate_stage, up_stage, q_shares)
    )
    q_stage = cross_sent(q_shares, False)
    sent_back = lax.ppermute(
        ext_frames[:, :, :HALO], SEQ, [(i + 1, i) for i in range(seq_devices - 1)]
    )
    wide_part = jnp.concatenate([added(*gate_stage), added(*up_stage)], axis=-1).astype(BF16)
    wide_stage = sent(shares(wide_part, "z", 0), "z")
    tail = ext_frames[:, :, frame - HALO :].astype(F32) + sent_back.astype(F32)
    pre_low = jnp.concatenate(
        [ext_frames[:, :, HALO : frame - HALO], tail.astype(BF16)], axis=2
    ).reshape(2, tall, 768)
    normed_part = (
        jnp.einsum("nf,df->nd", pre_low[0], w_q_one, preferred_element_type=F32)
        + jnp.einsum("nf,df->nd", pre_low[1], w_q_two, preferred_element_type=F32)
        + jnp.einsum("pnh,pdh->nd", logit_low, beta_pairs, preferred_element_type=F32)
    )
    part_low, wide_first = fence((normed_part[rows:].astype(BF16), wide_stage[1][0]))
    wide_stage = (wide_stage[0], [wide_first] + wide_stage[1][1:])
    normed_grad = normed_part[:rows] + swap(part_low).astype(F32)
    q_stage, normed_grad, normed, conv_part, logit_low, x_both = fence(
        (q_stage, normed_grad, normed, conv_part, logit_low, x_both)
    )

    q_shares, normed_grad, x_both = fence((early_shares(q_stage), normed_grad, x_both))
    q_stage = cross_sent(q_shares, True)
    x32 = x_both[:rows]
    scale_one = lax.rsqrt(jnp.mean(x32 * x32, axis=-1, keepdims=True) + EPS)
    unit_one = x32 * scale_one
    grad_norm1 = jnp.sum(normed_grad * unit_one, axis=0)
    inner_one = normed_grad * gain_one
    grad_input = middle_grad[:rows] + scale_one * (
        inner_one - unit_one * jnp.mean(inner_one * unit_one, axis=-1, keepdims=True)
    )
    grad_input = grad_input.reshape(1, rows, D)
    normed_tokens = normed.reshape(2, frame, D)[:, HALO:].reshape(tall, D)
    grad_beta = jnp.einsum(
        "nd,pnh->dph", normed_tokens, logit_low[:, :, :2], preferred_element_type=F32
    ).reshape(D, half)
    beta_full = jnp.where(
        first,
        jnp.pad(grad_beta, ((0, 0), (0, half))),
        jnp.pad(grad_beta, ((0, 0), (half, 0))),
    )
    conv_cols = conv_part.reshape(2, CONV, 3, 256).transpose(2, 0, 3, 1).reshape(3, 512, CONV)
    conv_full = jnp.where(
        first,
        jnp.pad(conv_cols, ((0, 0), (0, 512), (0, 0))),
        jnp.pad(conv_cols, ((0, 0), (512, 0), (0, 0))),
    )
    bias_heads = bias_part[:, :, :2].transpose(1, 0, 2).reshape(2, half)
    bias_heads = jnp.where(
        first,
        jnp.pad(bias_heads, ((0, 0), (0, half))),
        jnp.pad(bias_heads, ((0, 0), (half, 0))),
    )
    bias_grad = jnp.sum(choose_both[:, :, None] * bias_heads[:, None, :], axis=0)
    shared = jnp.concatenate([bias_grad.reshape(-1), gain_part[0, 0] + gain_part[1, 0]])
    shared = jnp.broadcast_to(shared, (2 * chips, shared.shape[0]))
    pack = jnp.concatenate(
        [
            grad_norm2.reshape(2 * chips, drows),
            beta_full.reshape(2 * chips, drows * H),
            conv_full.reshape(2 * chips, grows * CONV),
            shared,
        ],
        axis=1,
    )
    pack = jnp.pad(pack, ((0, 0), (0, -pack.shape[1] % DK)))
    norm_rows = jnp.pad(grad_norm1.reshape(2 * chips, drows), ((0, 0), (0, DK - drows)))
    pack = jnp.concatenate([norm_rows, pack], axis=1).reshape(chips, 2, -1)
    pack_own = lax.dynamic_index_in_dim(pack, core, 1, False)
    pack_got = swap(lax.dynamic_index_in_dim(pack, 1 - core, 1, False))
    pack = plane_shares((pack_own + pack_got).reshape(nz, ny, nx, -1))
    q_stage, pack = fence((q_stage, pack))

    q_shares = fence(shares(added(*q_stage).astype(BF16), "z", 0))
    q_stage = sent(q_shares, "z")
    pack = plane_sum(pack)
    own_down = added(*after(down_stage, q_shares))
    wide_own = own_rows(added(*after(wide_stage, q_shares)), core)
    own_gu = (
        wide_own[..., :FF]
        .reshape(2, drows, 2, chips, frows)
        .transpose(1, 2, 3, 0, 4)
        .reshape(drows, 2 * FF)
    )
    own_out = wide_own[..., FF:].transpose(1, 0, 2).reshape(drows, D)
    mine = z_sum(pack)
    q_stage, mine, own_gu, own_down, own_out = fence((q_stage, mine, own_gu, own_down, own_out))

    q_own = own_rows(added(*q_stage), core)
    own_qkv = jnp.concatenate(
        [
            q_own[c, :, (hp * 3 + kind) * 256 : (hp * 3 + kind + 1) * 256]
            for kind in range(3)
            for c in range(2)
            for hp in range(2)
        ],
        axis=1,
    )
    own_g1 = mine[:drows]
    at = DK
    own_g2 = mine[at : at + drows]
    at += drows
    own_beta = mine[at : at + drows * H].reshape(drows, H)
    at += drows * H
    own_conv = mine[at : at + grows * CONV].reshape(grows, CONV)
    at += grows * CONV
    bias_total = mine[at : at + NDOM * H].reshape(NDOM, H)
    at += NDOM * H
    gain_total = mine[at : at + DK]
    return (
        output,
        grad_input,
        own_g1,
        own_qkv,
        own_beta,
        own_conv,
        bias_total,
        gain_total,
        own_out,
        own_g2,
        own_gu,
        own_down,
    )


def solution(mesh):
    seq, batch = mesh.shape["seq"], mesh.shape["batch"]
    plane = batch // 2
    fine = Mesh(mesh.devices.reshape(seq // plane, plane, plane, 2), ALL)
    tokens = P(("x", "core"), ("z", "y"), None)
    rows = P(ALL, None)
    vector = P(ALL)
    return jax.shard_map(
        shards,
        mesh=fine,
        in_specs=(
            tokens,
            P(("x", "core")),
            vector,
            rows,
            rows,
            rows,
            P(),
            P(),
            rows,
            vector,
            rows,
            rows,
            tokens,
        ),
        out_specs=(
            tokens,
            tokens,
            vector,
            rows,
            rows,
            rows,
            P(),
            P(),
            rows,
            vector,
            rows,
            rows,
        ),
        check_vma=False,
    )
```

```python
import functools

import jax
import jax.numpy as jnp
from jax import lax
from jax.experimental import pallas as pl
from jax.experimental.pallas import tpu as pltpu
from jax.sharding import Mesh
from jax.sharding import PartitionSpec as P

D = 1024
H = 8
DK = 128
FF = 2816
CONV = 4
NDOM = 4
EPS = 1e-06
HALO = 16
F32 = jnp.float32
BF16 = jnp.bfloat16
SEQ = ("z", "y")
ALL = ("z", "y", "x", "core")
VMEM_LIMIT = 60 * 1024 * 1024


def swap(a):
    return lax.ppermute(a, "core", [(0, 1), (1, 0)])


def turned(a, axis, by):
    n = lax.axis_size(axis)
    return lax.ppermute(a, axis, [(i, (i + by) % n) for i in range(n)])


def after(a, *others):
    return lax.optimization_barrier((a, others))[0]


def in_place(parts, me):
    n = len(parts)
    if n == 2:
        first = me == 0
        return [jnp.where(first, *parts), jnp.where(first, *parts[::-1])]
    if n <= 4:
        return [lax.select_n((me - i) % n, *parts) for i in range(n)]
    back = parts[:0:-1] + parts[:1]
    wide = jnp.stack(back + back)
    return list(lax.dynamic_slice_in_dim(wide, n - 1 - me, n, axis=0))


def fetched(a, axis):
    return [a] + [turned(a, axis, k) for k in range(1, lax.axis_size(axis))]


def relayed(near, axis):
    n = lax.axis_size(axis)
    if n < 4:
        return near
    before, behind = [near[1]], [near[-1]]
    while len(before) < n // 2:
        before.append(turned(before[-1], axis, 1))
    while len(before) + len(behind) < n - 1:
        behind.append(turned(behind[-1], axis, n - 1))
    return near[:1] + before + behind[::-1]


def gather_axis(a, axis, dim):
    if lax.axis_size(axis) == 1:
        return jnp.expand_dims(a, dim)
    return jnp.stack(in_place(fetched(a, axis), lax.axis_index(axis)), axis=dim)


def shares(a, axis, dim):
    n, me = lax.axis_size(axis), lax.axis_index(axis)
    return [lax.dynamic_index_in_dim(a, (me + k) % n, dim, False) for k in range(n)]


def sent(parts, axis):
    return parts[0], [turned(a, axis, k) for k, a in enumerate(parts) if k]


def sends(a, axis, dim):
    return sent(shares(a, axis, dim), axis)


def added(own, got):
    total = own.astype(F32)
    for part in got:
        total = total + part.astype(F32)
    return total


def relays(parts, axis):
    n = lax.axis_size(axis)
    sums = []
    for chain, by in ((parts[n // 2 : 0 : -1], 1), (parts[n // 2 + 1 :], n - 1)):
        total = chain[0]
        for part in chain[1:]:
            total = added(part, [turned(total, axis, by)]).astype(BF16)
        sums.append(total)
    return parts[0], *sums


def crossed(a, early, by):
    n = lax.axis_size("x")
    pairs = []
    for y in range(n):
        for x in range(n):
            for core in range(2):
                along_x = (core == 0) == early
                to_x = (x + by) % n if along_x else x
                to_y = y if along_x else (y + by) % n
                pairs.append(((y * n + x) * 2 + core, (to_y * n + to_x) * 2 + core))
    return lax.ppermute(a, ("y", "x", "core"), pairs)


def cross_place(early):
    along_x = (lax.axis_index("core") == 0) == early
    return jnp.where(along_x, lax.axis_index("x"), lax.axis_index("y"))


def cross_fetched(a, early):
    return [a] + [crossed(a, early, k) for k in range(1, lax.axis_size("x"))]


def cross_stack(parts):
    return jnp.stack(in_place(parts, cross_place(True)))


def cross_end(parts):
    every = jnp.stack(in_place(parts, cross_place(False)))
    first = lax.axis_index("core") == 0
    return jnp.where(first, every, jnp.swapaxes(every, 0, 1)).transpose(2, 0, 1, 3, 4)


def assembled(groups):
    first = lax.axis_index("core") == 0
    far = []
    for parts in groups:
        every = jnp.stack(in_place(parts, cross_place(False)))
        grid = jnp.where(first, every, jnp.swapaxes(every, 0, 1))
        far += [grid[:, :, j] for j in range(grid.shape[2])]
    return jnp.stack(in_place(far, lax.axis_index("z")))


def spots(groups):
    out, base = [], 0
    for parts in groups:
        for k, part in enumerate(parts):
            out.append((len(out), base, k))
        base += parts[0].shape[1]
    return out


def grid_of(a):
    nz, ny, nx = (lax.axis_size(axis) for axis in ("z", "y", "x"))
    return a.reshape(nz, ny, nx, -1, a.shape[-1])


def late_shares(a):
    n = lax.axis_size("x")
    first = lax.axis_index("core") == 0
    y, x = lax.axis_index("y"), lax.axis_index("x")
    return [
        jnp.where(
            first,
            lax.dynamic_index_in_dim(a, (y + k) % n, 1, False),
            lax.dynamic_index_in_dim(a, (x + k) % n, 2, False),
        )
        for k in range(n)
    ]


def early_shares(stage):
    total = added(*stage).astype(BF16)
    n, me = lax.axis_size("x"), cross_place(True)
    return [lax.dynamic_index_in_dim(total, (me + k) % n, 1, False) for k in range(n)]


def cross_sent(parts, early):
    return parts[0], [crossed(a, early, k) for k, a in enumerate(parts) if k]


def core_pick(a, core):
    return (
        lax.dynamic_index_in_dim(a, core, 0, False),
        lax.dynamic_index_in_dim(a, 1 - core, 0, False),
    )


def chip_rows(mine, got, core):
    first = core == 0
    return jnp.concatenate(
        [jnp.where(first, mine, got), jnp.where(first, got, mine)], axis=-2
    )


def own_rows(total, core):
    mine, other = core_pick(total.reshape(2, -1, total.shape[-1]), core)
    got = swap(other)
    first = core == 0
    return jnp.stack([jnp.where(first, mine, got), jnp.where(first, got, mine)], axis=0)


def z_sum(a):
    parts = in_place([p if k == 0 else turned(p, "z", k) for k, p in enumerate(shares(a, "z", 0))], lax.axis_index("z"))
    total = parts[0]
    for part in parts[1:]:
        total = total + part
    return total


def plane_step(a, k):
    n = lax.axis_size("x")
    ky, kx = divmod(k, n)
    pairs = [(j * n + i, (j + ky) % n * n + (i + kx) % n) for j in range(n) for i in range(n)]
    return lax.ppermute(a, ("y", "x"), pairs)


def plane_fetched(a):
    return [a] + [plane_step(a, k) for k in range(1, lax.axis_size("x") ** 2)]


def plane_order(parts):
    n = lax.axis_size("x")
    rows_of = [in_place(parts[k * n : (k + 1) * n], lax.axis_index("x")) for k in range(n)]
    columns_of = [in_place([r[i] for r in rows_of], lax.axis_index("y")) for i in range(n)]
    return [[columns_of[i][j] for i in range(n)] for j in range(n)]


def plane_stack(parts):
    return jnp.stack([jnp.stack(row) for row in plane_order(parts)])


def plane_shares(a):
    n = lax.axis_size("x")
    y, x = lax.axis_index("y"), lax.axis_index("x")
    out = []
    for k in range(n * n):
        ky, kx = divmod(k, n)
        one = lax.dynamic_index_in_dim(a, (y + ky) % n, 1, False)
        out.append(lax.dynamic_index_in_dim(one, (x + kx) % n, 1, False))
    return out


def plane_sum(shares):
    parts = [a if k == 0 else plane_step(a, k) for k, a in enumerate(shares)]
    total = None
    for row in plane_order(parts):
        for part in row:
            total = part if total is None else total + part
    return total


def dot1(a, b, dims=((1,), (0,))):
    return lax.dot_general(
        a.astype(BF16), b.astype(BF16), (dims, ((), ())), preferred_element_type=F32
    )


TN = ((0,), (0,))
NT = ((1,), (1,))


def split(a):
    high = a.astype(BF16)
    return high, (a - high.astype(F32)).astype(BF16)


def dot3(a, b):
    ah, al = split(a)
    bh, bl = split(b)
    return dot1(ah, bh) + (dot1(ah, bl) + dot1(al, bh))


def sigmoid(v):
    return 1.0 / (1.0 + jnp.exp(-v))


def grid_masks(n):
    i = lax.broadcasted_iota(jnp.int32, (n, n), 0)
    j = lax.broadcasted_iota(jnp.int32, (n, n), 1)
    return i, j


def unit_inverses(lowers, i, j):
    n = lowers[0].shape[0]
    level = jnp.where(i > j, i ^ j, 0)
    eye = jnp.where(i == j, 1.0, 0.0).astype(F32)
    highs = [a.astype(BF16) for a in lowers]
    lows = [(a - h.astype(F32)).astype(BF16) for a, h in zip(lowers, highs)]
    inverses = [eye - jnp.where(level == 1, a, 0.0) for a in lowers]
    size = 2
    while size < n:
        corner = (level >= size) & (level < 2 * size)
        lefts = [t.astype(BF16) for t in inverses]
        inner = [dot1(jnp.where(corner, h, jnp.zeros_like(h)), t) for h, t in zip(highs, lefts)]
        inverses = [t - dot1(b, c) for t, b, c in zip(inverses, lefts, inner)]
        size *= 2
    parts = [split(t) for t in inverses]
    rests = [
        eye - t - (dot1(h, th) + (dot1(h, tl) + dot1(lo, th)))
        for t, h, lo, (th, tl) in zip(inverses, highs, lows, parts)
    ]
    return [t + dot1(th, r) for t, (th, _), r in zip(inverses, parts, rests)]


def conv_of(ext, taps, rows):
    total = taps[0:1, :] * ext[HALO - 3 : HALO - 3 + rows]
    for i in range(1, CONV):
        total = total + taps[i : i + 1, :] * ext[HALO - 3 + i : HALO - 3 + i + rows]
    return total


def block_moves(places, me_ref, parts, grid):
    nz, n, _ = grid
    core, my_y, my_x, my_z = (me_ref[i] for i in range(4))
    moves = []
    for (number, base, k), part in zip(places, parts):
        late = lax.rem(jnp.where(core == 0, my_y, my_x) + (n - k), n)
        for i in range(part.shape[0]):
            to_y = jnp.where(core == 0, late, i)
            to_x = jnp.where(core == 0, i, late)
            for j in range(part.shape[1]):
                to_z = lax.rem(my_z + (nz - base - j), nz)
                moves.append((part.at[i, j], (to_z, to_y, to_x)))
    return moves


def place_kernel(places, cuts, grid, me_ref, *refs):
    parts, outs, sem = refs[: len(places)], refs[-1 - len(cuts) : -1], refs[-1]
    copies = []
    for part, to in block_moves(places, me_ref, parts, grid):
        for (low, high), out in zip(cuts, outs):
            copies.append(
                pltpu.make_async_copy(
                    part.at[:, pl.ds(low, high - low)], out.at[to], sem.at[len(copies)]
                )
            )
            copies[-1].start()
    for copy in copies:
        copy.wait()


def first_kernel(half, places, me_ref, *refs):
    parts, refs = refs[: len(places)], refs[len(places) :]
    if half == 0:
        x_ref, g_ref, beta_ref, cv_ref, bias_ref = refs[:5]
        n_ref, w_ref, pre_ref, qkv_ref, t_ref, wu_ref, pd_ref, b_ref, sem = refs[5:]
    else:
        n_ref, beta_ref, cv_ref, bias_ref = refs[:4]
        w_ref, pre_ref, qkv_ref, t_ref, wu_ref, pd_ref, b_ref, sem = refs[-8:]
    rows = qkv_ref.shape[1] // 2
    frame = rows + HALO
    copies = []
    columns_of = pl.ds(half * 768, 768)
    for part, to in block_moves(places, me_ref, parts, w_ref.shape[:3]):
        copies.append(
            pltpu.make_async_copy(
                part.at[:, columns_of], w_ref.at[to], sem.at[len(copies)]
            )
        )
        copies[-1].start()
    if half == 0:
        x = x_ref[...].astype(F32)
        scale = lax.rsqrt(jnp.mean(x * x, axis=-1, keepdims=True) + EPS)
        n_ref[...] = (x * scale * g_ref[...]).astype(BF16)
    normed = n_ref[...]
    for copy in copies:
        copy.wait()
    pre_ref[0] = dot1(normed, w_ref[...].reshape(D, 768)).astype(BF16)
    linear = dot1(normed, beta_ref[0])
    i, j = grid_masks(rows)
    keys, rights, lowers = [], [], []
    for q in range(2):
        rate = sigmoid(linear[q * frame + HALO : (q + 1) * frame] + bias_ref[0, q : q + 1, :])
        b_ref[0, q * rows : (q + 1) * rows, :] = rate
        ext = pre_ref[0, q * frame : (q + 1) * frame, :].astype(F32)
        conv = conv_of(ext, cv_ref[0], rows)
        act = conv * sigmoid(conv)
        for h in range(2):
            place = pl.ds(q * rows, rows)
            parts = []
            for kind in range(3):
                lane = (kind * 2 + h) * DK
                one = act[:, lane : lane + DK]
                if kind < 2:
                    one = one * lax.rsqrt(jnp.sum(one * one, axis=-1, keepdims=True) + EPS)
                if kind == 0:
                    one = one * DK ** (-0.5)
                one = one.astype(BF16)
                qkv_ref[0, place, lane : lane + DK] = one
                parts.append(one)
            key, value = parts[1], parts[2]
            col = rate[:, h : h + 1]
            keys.append(key)
            rights.append(jnp.concatenate([key, value], axis=1).astype(F32) * col)
            lowers.append(jnp.where(i > j, dot1(key, key, NT) * col, 0.0))
    inverses = unit_inverses(lowers, i, j)
    boths = [dot3(t, r) for t, r in zip(inverses, rights)]
    for p in range(4):
        t_ref[0, p] = inverses[p].astype(BF16)
        wu_ref[0, p] = boths[p].astype(BF16)
    for p in range(4):
        pd_ref[0, p] = dot1(keys[p], boths[p], TN).astype(BF16)


def state_kernel(pd_ref, s_ref):
    count = pd_ref.shape[0]
    state = jnp.zeros((DK, DK), F32)
    for s in range(count):
        s_ref[s] = state.astype(BF16)
        if s + 1 < count:
            high, low = split(state)
            move = pd_ref[s, :, :DK]
            state = state - (dot1(move, high) + dot1(move, low)) + pd_ref[s, :, DK:].astype(F32)


def adjoint_kernel(pd_ref, g_ref, l_ref):
    count = pd_ref.shape[0]
    adjoint = jnp.zeros((DK, DK), F32)
    for s in range(count - 1, -1, -1):
        l_ref[s] = adjoint.astype(BF16)
        if s > 0:
            high, low = split(adjoint)
            move = pd_ref[s, :, :DK]
            adjoint = (
                adjoint - (dot1(move, high, TN) + dot1(move, low, TN)) + g_ref[s].astype(F32)
            )


def pair_places(rows):
    return [
        (q * 2 + h, pl.ds(q * rows, rows), pl.ds(h * DK, DK), h) for q in range(2) for h in range(2)
    ]


def kind_lanes(kind, h):
    return pl.ds((kind * 2 + h) * DK, DK)


def second_kernel(qkv_ref, wu_ref, s_ref, hg_ref, f_ref, m_ref, h_ref):
    rows = qkv_ref.shape[1] // 2
    i, j = grid_masks(rows)
    pairs = pair_places(rows)
    queries = [qkv_ref[0, at, kind_lanes(0, h)] for _, at, _, h in pairs]
    keys = [qkv_ref[0, at, kind_lanes(1, h)] for _, at, _, h in pairs]
    scores = [jnp.where(i >= j, dot1(a, b, NT), 0.0).astype(BF16) for a, b in zip(queries, keys)]
    freshes = [
        (wu_ref[0, p, :, DK:].astype(F32) - dot1(wu_ref[0, p, :, :DK], s_ref[p])).astype(BF16)
        for p, _, _, _ in pairs
    ]
    mixes = [
        dot1(queries[p], s_ref[p]) + dot1(scores[p], freshes[p]) for p, _, _, _ in pairs
    ]
    for p, at, lanes, _ in pairs:
        mixed = mixes[p]
        scale = lax.rsqrt(jnp.mean(mixed * mixed, axis=-1, keepdims=True) + EPS)
        f_ref[at, lanes] = freshes[p]
        m_ref[at, lanes] = mixed
        h_ref[at, lanes] = (mixed * scale * hg_ref[...]).astype(BF16)


def third_kernel(qkv_ref, wu_ref, s_ref, f_ref, m_ref, dh_ref, hg_ref, sg_ref, gf_ref, gq_ref, gk_ref, ghg_ref):
    rows = qkv_ref.shape[1] // 2
    i, j = grid_masks(rows)
    gain = hg_ref[...]
    gain_grad = jnp.zeros((1, DK), F32)
    pairs = pair_places(rows)
    queries = [qkv_ref[0, at, kind_lanes(0, h)] for _, at, _, h in pairs]
    keys = [qkv_ref[0, at, kind_lanes(1, h)] for _, at, _, h in pairs]
    scores = [jnp.where(i >= j, dot1(a, b, NT), 0.0).astype(BF16) for a, b in zip(queries, keys)]
    grads = []
    for _, at, lanes, _ in pairs:
        mixed = m_ref[at, lanes]
        up = dh_ref[at, lanes].astype(F32)
        scale = lax.rsqrt(jnp.mean(mixed * mixed, axis=-1, keepdims=True) + EPS)
        unit = mixed * scale
        gain_grad = gain_grad + jnp.sum(up * unit, axis=0, keepdims=True)
        inner = up * gain
        grad = scale * (inner - unit * jnp.mean(inner * unit, axis=-1, keepdims=True))
        grads.append(grad.astype(BF16))
    ghg_ref[0] = jnp.broadcast_to(gain_grad, ghg_ref.shape[1:])
    fresh_grads = [dot1(a, g, TN) for a, g in zip(scores, grads)]
    starts = [
        dot1(queries[p], grads[p], TN) - dot1(wu_ref[0, p, :, :DK], fresh_grads[p], TN)
        for p in range(4)
    ]
    score_grads = [
        jnp.where(i >= j, dot1(grads[p], f_ref[at, lanes], NT), 0.0).astype(BF16)
        for p, at, lanes, _ in pairs
    ]
    for p, at, lanes, _ in pairs:
        gf_ref[at, lanes] = fresh_grads[p]
        sg_ref[0, p] = starts[p].astype(BF16)
        gq_ref[at, lanes] = dot1(grads[p], s_ref[p], NT) + dot1(score_grads[p], keys[p])
        gk_ref[at, lanes] = dot1(score_grads[p], queries[p], TN)


def fourth_kernel(qkv_ref, pre_ref, cv_ref, b_ref, t_ref, wu_ref, s_ref, l_ref, f_ref, gf_ref, gq_ref, gk_ref, eg_ref, gc_ref, lg_ref, gb_ref):
    rows = qkv_ref.shape[1] // 2
    frame = rows + HALO
    i, j = grid_masks(rows)
    lane = lax.broadcasted_iota(jnp.int32, (rows, DK), 1)
    pairs = pair_places(rows)
    keys = [qkv_ref[0, at, kind_lanes(1, h)] for _, at, _, h in pairs]
    values = [qkv_ref[0, at, kind_lanes(2, h)] for _, at, _, h in pairs]
    cols = [b_ref[0, at, h : h + 1] for _, at, _, h in pairs]
    fresh_grads = [
        gf_ref[at, lanes] + dot1(keys[p], l_ref[p]) for p, at, lanes, _ in pairs
    ]
    lows = [g.astype(BF16) for g in fresh_grads]
    factor_grads = [
        jnp.concatenate([-dot1(lows[p], s_ref[p], NT).astype(BF16), lows[p]], axis=1)
        for p in range(4)
    ]
    solved = [dot1(t_ref[0, p], factor_grads[p], TN) for p in range(4)]
    inners = [dot1(k, k, NT) for k in keys]
    system_grads = [
        jnp.where(i > j, -dot1(solved[p], wu_ref[0, p], NT), 0.0) for p in range(4)
    ]
    inner_grads = [(g * c).astype(BF16) for g, c in zip(system_grads, cols)]
    key_grads = [
        gk_ref[at, lanes]
        + dot1(f_ref[at, lanes], l_ref[p], NT)
        + cols[p] * solved[p][:, :DK]
        + dot1(inner_grads[p], keys[p])
        + dot1(inner_grads[p], keys[p], TN)
        for p, at, lanes, _ in pairs
    ]
    rate_grads = [
        (
            jnp.sum(
                solved[p][:, :DK] * keys[p].astype(F32) + solved[p][:, DK:] * values[p].astype(F32),
                axis=-1,
                keepdims=True,
            )
            + jnp.sum(system_grads[p] * inners[p], axis=-1, keepdims=True)
        )
        * cols[p]
        * (1.0 - cols[p])
        for p in range(4)
    ]
    for q in range(2):
        place = pl.ds(q * rows, rows)
        logit = jnp.where(
            lane == 0, rate_grads[2 * q], jnp.where(lane == 1, rate_grads[2 * q + 1], 0.0)
        )
        lg_ref[0, place, :] = logit.astype(BF16)
        gb_ref[0, q : q + 1, :] = jnp.sum(logit, axis=0, keepdims=True)
    zero = jnp.zeros((HALO, DK), F32)
    for kind in range(3):
        for h in range(2):
            at = kind_lanes(kind, h)
            tap = cv_ref[0, :, at]
            conv_grad = [jnp.zeros((1, DK), F32) for _ in range(CONV)]
            for q in range(2):
                p = q * 2 + h
                ext = pre_ref[0, q * frame : (q + 1) * frame, at].astype(F32)
                views = [ext[HALO - 3 + t : HALO - 3 + t + rows] for t in range(CONV)]
                conv = tap[0:1, :] * views[0]
                for t in range(1, CONV):
                    conv = conv + tap[t : t + 1, :] * views[t]
                sig = sigmoid(conv)
                act = conv * sig
                if kind == 0:
                    grad = gq_ref[q * rows : (q + 1) * rows, h * DK : (h + 1) * DK] * DK ** (-0.5)
                elif kind == 1:
                    grad = key_grads[p]
                else:
                    grad = cols[p] * solved[p][:, DK:]
                if kind < 2:
                    scale = lax.rsqrt(jnp.sum(act * act, axis=-1, keepdims=True) + EPS)
                    unit = act * scale
                    grad = scale * (grad - unit * jnp.sum(grad * unit, axis=-1, keepdims=True))
                grad = grad * (sig * (1.0 + conv * (1.0 - sig)))
                wide = jnp.concatenate([zero, grad, zero], axis=0)
                total = tap[0:1, :] * wide[3 : 3 + frame]
                for t in range(1, CONV):
                    total = total + tap[t : t + 1, :] * wide[3 - t : 3 - t + frame]
                eg_ref[q * frame : (q + 1) * frame, at] = total.astype(BF16)
                for t in range(CONV):
                    conv_grad[t] = conv_grad[t] + jnp.sum(grad * views[t], axis=0, keepdims=True)
            for t in range(CONV):
                gc_ref[0, t : t + 1, at] = conv_grad[t]


def lead(*shape):
    return pl.BlockSpec((1,) + shape, lambda p: (p,) + (0,) * len(shape))


def at_half(half, *shape):
    return pl.BlockSpec((1,) + shape, lambda p: (half,) + (0,) * len(shape))


def whole(*shape):
    return pl.BlockSpec(shape, lambda p: (0,) * len(shape))


def columns(rows, cols):
    return pl.BlockSpec((rows, cols), lambda p: (0, p))


def quarter():
    return pl.BlockSpec((4, DK, DK), lambda p: (p, 0, 0))


def cost(microseconds):
    return pl.CostEstimate(
        flops=int(microseconds * 1.15e9), bytes_accessed=0, transcendentals=0
    )


def on_core(kernel, outs, in_specs, out_specs, name, microseconds):
    return pl.pallas_call(
        kernel,
        out_shape=outs,
        grid=(2,),
        in_specs=in_specs,
        out_specs=out_specs,
        compiler_params=pltpu.CompilerParams(
            vmem_limit_bytes=VMEM_LIMIT, dimension_semantics=("arbitrary",)
        ),
        cost_estimate=cost(microseconds),
        name=name,
    )


def sds(shape, kind):
    return jax.ShapeDtypeStruct(shape, kind)


def all_ranges(a):
    if lax.axis_size("z") * lax.axis_size("y") == a.shape[0]:
        return lax.all_to_all(a, SEQ, 0, 0, tiled=True)
    return lax.all_gather(a, SEQ)


def scan_states(every):
    count = lax.axis_size("z") * lax.axis_size("y")
    if every.ndim == 3:
        return pl.pallas_call(
            state_kernel,
            out_shape=sds((count, DK, DK), BF16),
            cost_estimate=cost(3),
            name="state_scan",
        )(every)

    def step(s, state):
        one = lax.dynamic_index_in_dim(every, s, 0, False).astype(F32)
        moved = jnp.einsum(
            "pij,pjk->pik", one[:, :, :DK], state, precision=lax.Precision.HIGHEST
        )
        return state - moved + one[:, :, DK:]

    start = jnp.zeros((every.shape[1], DK, DK), F32)
    return lax.fori_loop(0, lax.axis_index(SEQ), step, start).astype(BF16)


def scan_adjoints(every, grads):
    count = lax.axis_size("z") * lax.axis_size("y")
    if every.ndim == 3:
        return pl.pallas_call(
            adjoint_kernel,
            out_shape=sds((count, DK, DK), BF16),
            cost_estimate=cost(3),
            name="adjoint_scan",
        )(every, grads)

    def step(k, adjoint):
        s = count - 1 - k
        one = lax.dynamic_index_in_dim(every, s, 0, False).astype(F32)
        moved = jnp.einsum(
            "pji,pjk->pik", one[:, :, :DK], adjoint, precision=lax.Precision.HIGHEST
        )
        return adjoint - moved + lax.dynamic_index_in_dim(grads, s, 0, False).astype(F32)

    start = jnp.zeros((every.shape[1], DK, DK), F32)
    steps = count - 1 - lax.axis_index(SEQ)
    return lax.fori_loop(0, steps, step, start).astype(BF16)


def own_range(a):
    if lax.axis_size("z") * lax.axis_size("y") == H:
        return lax.all_to_all(a, SEQ, 0, 0, tiled=True)
    return a


def shards(
    inputs,
    domain_ids,
    norm1_gain,
    w_qkv,
    w_beta,
    conv_weight,
    domain_bias,
    head_gain,
    w_out,
    norm2_gain,
    w_gate_up,
    w_down,
    cotangent,
):
    core = lax.axis_index("core")
    nz, ny, nx = (lax.axis_size(a) for a in ("z", "y", "x"))
    z, y, x = (lax.axis_index(a) for a in ("z", "y", "x"))
    chips = nz * ny * nx
    seq_devices = nz * ny
    rows = inputs.shape[1]
    frame = rows + HALO
    tall = 2 * rows
    drows = w_qkv.shape[0]
    both_rows = 2 * drows
    frows = w_down.shape[0]
    grows = conv_weight.shape[0]
    first = core == 0
    half = H // 2
    fence = lax.optimization_barrier

    q_mine, q_other = core_pick(
        w_qkv.reshape(drows, 3, 2, 2, 256).transpose(2, 0, 3, 1, 4).reshape(2, drows, 1536), core
    )
    q_got = swap(q_other)
    small = jnp.concatenate(
        [norm1_gain, norm2_gain, w_beta.reshape(-1), conv_weight.reshape(-1)]
    )
    n_small = small.shape[0]
    small = jnp.pad(small, (0, 768 - n_small)).reshape(1, 768)
    small_got = swap(small)
    x_own = inputs.reshape(rows, D)
    small = jnp.concatenate(
        [jnp.where(first, small, small_got), jnp.where(first, small_got, small)], axis=1
    )
    small = jnp.pad(small, ((0, 7), (0, 0)))
    q_part = jnp.concatenate([chip_rows(q_mine, q_got, core), small], axis=0)
    q_part, x_own, w_gate_up, w_out, w_down, cotangent = fence(
        (q_part, x_own, w_gate_up, w_out, w_down, cotangent)
    )

    q_far = [q_part] + [turned(q_part, "z", k) for k in sorted({1, nz - 1})]
    q_far = relayed(q_far, "z")
    out_cols = w_out.reshape(drows, 2, 2, 256).transpose(1, 2, 0, 3)
    gu_cols = (
        w_gate_up.reshape(drows, 2, chips, 2, frows)
        .transpose(3, 1, 0, 2, 4)
        .reshape(2, 2, drows, FF // 2)
    )
    wide_cols = jnp.concatenate(
        [gu_cols[:, 0], gu_cols[:, 1], out_cols[:, 0], out_cols[:, 1]], axis=-1
    )
    wide_mine, wide_other = core_pick(wide_cols, core)
    wide_part = chip_rows(wide_mine, swap(wide_other), core)
    q_far, x_own, cotangent, wide_part, w_down = fence(
        (q_far, x_own, cotangent, wide_part, w_down)
    )
    halo = lax.ppermute(
        x_own[rows - HALO :], SEQ, [(i, i + 1) for i in range(seq_devices - 1)]
    )
    choose = (domain_ids[0] == jnp.arange(NDOM, dtype=jnp.int32)).astype(BF16)
    bias_own = jnp.sum(domain_bias.astype(F32) * choose.astype(F32)[:, None], axis=0)
    extra = jnp.pad(jnp.concatenate([bias_own.astype(BF16), choose]), (0, D - H - NDOM))
    extra = jnp.pad(extra.reshape(1, D), ((0, HALO - 1), (0, 0)))
    frame_own = jnp.concatenate([halo, x_own, extra], axis=0)
    frame_other = swap(frame_own)
    g_own = cotangent.reshape(rows, D)
    g_other = swap(g_own)

    q_parts = cross_fetched(jnp.stack([a[:both_rows] for a in q_far]), True)
    smalls = jnp.stack(in_place([a[both_rows].reshape(2, 768) for a in q_far], z))
    smalls = plane_fetched(smalls)
    ends = sorted({1, nz - 1})
    wide_near = [wide_part, turned(wide_part, "z", 1)]
    q_parts, w_down, smalls = fence((q_parts, w_down, smalls))
    smalls = plane_stack(smalls).transpose(2, 0, 1, 3, 4).reshape(2 * chips, 768)[:, :n_small]
    gain_one = smalls[:, :drows].reshape(1, D).astype(F32)
    gain_two = smalls[:, drows : 2 * drows].reshape(1, D).astype(F32)
    full_beta = smalls[:, 2 * drows : 2 * drows + drows * H].reshape(D, 2, half)
    full_conv = smalls[:, 2 * drows + drows * H :].reshape(3, 2, 2, 256, CONV)
    beta_mine = lax.dynamic_index_in_dim(full_beta, core, 1, False)
    conv_mine = (
        lax.dynamic_index_in_dim(full_conv, core, 1, False)
        .transpose(1, 3, 0, 2)
        .reshape(2, CONV, 768)
        .astype(F32)
    )
    beta_pairs = jnp.pad(
        beta_mine.reshape(D, 2, 2).transpose(1, 0, 2), ((0, 0), (0, 0), (0, DK - 2))
    )

    q_parts = cross_fetched(cross_stack(q_parts), False)
    wide_near, frame_own, frame_other = fence((wide_near, frame_own, frame_other))
    wide_rest = [turned(wide_near[0], "z", k) for k in ends[1:]]
    x_frames = jnp.concatenate([frame_own[:frame], frame_other[:frame]], axis=0)
    bias_both = jnp.stack([frame_own[frame, :H], frame_other[frame, :H]]).astype(F32)
    choose_both = jnp.stack(
        [frame_own[frame, H : H + NDOM], frame_other[frame, H : H + NDOM]]
    ).astype(F32)
    bias_mine = lax.dynamic_index_in_dim(bias_both.reshape(2, 2, half), core, 1, False)
    bias_pairs = jnp.pad(
        bias_mine.reshape(2, 2, 2).transpose(1, 0, 2), ((0, 0), (0, 0), (0, DK - 2))
    )
    x_both = jnp.concatenate(
        [frame_own[HALO:frame], frame_other[HALO:frame]], axis=0
    ).astype(F32)
    g_both = jnp.concatenate([g_own, g_other], axis=0)
    (
        q_parts,
        wide_near,
        wide_rest,
        w_down,
        gain_one,
        gain_two,
        beta_pairs,
        conv_mine,
        bias_pairs,
        x_frames,
        x_both,
        g_both,
    ) = fence(
        (
            q_parts,
            wide_near,
            wide_rest,
            w_down,
            gain_one,
            gain_two,
            beta_pairs,
            conv_mine,
            bias_pairs,
            x_frames,
            x_both,
            g_both,
        )
    )

    q_places = spots((q_parts,))
    blocks = chips
    if both_rows % 16 == 0:
        w_shape = sds((nz, ny, nx, both_rows, 768), BF16)
    else:
        w_shape = sds((1, 1, 1, D, 768), BF16)
        q_parts, q_places, blocks = [assembled((q_parts,)).reshape(1, 1, D, 1536)], [(0, 0, 0)], 1
    place = jnp.stack([core, y, x, z]).astype(jnp.int32)
    kept = (
        sds((2, 2 * frame, 768), BF16),
        sds((2, tall, 768), BF16),
        sds((2, 4, rows, rows), BF16),
        sds((2, 4, rows, 2 * DK), BF16),
        sds((2, 4, DK, 2 * DK), BF16),
        sds((2, tall, DK), F32),
    )
    anywhere = pl.BlockSpec(memory_space=pl.ANY)

    def local(number, parts, ins, in_specs, outs, out_specs, held):
        fixed = [at_half(number, D, DK), at_half(number, CONV, 768), at_half(number, 2, DK)]
        first_held = 1 + len(parts) + len(ins) + 3
        return pl.pallas_call(
            functools.partial(first_kernel, number, q_places),
            out_shape=outs + (w_shape,) + kept,
            grid=(1,),
            in_specs=[pl.BlockSpec(memory_space=pltpu.SMEM)]
            + [anywhere] * len(parts)
            + in_specs
            + fixed
            + [anywhere] * len(held),
            out_specs=out_specs
            + (whole(*w_shape.shape),)
            + tuple(at_half(number, *k.shape[1:]) for k in kept),
            scratch_shapes=[pltpu.SemaphoreType.DMA((blocks,))],
            input_output_aliases={
                first_held + k: len(outs) + 1 + k for k in range(len(held))
            },
            compiler_params=pltpu.CompilerParams(vmem_limit_bytes=VMEM_LIMIT),
            cost_estimate=cost(10),
            name="delta_local",
        )(place, *parts, *ins, beta_pairs, conv_mine, bias_pairs, *held)

    wide_rest = relayed(wide_near + wide_rest, "z")[2:]
    wide_u = cross_fetched(jnp.stack(wide_near), True)
    normed, w_q_one, *held = local(
        0,
        q_parts,
        (x_frames, gain_one),
        [whole(2 * frame, D), whole(1, D)],
        (sds((2 * frame, D), BF16),),
        (whole(2 * frame, D),),
        (),
    )
    normed, w_q_one, held, wide_rest, wide_u, q_parts, w_down = fence(
        (normed, w_q_one, held, wide_rest, wide_u, q_parts, w_down)
    )

    wide_rest, wide_two = jnp.stack(wide_rest), cross_stack(wide_u)
    wide_v = cross_fetched(wide_rest, True)
    wide_u = cross_fetched(wide_two, False)
    down_z = fetched(w_down, "z")
    w_q_two, *held = local(
        1,
        q_parts,
        (after(normed, wide_rest, wide_two),),
        [whole(2 * frame, D)],
        (),
        (),
        tuple(held),
    )
    pre, qkv, inverse, factors, pd, rates = held
    w_q_one = w_q_one.reshape(D, 768)
    w_q_two = w_q_two.reshape(D, 768)
    (
        normed,
        w_q_one,
        w_q_two,
        pre,
        qkv,
        inverse,
        factors,
        pd,
        rates,
        down_z,
        wide_v,
    ) = fence(
        (
            normed,
            w_q_one,
            w_q_two,
            pre,
            qkv,
            inverse,
            factors,
            pd,
            rates,
            down_z,
            wide_v,
        )
    )

    every = all_ranges(pd.reshape(H, DK, 2 * DK))
    down_stack = jnp.stack(in_place(down_z, z))
    wide_v = cross_fetched(cross_stack(wide_v), False)
    every, wide_u, down_stack = fence((every, wide_u, down_stack))

    states = scan_states(every)
    def placed(parts, places, held):
        return pl.pallas_call(
            functools.partial(place_kernel, places, cuts, (nz, ny, nx)),
            out_shape=[sds((nz, ny, nx, both_rows, hi - lo), BF16) for lo, hi in cuts],
            in_specs=[pl.BlockSpec(memory_space=pltpu.SMEM)]
            + [pl.BlockSpec(memory_space=pltpu.VMEM)] * len(parts)
            + [anywhere] * len(held),
            out_specs=[anywhere] * len(cuts),
            input_output_aliases={1 + len(parts) + k: k for k in range(len(held))},
            scratch_shapes=[
                pltpu.SemaphoreType.DMA(
                    (sum(p.shape[0] * p.shape[1] for p in parts) * len(cuts),)
                )
            ],
            compiler_params=pltpu.CompilerParams(vmem_limit_bytes=VMEM_LIMIT),
            cost_estimate=cost(3),
            name="placed",
        )(place, *parts, *held)

    cuts = ((FF, FF + D // 2), (0, FF // 2), (FF // 2, FF))
    wide_places = spots((wide_u, wide_v))
    wide = ()
    if both_rows % 16 == 0:
        wide = tuple(placed(after(wide_u, states), wide_places[: len(wide_u)], ()))
    states = after(own_range(states), wide)
    down_parts = cross_fetched(after(down_stack, wide), True)
    gain_head = head_gain.astype(F32).reshape(1, DK)
    fresh, mixed, heads_mine = on_core(
        second_kernel,
        (sds((tall, 512), BF16), sds((tall, 512), F32), sds((tall, 512), BF16)),
        [lead(tall, 768), lead(4, rows, 2 * DK), quarter(), whole(1, DK)],
        (columns(tall, 256), columns(tall, 256), columns(tall, 256)),
        "delta_mix",
        2,
    )(qkv, factors, states, gain_head)
    heads_got = swap(heads_mine)
    wide, wide_v, states, fresh, mixed, heads_mine, heads_got = fence(
        (wide, wide_v, states, fresh, mixed, heads_mine, heads_got)
    )

    down_parts = cross_fetched(cross_stack(down_parts), False)
    if both_rows % 16 == 0:
        out_mine, w_gate, w_up = placed(wide_v, wide_places[len(wide_u) :], wide)
    else:
        wide = assembled((wide_u, wide_v))
        out_mine, w_gate, w_up = (wide[..., lo:hi] for lo, hi in cuts)
    out_mine, w_gate, w_up = (a.reshape(D, -1) for a in (out_mine, w_gate, w_up))
    out_got = swap(out_mine)
    full_out = jnp.concatenate(
        [jnp.where(first, out_mine, out_got), jnp.where(first, out_got, out_mine)], axis=1
    )
    heads_got = jnp.concatenate([heads_got[rows:], heads_got[:rows]], axis=0)
    heads = jnp.concatenate(
        [jnp.where(first, heads_mine, heads_got), jnp.where(first, heads_got, heads_mine)], axis=1
    )
    middle = x_both + jnp.dot(heads, full_out, preferred_element_type=F32)
    scale_two = lax.rsqrt(jnp.mean(middle * middle, axis=-1, keepdims=True) + EPS)
    unit_two = middle * scale_two
    normed_two = (unit_two * gain_two).astype(BF16)
    gate = jnp.dot(normed_two, w_gate, preferred_element_type=F32)
    up = jnp.dot(normed_two, w_up, preferred_element_type=F32)
    sig = jax.nn.sigmoid(gate)
    hidden = (gate * sig * up).astype(BF16)
    grad_down = jnp.einsum("nf,nd->fd", hidden, g_both, preferred_element_type=F32).astype(BF16)
    down_shares = late_shares(grid_of(grad_down))
    down_stage = cross_sent(down_shares, False)
    w_down_mine = cross_end(after(down_parts, down_shares)).reshape(chips * frows, D)
    hidden_grad = jnp.einsum("nd,fd->nf", g_both, w_down_mine, preferred_element_type=F32)
    up_grad = (hidden_grad * gate * sig).astype(BF16)
    gate_grad = (hidden_grad * up * sig * (1.0 + gate * (1.0 - sig))).astype(BF16)
    up_grad, gate_grad = fence((up_grad, gate_grad))

    grad_gate = jnp.einsum("nd,nf->df", normed_two, gate_grad, preferred_element_type=F32)
    gate_shares = late_shares(grid_of(grad_gate.astype(BF16)))
    gate_stage = cross_sent(gate_shares, False)
    normed_two_part = jnp.einsum(
        "nf,df->nd", after(gate_grad, gate_shares), w_gate, preferred_element_type=F32
    ) + jnp.einsum("nf,df->nd", up_grad, w_up, preferred_element_type=F32)
    part_low = normed_two_part.astype(BF16)
    part_got, down_stage = fence((swap(part_low), down_stage))
    grad_up = jnp.einsum(
        "nd,nf->df", after(normed_two, part_low), up_grad, preferred_element_type=F32
    ).astype(BF16)
    up_shares = late_shares(grid_of(grad_up))
    up_stage = cross_sent(up_shares, False)
    part_got = after(part_got, up_shares)
    part_got = jnp.concatenate([part_got[rows:], part_got[:rows]], axis=0)
    normed_two_grad = normed_two_part + part_got.astype(F32)
    grad_norm2 = jnp.sum(normed_two_grad[:rows] * unit_two[:rows], axis=0)
    inner = normed_two_grad * gain_two
    middle_grad = g_both.astype(F32) + scale_two * (
        inner - unit_two * jnp.mean(inner * unit_two, axis=-1, keepdims=True)
    )
    middle_low = middle_grad.astype(BF16)
    out_rows = lax.dynamic_slice_in_dim(full_out, core * 512, 512, 0)
    heads_grad = jnp.einsum("ne,de->nd", middle_low, out_rows, preferred_element_type=F32)
    start_grad, fresh_grad, query_grad, key_grad, gain_part = on_core(
        third_kernel,
        (
            sds((2, 4, DK, DK), BF16),
            sds((tall, 512), F32),
            sds((tall, 512), F32),
            sds((tall, 512), F32),
            sds((2, 8, DK), F32),
        ),
        [
            lead(tall, 768),
            lead(4, rows, 2 * DK),
            quarter(),
            columns(tall, 256),
            columns(tall, 256),
            columns(tall, 256),
            whole(1, DK),
        ],
        (
            lead(4, DK, DK),
            columns(tall, 256),
            columns(tall, 256),
            columns(tall, 256),
            lead(8, DK),
        ),
        "delta_back_local",
        5,
    )(qkv, factors, states, fresh, mixed, heads_grad, gain_head)
    (
        start_grad,
        fresh_grad,
        query_grad,
        key_grad,
        gain_part,
        middle_low,
        hidden,
    ) = fence(
        (
            start_grad,
            fresh_grad,
            query_grad,
            key_grad,
            gain_part,
            middle_low,
            hidden,
        )
    )

    start_grads = all_ranges(start_grad.reshape(H, DK, DK))
    low_cols = lax.dynamic_slice_in_dim(middle_low, core * 512, 512, 1)
    grad_out = jnp.einsum("nd,ne->de", heads, low_cols, preferred_element_type=F32)
    out_shares = late_shares(grid_of(grad_out.astype(BF16)))
    out_stage = cross_sent(out_shares, False)
    adjoints = scan_adjoints(every, after(start_grads, out_shares))
    down_shares = early_shares(after(down_stage, adjoints))
    down_stage = cross_sent(down_shares, True)
    gate_shares = early_shares(after(gate_stage, down_shares))
    gate_stage = cross_sent(gate_shares, True)
    up_shares = [
        jnp.concatenate(cut, axis=-1)
        for cut in zip(*(early_shares(stage) for stage in after((up_stage, out_stage), adjoints)))
    ]
    up_stage = cross_sent(up_shares, True)
    down_part = jnp.dot(after(hidden, adjoints), w_down_mine, preferred_element_type=F32)
    output = (middle[:rows] + down_part[:rows]) + swap(down_part[rows:].astype(BF16)).astype(F32)
    output = output.astype(BF16).reshape(1, rows, D)
    adjoints = own_range(adjoints)
    down_shares = shares(added(*after(down_stage, gate_shares)).astype(BF16), "z", 0)
    down_stage = sent(down_shares, "z")
    adjoints = after(adjoints, up_shares, down_shares, output)
    ext_grad, conv_part, logit_low, bias_part = on_core(
        fourth_kernel,
        (
            sds((2 * frame, 1536), BF16),
            sds((2, CONV, 768), F32),
            sds((2, tall, DK), BF16),
            sds((2, 2, DK), F32),
        ),
        [
            lead(tall, 768),
            lead(2 * frame, 768),
            lead(CONV, 768),
            lead(tall, DK),
            lead(4, rows, rows),
            lead(4, rows, 2 * DK),
            quarter(),
            quarter(),
            columns(tall, 256),
            columns(tall, 256),
            columns(tall, 256),
            columns(tall, 256),
        ],
        (columns(2 * frame, 768), lead(CONV, 768), lead(tall, DK), lead(2, DK)),
        "delta_back",
        15,
    )(qkv, pre, conv_mine, rates, inverse, factors, states, adjoints, fresh, fresh_grad, query_grad, key_grad)
    ext_grad, conv_part, logit_low, bias_part, gate_stage, up_stage, down_stage = fence(
        (ext_grad, conv_part, logit_low, bias_part, gate_stage, up_stage, down_stage)
    )

    ext_frames = ext_grad.reshape(2, frame, 1536)
    grad_q = jnp.einsum("nd,nf->df", normed, ext_grad, preferred_element_type=F32).astype(BF16)
    q_shares = late_shares(grid_of(grad_q))
    ext_frames, gate_stage, up_stage, q_shares = fence(
        (ext_frames, gate_stage, up_stage, q_shares)
    )
    q_stage = cross_sent(q_shares, False)
    sent_back = lax.ppermute(
        ext_frames[:, :HALO], SEQ, [(i + 1, i) for i in range(seq_devices - 1)]
    )
    wide_part = jnp.concatenate([added(*gate_stage), added(*up_stage)], axis=-1).astype(BF16)
    wide_own, ahead, behind = relays(shares(wide_part, "z", 0), "z")
    behind = turned(behind, "z", nz - 1)
    tail = ext_frames[:, frame - HALO :].astype(F32) + sent_back.astype(F32)
    pre_low = jnp.concatenate(
        [ext_frames[:, HALO : frame - HALO], tail.astype(BF16)], axis=1
    ).reshape(tall, 1536)
    normed_part = (
        jnp.einsum("nf,df->nd", pre_low[:, :768], w_q_one, preferred_element_type=F32)
        + jnp.einsum("nf,df->nd", pre_low[:, 768:], w_q_two, preferred_element_type=F32)
        + jnp.einsum("pnh,pdh->nd", logit_low, beta_pairs, preferred_element_type=F32)
    )
    part_low, ahead, behind = fence((normed_part[rows:].astype(BF16), ahead, behind))
    wide_stage = (wide_own, [turned(ahead, "z", 1), behind])
    normed_grad = normed_part[:rows] + swap(part_low).astype(F32)
    q_stage, normed_grad, normed, conv_part, logit_low, x_both = fence(
        (q_stage, normed_grad, normed, conv_part, logit_low, x_both)
    )

    q_shares, normed_grad, x_both = fence((early_shares(q_stage), normed_grad, x_both))
    q_stage = cross_sent(q_shares, True)
    x32 = x_both[:rows]
    scale_one = lax.rsqrt(jnp.mean(x32 * x32, axis=-1, keepdims=True) + EPS)
    unit_one = x32 * scale_one
    grad_norm1 = jnp.sum(normed_grad * unit_one, axis=0)
    inner_one = normed_grad * gain_one
    grad_input = middle_grad[:rows] + scale_one * (
        inner_one - unit_one * jnp.mean(inner_one * unit_one, axis=-1, keepdims=True)
    )
    grad_input = grad_input.reshape(1, rows, D)
    normed_tokens = normed.reshape(2, frame, D)[:, HALO:].reshape(tall, D)
    grad_beta = jnp.einsum(
        "nd,pnh->dph", normed_tokens, logit_low[:, :, :2], preferred_element_type=F32
    ).reshape(D, half)
    beta_full = jnp.where(
        first,
        jnp.pad(grad_beta, ((0, 0), (0, half))),
        jnp.pad(grad_beta, ((0, 0), (half, 0))),
    )
    conv_cols = conv_part.reshape(2, CONV, 3, 256).transpose(2, 0, 3, 1).reshape(3, 512, CONV)
    conv_full = jnp.where(
        first,
        jnp.pad(conv_cols, ((0, 0), (0, 512), (0, 0))),
        jnp.pad(conv_cols, ((0, 0), (512, 0), (0, 0))),
    )
    bias_heads = bias_part[:, :, :2].transpose(1, 0, 2).reshape(2, half)
    bias_heads = jnp.where(
        first,
        jnp.pad(bias_heads, ((0, 0), (0, half))),
        jnp.pad(bias_heads, ((0, 0), (half, 0))),
    )
    bias_grad = jnp.sum(choose_both[:, :, None] * bias_heads[:, None, :], axis=0)
    shared = jnp.concatenate([bias_grad.reshape(-1), gain_part[0, 0] + gain_part[1, 0]])
    shared = jnp.broadcast_to(shared, (2 * chips, shared.shape[0]))
    pack = jnp.concatenate(
        [
            grad_norm2.reshape(2 * chips, drows),
            beta_full.reshape(2 * chips, drows * H),
            conv_full.reshape(2 * chips, grows * CONV),
            shared,
        ],
        axis=1,
    )
    pack = jnp.pad(pack, ((0, 0), (0, -pack.shape[1] % DK)))
    norm_rows = jnp.pad(grad_norm1.reshape(2 * chips, drows), ((0, 0), (0, DK - drows)))
    pack = jnp.concatenate([norm_rows, pack], axis=1).reshape(chips, 2, -1)
    pack_own = lax.dynamic_index_in_dim(pack, core, 1, False)
    pack_got = swap(lax.dynamic_index_in_dim(pack, 1 - core, 1, False))
    pack = plane_shares((pack_own + pack_got).reshape(nz, ny, nx, -1))
    q_stage, pack = fence((q_stage, pack))

    q_shares = fence(shares(added(*q_stage).astype(BF16), "z", 0))
    q_own, ahead, behind = relays(q_shares, "z")
    behind = turned(behind, "z", nz - 1)
    pack = plane_sum(pack)
    own_down = added(*after(down_stage, q_shares))
    wide_own = own_rows(added(*after(wide_stage, q_shares)), core)
    ahead, behind, pack, own_down, wide_own = fence((ahead, behind, pack, own_down, wide_own))
    q_stage = (q_own, [turned(ahead, "z", 1), behind])
    own_gu = (
        wide_own[..., :FF]
        .reshape(2, drows, 2, chips, frows)
        .transpose(1, 2, 3, 0, 4)
        .reshape(drows, 2 * FF)
    )
    own_out = wide_own[..., FF:].transpose(1, 0, 2).reshape(drows, D)
    mine = z_sum(pack)
    q_stage, mine, own_gu, own_down, own_out = fence((q_stage, mine, own_gu, own_down, own_out))

    q_own = own_rows(added(*q_stage), core)
    own_qkv = jnp.concatenate(
        [
            q_own[c, :, (hp * 3 + kind) * 256 : (hp * 3 + kind + 1) * 256]
            for kind in range(3)
            for c in range(2)
            for hp in range(2)
        ],
        axis=1,
    )
    own_g1 = mine[:drows]
    at = DK
    own_g2 = mine[at : at + drows]
    at += drows
    own_beta = mine[at : at + drows * H].reshape(drows, H)
    at += drows * H
    own_conv = mine[at : at + grows * CONV].reshape(grows, CONV)
    at += grows * CONV
    bias_total = mine[at : at + NDOM * H].reshape(NDOM, H)
    at += NDOM * H
    gain_total = mine[at : at + DK]
    return (
        output,
        grad_input,
        own_g1,
        own_qkv,
        own_beta,
        own_conv,
        bias_total,
        gain_total,
        own_out,
        own_g2,
        own_gu,
        own_down,
    )


def solution(mesh):
    seq, batch = mesh.shape["seq"], mesh.shape["batch"]
    plane = batch // 2
    fine = Mesh(mesh.devices.reshape(seq // plane, plane, plane, 2), ALL)
    tokens = P(("x", "core"), ("z", "y"), None)
    rows = P(ALL, None)
    vector = P(ALL)
    return jax.shard_map(
        shards,
        mesh=fine,
        in_specs=(
            tokens,
            P(("x", "core")),
            vector,
            rows,
            rows,
            rows,
            P(),
            P(),
            rows,
            vector,
            rows,
            rows,
            tokens,
        ),
        out_specs=(
            tokens,
            tokens,
            vector,
            rows,
            rows,
            rows,
            P(),
            P(),
            rows,
            vector,
            rows,
            rows,
        ),
        check_vma=False,
    )
```

```python
import functools

import jax
import jax.numpy as jnp
from jax import lax
from jax.experimental import pallas as pl
from jax.experimental.pallas import tpu as pltpu
from jax.sharding import Mesh
from jax.sharding import PartitionSpec as P

D = 1024
H = 8
DK = 128
FF = 2816
CONV = 4
NDOM = 4
EPS = 1e-06
HALO = 16
F32 = jnp.float32
BF16 = jnp.bfloat16
SEQ = ("z", "y")
ALL = ("z", "y", "x", "core")
VMEM_LIMIT = 60 * 1024 * 1024


def swap(a):
    return lax.ppermute(a, "core", [(0, 1), (1, 0)])


def turned(a, axis, by):
    n = lax.axis_size(axis)
    return lax.ppermute(a, axis, [(i, (i + by) % n) for i in range(n)])


def after(a, *others):
    return lax.optimization_barrier((a, others))[0]


def in_place(parts, me):
    n = len(parts)
    if n == 2:
        first = me == 0
        return [jnp.where(first, *parts), jnp.where(first, *parts[::-1])]
    if n <= 4:
        return [lax.select_n((me - i) % n, *parts) for i in range(n)]
    back = parts[:0:-1] + parts[:1]
    wide = jnp.stack(back + back)
    return list(lax.dynamic_slice_in_dim(wide, n - 1 - me, n, axis=0))


def fetched(a, axis):
    return [a] + [turned(a, axis, k) for k in range(1, lax.axis_size(axis))]


def relayed(near, axis):
    n = lax.axis_size(axis)
    if n < 4:
        return near
    before, behind = [near[1]], [near[-1]]
    while len(before) < n // 2:
        before.append(turned(before[-1], axis, 1))
    while len(before) + len(behind) < n - 1:
        behind.append(turned(behind[-1], axis, n - 1))
    return near[:1] + before + behind[::-1]


def gather_axis(a, axis, dim):
    if lax.axis_size(axis) == 1:
        return jnp.expand_dims(a, dim)
    return jnp.stack(in_place(fetched(a, axis), lax.axis_index(axis)), axis=dim)


def shares(a, axis, dim):
    n, me = lax.axis_size(axis), lax.axis_index(axis)
    return [lax.dynamic_index_in_dim(a, (me + k) % n, dim, False) for k in range(n)]


def sent(parts, axis):
    return parts[0], [turned(a, axis, k) for k, a in enumerate(parts) if k]


def sends(a, axis, dim):
    return sent(shares(a, axis, dim), axis)


def added(own, got):
    total = own.astype(F32)
    for part in got:
        total = total + part.astype(F32)
    return total


def relays(parts, axis):
    n = lax.axis_size(axis)
    sums = []
    for chain, by in ((parts[n // 2 : 0 : -1], 1), (parts[n // 2 + 1 :], n - 1)):
        total = chain[0]
        for part in chain[1:]:
            total = added(part, [turned(total, axis, by)]).astype(BF16)
        sums.append(total)
    return parts[0], *sums


def crossed(a, early, by):
    n = lax.axis_size("x")
    pairs = []
    for y in range(n):
        for x in range(n):
            for core in range(2):
                along_x = (core == 0) == early
                to_x = (x + by) % n if along_x else x
                to_y = y if along_x else (y + by) % n
                pairs.append(((y * n + x) * 2 + core, (to_y * n + to_x) * 2 + core))
    return lax.ppermute(a, ("y", "x", "core"), pairs)


def cross_place(early):
    along_x = (lax.axis_index("core") == 0) == early
    return jnp.where(along_x, lax.axis_index("x"), lax.axis_index("y"))


def cross_fetched(a, early):
    return [a] + [crossed(a, early, k) for k in range(1, lax.axis_size("x"))]


def cross_stack(parts):
    return jnp.stack(in_place(parts, cross_place(True)))


def cross_end(parts):
    every = jnp.stack(in_place(parts, cross_place(False)))
    first = lax.axis_index("core") == 0
    return jnp.where(first, every, jnp.swapaxes(every, 0, 1)).transpose(2, 0, 1, 3, 4)


def assembled(groups):
    first = lax.axis_index("core") == 0
    far = []
    for parts in groups:
        every = jnp.stack(in_place(parts, cross_place(False)))
        grid = jnp.where(first, every, jnp.swapaxes(every, 0, 1))
        far += [grid[:, :, j] for j in range(grid.shape[2])]
    return jnp.stack(in_place(far, lax.axis_index("z")))


def spots(groups):
    out, base = [], 0
    for parts in groups:
        for k, part in enumerate(parts):
            out.append((len(out), base, k))
        base += parts[0].shape[1]
    return out


def grid_of(a):
    nz, ny, nx = (lax.axis_size(axis) for axis in ("z", "y", "x"))
    return a.reshape(nz, ny, nx, -1, a.shape[-1])


def late_shares(a):
    n = lax.axis_size("x")
    first = lax.axis_index("core") == 0
    y, x = lax.axis_index("y"), lax.axis_index("x")
    return [
        jnp.where(
            first,
            lax.dynamic_index_in_dim(a, (y + k) % n, 1, False),
            lax.dynamic_index_in_dim(a, (x + k) % n, 2, False),
        )
        for k in range(n)
    ]


def early_shares(stage):
    total = added(*stage).astype(BF16)
    n, me = lax.axis_size("x"), cross_place(True)
    return [lax.dynamic_index_in_dim(total, (me + k) % n, 1, False) for k in range(n)]


def cross_sent(parts, early):
    return parts[0], [crossed(a, early, k) for k, a in enumerate(parts) if k]


def core_pick(a, core):
    return (
        lax.dynamic_index_in_dim(a, core, 0, False),
        lax.dynamic_index_in_dim(a, 1 - core, 0, False),
    )


def chip_rows(mine, got, core):
    first = core == 0
    return jnp.concatenate(
        [jnp.where(first, mine, got), jnp.where(first, got, mine)], axis=-2
    )


def own_rows(total, core):
    mine, other = core_pick(total.reshape(2, -1, total.shape[-1]), core)
    got = swap(other)
    first = core == 0
    return jnp.stack([jnp.where(first, mine, got), jnp.where(first, got, mine)], axis=0)


def z_sum(a):
    parts = in_place([p if k == 0 else turned(p, "z", k) for k, p in enumerate(shares(a, "z", 0))], lax.axis_index("z"))
    total = parts[0]
    for part in parts[1:]:
        total = total + part
    return total


def plane_step(a, k):
    n = lax.axis_size("x")
    ky, kx = divmod(k, n)
    pairs = [(j * n + i, (j + ky) % n * n + (i + kx) % n) for j in range(n) for i in range(n)]
    return lax.ppermute(a, ("y", "x"), pairs)


def plane_fetched(a):
    return [a] + [plane_step(a, k) for k in range(1, lax.axis_size("x") ** 2)]


def plane_order(parts):
    n = lax.axis_size("x")
    rows_of = [in_place(parts[k * n : (k + 1) * n], lax.axis_index("x")) for k in range(n)]
    columns_of = [in_place([r[i] for r in rows_of], lax.axis_index("y")) for i in range(n)]
    return [[columns_of[i][j] for i in range(n)] for j in range(n)]


def plane_stack(parts):
    return jnp.stack([jnp.stack(row) for row in plane_order(parts)])


def plane_shares(a):
    n = lax.axis_size("x")
    y, x = lax.axis_index("y"), lax.axis_index("x")
    out = []
    for k in range(n * n):
        ky, kx = divmod(k, n)
        one = lax.dynamic_index_in_dim(a, (y + ky) % n, 1, False)
        out.append(lax.dynamic_index_in_dim(one, (x + kx) % n, 1, False))
    return out


def plane_sum(shares):
    parts = [a if k == 0 else plane_step(a, k) for k, a in enumerate(shares)]
    total = None
    for row in plane_order(parts):
        for part in row:
            total = part if total is None else total + part
    return total


def dot1(a, b, dims=((1,), (0,))):
    return lax.dot_general(
        a.astype(BF16), b.astype(BF16), (dims, ((), ())), preferred_element_type=F32
    )


TN = ((0,), (0,))
NT = ((1,), (1,))


def split(a):
    high = a.astype(BF16)
    return high, (a - high.astype(F32)).astype(BF16)


def dot3(a, b):
    ah, al = split(a)
    bh, bl = split(b)
    return dot1(ah, bh) + (dot1(ah, bl) + dot1(al, bh))


def sigmoid(v):
    return 1.0 / (1.0 + jnp.exp(-v))


def grid_masks(n):
    i = lax.broadcasted_iota(jnp.int32, (n, n), 0)
    j = lax.broadcasted_iota(jnp.int32, (n, n), 1)
    return i, j


def unit_inverses(lowers, i, j):
    n = lowers[0].shape[0]
    level = jnp.where(i > j, i ^ j, 0)
    eye = jnp.where(i == j, 1.0, 0.0).astype(F32)
    highs = [a.astype(BF16) for a in lowers]
    lows = [(a - h.astype(F32)).astype(BF16) for a, h in zip(lowers, highs)]
    inverses = [eye - jnp.where(level == 1, a, 0.0) for a in lowers]
    size = 2
    while size < n:
        corner = (level >= size) & (level < 2 * size)
        lefts = [t.astype(BF16) for t in inverses]
        inner = [dot1(jnp.where(corner, h, jnp.zeros_like(h)), t) for h, t in zip(highs, lefts)]
        inverses = [t - dot1(b, c) for t, b, c in zip(inverses, lefts, inner)]
        size *= 2
    parts = [split(t) for t in inverses]
    rests = [
        eye - t - (dot1(h, th) + (dot1(h, tl) + dot1(lo, th)))
        for t, h, lo, (th, tl) in zip(inverses, highs, lows, parts)
    ]
    return [t + dot1(th, r) for t, (th, _), r in zip(inverses, parts, rests)]


def conv_of(ext, taps, rows):
    total = taps[0:1, :] * ext[HALO - 3 : HALO - 3 + rows]
    for i in range(1, CONV):
        total = total + taps[i : i + 1, :] * ext[HALO - 3 + i : HALO - 3 + i + rows]
    return total


def block_moves(places, me_ref, parts, grid):
    nz, n, _ = grid
    core, my_y, my_x, my_z = (me_ref[i] for i in range(4))
    moves = []
    for (number, base, k), part in zip(places, parts):
        late = lax.rem(jnp.where(core == 0, my_y, my_x) + (n - k), n)
        for i in range(part.shape[0]):
            to_y = jnp.where(core == 0, late, i)
            to_x = jnp.where(core == 0, i, late)
            for j in range(part.shape[1]):
                to_z = lax.rem(my_z + (nz - base - j), nz)
                moves.append((part.at[i, j], (to_z, to_y, to_x)))
    return moves


def place_kernel(places, cuts, grid, me_ref, *refs):
    parts, outs, sem = refs[: len(places)], refs[-1 - len(cuts) : -1], refs[-1]
    copies = []
    for part, to in block_moves(places, me_ref, parts, grid):
        for (low, high), out in zip(cuts, outs):
            copies.append(
                pltpu.make_async_copy(
                    part.at[:, pl.ds(low, high - low)], out.at[to], sem.at[len(copies)]
                )
            )
            copies[-1].start()
    for copy in copies:
        copy.wait()


def first_kernel(half, places, me_ref, *refs):
    parts, refs = refs[: len(places)], refs[len(places) :]
    if half == 0:
        x_ref, g_ref, beta_ref, cv_ref, bias_ref = refs[:5]
        n_ref, w_ref, pre_ref, qkv_ref, t_ref, wu_ref, pd_ref, b_ref, sem = refs[5:]
    else:
        n_ref, beta_ref, cv_ref, bias_ref = refs[:4]
        w_ref, pre_ref, qkv_ref, t_ref, wu_ref, pd_ref, b_ref, sem = refs[-8:]
    rows = qkv_ref.shape[1] // 2
    frame = rows + HALO
    copies = []
    columns_of = pl.ds(half * 768, 768)
    for part, to in block_moves(places, me_ref, parts, w_ref.shape[:3]):
        copies.append(
            pltpu.make_async_copy(
                part.at[:, columns_of], w_ref.at[to], sem.at[len(copies)]
            )
        )
        copies[-1].start()
    if half == 0:
        x = x_ref[...].astype(F32)
        scale = lax.rsqrt(jnp.mean(x * x, axis=-1, keepdims=True) + EPS)
        n_ref[...] = (x * scale * g_ref[...]).astype(BF16)
    normed = n_ref[...]
    for copy in copies:
        copy.wait()
    pre_ref[0] = dot1(normed, w_ref[...].reshape(D, 768)).astype(BF16)
    linear = dot1(normed, beta_ref[0])
    i, j = grid_masks(rows)
    keys, rights, lowers = [], [], []
    for q in range(2):
        rate = sigmoid(linear[q * frame + HALO : (q + 1) * frame] + bias_ref[0, q : q + 1, :])
        b_ref[0, q * rows : (q + 1) * rows, :] = rate
        ext = pre_ref[0, q * frame : (q + 1) * frame, :].astype(F32)
        conv = conv_of(ext, cv_ref[0], rows)
        act = conv * sigmoid(conv)
        for h in range(2):
            place = pl.ds(q * rows, rows)
            parts = []
            for kind in range(3):
                lane = (kind * 2 + h) * DK
                one = act[:, lane : lane + DK]
                if kind < 2:
                    one = one * lax.rsqrt(jnp.sum(one * one, axis=-1, keepdims=True) + EPS)
                if kind == 0:
                    one = one * DK ** (-0.5)
                one = one.astype(BF16)
                qkv_ref[0, place, lane : lane + DK] = one
                parts.append(one)
            key, value = parts[1], parts[2]
            col = rate[:, h : h + 1]
            keys.append(key)
            rights.append(jnp.concatenate([key, value], axis=1).astype(F32) * col)
            lowers.append(jnp.where(i > j, dot1(key, key, NT) * col, 0.0))
    inverses = unit_inverses(lowers, i, j)
    boths = [dot3(t, r) for t, r in zip(inverses, rights)]
    for p in range(4):
        t_ref[0, p] = inverses[p].astype(BF16)
        wu_ref[0, p] = boths[p].astype(BF16)
    for p in range(4):
        pd_ref[0, p] = dot1(keys[p], boths[p], TN).astype(BF16)


def state_kernel(pd_ref, s_ref):
    count = pd_ref.shape[0]
    state = jnp.zeros((DK, DK), F32)
    for s in range(count):
        s_ref[s] = state.astype(BF16)
        if s + 1 < count:
            high, low = split(state)
            move = pd_ref[s, :, :DK]
            state = state - (dot1(move, high) + dot1(move, low)) + pd_ref[s, :, DK:].astype(F32)


def adjoint_kernel(pd_ref, g_ref, l_ref):
    count = pd_ref.shape[0]
    adjoint = jnp.zeros((DK, DK), F32)
    for s in range(count - 1, -1, -1):
        l_ref[s] = adjoint.astype(BF16)
        if s > 0:
            high, low = split(adjoint)
            move = pd_ref[s, :, :DK]
            adjoint = (
                adjoint - (dot1(move, high, TN) + dot1(move, low, TN)) + g_ref[s].astype(F32)
            )


def pair_places(rows):
    return [
        (q * 2 + h, pl.ds(q * rows, rows), pl.ds(h * DK, DK), h) for q in range(2) for h in range(2)
    ]


def kind_lanes(kind, h):
    return pl.ds((kind * 2 + h) * DK, DK)


def second_kernel(qkv_ref, wu_ref, s_ref, hg_ref, f_ref, m_ref, h_ref):
    rows = qkv_ref.shape[1] // 2
    i, j = grid_masks(rows)
    pairs = pair_places(rows)
    queries = [qkv_ref[0, at, kind_lanes(0, h)] for _, at, _, h in pairs]
    keys = [qkv_ref[0, at, kind_lanes(1, h)] for _, at, _, h in pairs]
    scores = [jnp.where(i >= j, dot1(a, b, NT), 0.0).astype(BF16) for a, b in zip(queries, keys)]
    freshes = [
        (wu_ref[0, p, :, DK:].astype(F32) - dot1(wu_ref[0, p, :, :DK], s_ref[p])).astype(BF16)
        for p, _, _, _ in pairs
    ]
    mixes = [
        dot1(queries[p], s_ref[p]) + dot1(scores[p], freshes[p]) for p, _, _, _ in pairs
    ]
    for p, at, lanes, _ in pairs:
        mixed = mixes[p]
        scale = lax.rsqrt(jnp.mean(mixed * mixed, axis=-1, keepdims=True) + EPS)
        f_ref[at, lanes] = freshes[p]
        m_ref[at, lanes] = mixed
        h_ref[at, lanes] = (mixed * scale * hg_ref[...]).astype(BF16)


def third_kernel(qkv_ref, wu_ref, s_ref, f_ref, m_ref, dh_ref, hg_ref, sg_ref, gf_ref, gq_ref, gk_ref, ghg_ref):
    rows = qkv_ref.shape[1] // 2
    i, j = grid_masks(rows)
    gain = hg_ref[...]
    gain_grad = jnp.zeros((1, DK), F32)
    pairs = pair_places(rows)
    queries = [qkv_ref[0, at, kind_lanes(0, h)] for _, at, _, h in pairs]
    keys = [qkv_ref[0, at, kind_lanes(1, h)] for _, at, _, h in pairs]
    scores = [jnp.where(i >= j, dot1(a, b, NT), 0.0).astype(BF16) for a, b in zip(queries, keys)]
    grads = []
    for _, at, lanes, _ in pairs:
        mixed = m_ref[at, lanes]
        up = dh_ref[at, lanes].astype(F32)
        scale = lax.rsqrt(jnp.mean(mixed * mixed, axis=-1, keepdims=True) + EPS)
        unit = mixed * scale
        gain_grad = gain_grad + jnp.sum(up * unit, axis=0, keepdims=True)
        inner = up * gain
        grad = scale * (inner - unit * jnp.mean(inner * unit, axis=-1, keepdims=True))
        grads.append(grad.astype(BF16))
    ghg_ref[0] = jnp.broadcast_to(gain_grad, ghg_ref.shape[1:])
    fresh_grads = [dot1(a, g, TN) for a, g in zip(scores, grads)]
    starts = [
        dot1(queries[p], grads[p], TN) - dot1(wu_ref[0, p, :, :DK], fresh_grads[p], TN)
        for p in range(4)
    ]
    score_grads = [
        jnp.where(i >= j, dot1(grads[p], f_ref[at, lanes], NT), 0.0).astype(BF16)
        for p, at, lanes, _ in pairs
    ]
    for p, at, lanes, _ in pairs:
        gf_ref[at, lanes] = fresh_grads[p]
        sg_ref[0, p] = starts[p].astype(BF16)
        gq_ref[at, lanes] = dot1(grads[p], s_ref[p], NT) + dot1(score_grads[p], keys[p])
        gk_ref[at, lanes] = dot1(score_grads[p], queries[p], TN)


def fourth_kernel(qkv_ref, pre_ref, cv_ref, b_ref, t_ref, wu_ref, s_ref, l_ref, f_ref, gf_ref, gq_ref, gk_ref, eg_ref, gc_ref, lg_ref, gb_ref):
    rows = qkv_ref.shape[1] // 2
    frame = rows + HALO
    i, j = grid_masks(rows)
    lane = lax.broadcasted_iota(jnp.int32, (rows, DK), 1)
    pairs = pair_places(rows)
    keys = [qkv_ref[0, at, kind_lanes(1, h)] for _, at, _, h in pairs]
    values = [qkv_ref[0, at, kind_lanes(2, h)] for _, at, _, h in pairs]
    cols = [b_ref[0, at, h : h + 1] for _, at, _, h in pairs]
    fresh_grads = [
        gf_ref[at, lanes] + dot1(keys[p], l_ref[p]) for p, at, lanes, _ in pairs
    ]
    lows = [g.astype(BF16) for g in fresh_grads]
    factor_grads = [
        jnp.concatenate([-dot1(lows[p], s_ref[p], NT).astype(BF16), lows[p]], axis=1)
        for p in range(4)
    ]
    solved = [dot1(t_ref[0, p], factor_grads[p], TN) for p in range(4)]
    inners = [dot1(k, k, NT) for k in keys]
    system_grads = [
        jnp.where(i > j, -dot1(solved[p], wu_ref[0, p], NT), 0.0) for p in range(4)
    ]
    inner_grads = [(g * c).astype(BF16) for g, c in zip(system_grads, cols)]
    key_grads = [
        gk_ref[at, lanes]
        + dot1(f_ref[at, lanes], l_ref[p], NT)
        + cols[p] * solved[p][:, :DK]
        + dot1(inner_grads[p], keys[p])
        + dot1(inner_grads[p], keys[p], TN)
        for p, at, lanes, _ in pairs
    ]
    rate_grads = [
        (
            jnp.sum(
                solved[p][:, :DK] * keys[p].astype(F32) + solved[p][:, DK:] * values[p].astype(F32),
                axis=-1,
                keepdims=True,
            )
            + jnp.sum(system_grads[p] * inners[p], axis=-1, keepdims=True)
        )
        * cols[p]
        * (1.0 - cols[p])
        for p in range(4)
    ]
    for q in range(2):
        place = pl.ds(q * rows, rows)
        logit = jnp.where(
            lane == 0, rate_grads[2 * q], jnp.where(lane == 1, rate_grads[2 * q + 1], 0.0)
        )
        lg_ref[0, place, :] = logit.astype(BF16)
        gb_ref[0, q : q + 1, :] = jnp.sum(logit, axis=0, keepdims=True)
    zero = jnp.zeros((HALO, DK), F32)
    for kind in range(3):
        for h in range(2):
            at = kind_lanes(kind, h)
            tap = cv_ref[0, :, at]
            conv_grad = [jnp.zeros((1, DK), F32) for _ in range(CONV)]
            for q in range(2):
                p = q * 2 + h
                ext = pre_ref[0, q * frame : (q + 1) * frame, at].astype(F32)
                views = [ext[HALO - 3 + t : HALO - 3 + t + rows] for t in range(CONV)]
                conv = tap[0:1, :] * views[0]
                for t in range(1, CONV):
                    conv = conv + tap[t : t + 1, :] * views[t]
                sig = sigmoid(conv)
                act = conv * sig
                if kind == 0:
                    grad = gq_ref[q * rows : (q + 1) * rows, h * DK : (h + 1) * DK] * DK ** (-0.5)
                elif kind == 1:
                    grad = key_grads[p]
                else:
                    grad = cols[p] * solved[p][:, DK:]
                if kind < 2:
                    scale = lax.rsqrt(jnp.sum(act * act, axis=-1, keepdims=True) + EPS)
                    unit = act * scale
                    grad = scale * (grad - unit * jnp.sum(grad * unit, axis=-1, keepdims=True))
                grad = grad * (sig * (1.0 + conv * (1.0 - sig)))
                wide = jnp.concatenate([zero, grad, zero], axis=0)
                total = tap[0:1, :] * wide[3 : 3 + frame]
                for t in range(1, CONV):
                    total = total + tap[t : t + 1, :] * wide[3 - t : 3 - t + frame]
                eg_ref[q * frame : (q + 1) * frame, at] = total.astype(BF16)
                for t in range(CONV):
                    conv_grad[t] = conv_grad[t] + jnp.sum(grad * views[t], axis=0, keepdims=True)
            for t in range(CONV):
                gc_ref[0, t : t + 1, at] = conv_grad[t]


def lead(*shape):
    return pl.BlockSpec((1,) + shape, lambda p: (p,) + (0,) * len(shape))


def at_half(half, *shape):
    return pl.BlockSpec((1,) + shape, lambda p: (half,) + (0,) * len(shape))


def whole(*shape):
    return pl.BlockSpec(shape, lambda p: (0,) * len(shape))


def columns(rows, cols):
    return pl.BlockSpec((rows, cols), lambda p: (0, p))


def quarter():
    return pl.BlockSpec((4, DK, DK), lambda p: (p, 0, 0))


def cost(microseconds):
    return pl.CostEstimate(
        flops=int(microseconds * 1.15e9), bytes_accessed=0, transcendentals=0
    )


def on_core(kernel, outs, in_specs, out_specs, name, microseconds):
    return pl.pallas_call(
        kernel,
        out_shape=outs,
        grid=(2,),
        in_specs=in_specs,
        out_specs=out_specs,
        compiler_params=pltpu.CompilerParams(
            vmem_limit_bytes=VMEM_LIMIT, dimension_semantics=("arbitrary",)
        ),
        cost_estimate=cost(microseconds),
        name=name,
    )


def sds(shape, kind):
    return jax.ShapeDtypeStruct(shape, kind)


def all_ranges(a):
    if lax.axis_size("z") * lax.axis_size("y") == a.shape[0]:
        return lax.all_to_all(a, SEQ, 0, 0, tiled=True)
    return lax.all_gather(a, SEQ)


def scan_states(every):
    count = lax.axis_size("z") * lax.axis_size("y")
    if every.ndim == 3:
        return pl.pallas_call(
            state_kernel,
            out_shape=sds((count, DK, DK), BF16),
            cost_estimate=cost(3),
            name="state_scan",
        )(every)

    def step(s, state):
        one = lax.dynamic_index_in_dim(every, s, 0, False).astype(F32)
        moved = jnp.einsum(
            "pij,pjk->pik", one[:, :, :DK], state, precision=lax.Precision.HIGHEST
        )
        return state - moved + one[:, :, DK:]

    start = jnp.zeros((every.shape[1], DK, DK), F32)
    return lax.fori_loop(0, lax.axis_index(SEQ), step, start).astype(BF16)


def scan_adjoints(every, grads):
    count = lax.axis_size("z") * lax.axis_size("y")
    if every.ndim == 3:
        return pl.pallas_call(
            adjoint_kernel,
            out_shape=sds((count, DK, DK), BF16),
            cost_estimate=cost(3),
            name="adjoint_scan",
        )(every, grads)

    def step(k, adjoint):
        s = count - 1 - k
        one = lax.dynamic_index_in_dim(every, s, 0, False).astype(F32)
        moved = jnp.einsum(
            "pji,pjk->pik", one[:, :, :DK], adjoint, precision=lax.Precision.HIGHEST
        )
        return adjoint - moved + lax.dynamic_index_in_dim(grads, s, 0, False).astype(F32)

    start = jnp.zeros((every.shape[1], DK, DK), F32)
    steps = count - 1 - lax.axis_index(SEQ)
    return lax.fori_loop(0, steps, step, start).astype(BF16)


def own_range(a):
    if lax.axis_size("z") * lax.axis_size("y") == H:
        return lax.all_to_all(a, SEQ, 0, 0, tiled=True)
    return a


def shards(
    inputs,
    domain_ids,
    norm1_gain,
    w_qkv,
    w_beta,
    conv_weight,
    domain_bias,
    head_gain,
    w_out,
    norm2_gain,
    w_gate_up,
    w_down,
    cotangent,
):
    core = lax.axis_index("core")
    nz, ny, nx = (lax.axis_size(a) for a in ("z", "y", "x"))
    z, y, x = (lax.axis_index(a) for a in ("z", "y", "x"))
    chips = nz * ny * nx
    seq_devices = nz * ny
    rows = inputs.shape[1]
    frame = rows + HALO
    tall = 2 * rows
    drows = w_qkv.shape[0]
    both_rows = 2 * drows
    frows = w_down.shape[0]
    grows = conv_weight.shape[0]
    first = core == 0
    half = H // 2
    fence = lax.optimization_barrier

    q_mine, q_other = core_pick(
        w_qkv.reshape(drows, 3, 2, 2, 256).transpose(2, 0, 3, 1, 4).reshape(2, drows, 1536), core
    )
    q_got = swap(q_other)
    small = jnp.concatenate(
        [norm1_gain, norm2_gain, w_beta.reshape(-1), conv_weight.reshape(-1)]
    )
    n_small = small.shape[0]
    small = jnp.pad(small, (0, 768 - n_small)).reshape(1, 768)
    small_got = swap(small)
    x_own = inputs.reshape(rows, D)
    small = jnp.concatenate(
        [jnp.where(first, small, small_got), jnp.where(first, small_got, small)], axis=1
    )
    small = jnp.pad(small, ((0, 7), (0, 0)))
    q_part = jnp.concatenate([chip_rows(q_mine, q_got, core), small], axis=0)
    q_part, x_own, w_gate_up, w_out, w_down, cotangent = fence(
        (q_part, x_own, w_gate_up, w_out, w_down, cotangent)
    )

    q_far = [q_part] + [turned(q_part, "z", k) for k in sorted({1, nz - 1})]
    q_far = relayed(q_far, "z")
    out_cols = w_out.reshape(drows, 2, 2, 256).transpose(1, 2, 0, 3)
    gu_cols = (
        w_gate_up.reshape(drows, 2, chips, 2, frows)
        .transpose(3, 1, 0, 2, 4)
        .reshape(2, 2, drows, FF // 2)
    )
    wide_cols = jnp.concatenate(
        [gu_cols[:, 0], gu_cols[:, 1], out_cols[:, 0], out_cols[:, 1]], axis=-1
    )
    wide_mine, wide_other = core_pick(wide_cols, core)
    wide_part = chip_rows(wide_mine, swap(wide_other), core)
    q_far, x_own, cotangent, wide_part, w_down = fence(
        (q_far, x_own, cotangent, wide_part, w_down)
    )
    halo = lax.ppermute(
        x_own[rows - HALO :], SEQ, [(i, i + 1) for i in range(seq_devices - 1)]
    )
    choose = (domain_ids[0] == jnp.arange(NDOM, dtype=jnp.int32)).astype(BF16)
    bias_own = jnp.sum(domain_bias.astype(F32) * choose.astype(F32)[:, None], axis=0)
    extra = jnp.pad(jnp.concatenate([bias_own.astype(BF16), choose]), (0, D - H - NDOM))
    extra = jnp.pad(extra.reshape(1, D), ((0, HALO - 1), (0, 0)))
    frame_own = jnp.concatenate([halo, x_own, extra], axis=0)
    frame_other = swap(frame_own)
    g_own = cotangent.reshape(rows, D)
    g_other = swap(g_own)

    q_parts = cross_fetched(jnp.stack([a[:both_rows] for a in q_far]), True)
    smalls = jnp.stack(in_place([a[both_rows].reshape(2, 768) for a in q_far], z))
    smalls = plane_fetched(smalls)
    ends = sorted({1, nz - 1})
    wide_near = [wide_part, turned(wide_part, "z", 1)]
    q_parts, w_down, smalls = fence((q_parts, w_down, smalls))
    smalls = plane_stack(smalls).transpose(2, 0, 1, 3, 4).reshape(2 * chips, 768)[:, :n_small]
    gain_one = smalls[:, :drows].reshape(1, D).astype(F32)
    gain_two = smalls[:, drows : 2 * drows].reshape(1, D).astype(F32)
    full_beta = smalls[:, 2 * drows : 2 * drows + drows * H].reshape(D, 2, half)
    full_conv = smalls[:, 2 * drows + drows * H :].reshape(3, 2, 2, 256, CONV)
    beta_mine = lax.dynamic_index_in_dim(full_beta, core, 1, False)
    conv_mine = (
        lax.dynamic_index_in_dim(full_conv, core, 1, False)
        .transpose(1, 3, 0, 2)
        .reshape(2, CONV, 768)
        .astype(F32)
    )
    beta_pairs = jnp.pad(
        beta_mine.reshape(D, 2, 2).transpose(1, 0, 2), ((0, 0), (0, 0), (0, DK - 2))
    )

    q_parts = cross_fetched(cross_stack(q_parts), False)
    wide_near, frame_own, frame_other = fence((wide_near, frame_own, frame_other))
    wide_rest = [turned(wide_near[0], "z", k) for k in ends[1:]]
    x_frames = jnp.concatenate([frame_own[:frame], frame_other[:frame]], axis=0)
    bias_both = jnp.stack([frame_own[frame, :H], frame_other[frame, :H]]).astype(F32)
    choose_both = jnp.stack(
        [frame_own[frame, H : H + NDOM], frame_other[frame, H : H + NDOM]]
    ).astype(F32)
    bias_mine = lax.dynamic_index_in_dim(bias_both.reshape(2, 2, half), core, 1, False)
    bias_pairs = jnp.pad(
        bias_mine.reshape(2, 2, 2).transpose(1, 0, 2), ((0, 0), (0, 0), (0, DK - 2))
    )
    x_both = jnp.concatenate(
        [frame_own[HALO:frame], frame_other[HALO:frame]], axis=0
    ).astype(F32)
    g_both = jnp.concatenate([g_own, g_other], axis=0)
    (
        q_parts,
        wide_near,
        wide_rest,
        w_down,
        gain_one,
        gain_two,
        beta_pairs,
        conv_mine,
        bias_pairs,
        x_frames,
        x_both,
        g_both,
    ) = fence(
        (
            q_parts,
            wide_near,
            wide_rest,
            w_down,
            gain_one,
            gain_two,
            beta_pairs,
            conv_mine,
            bias_pairs,
            x_frames,
            x_both,
            g_both,
        )
    )

    q_places = spots((q_parts,))
    blocks = chips
    if both_rows % 16 == 0:
        w_shape = sds((nz, ny, nx, both_rows, 768), BF16)
    else:
        w_shape = sds((1, 1, 1, D, 768), BF16)
        q_parts, q_places, blocks = [assembled((q_parts,)).reshape(1, 1, D, 1536)], [(0, 0, 0)], 1
    place = jnp.stack([core, y, x, z]).astype(jnp.int32)
    kept = (
        sds((2, 2 * frame, 768), BF16),
        sds((2, tall, 768), BF16),
        sds((2, 4, rows, rows), BF16),
        sds((2, 4, rows, 2 * DK), BF16),
        sds((2, 4, DK, 2 * DK), BF16),
        sds((2, tall, DK), F32),
    )
    anywhere = pl.BlockSpec(memory_space=pl.ANY)

    def local(number, parts, ins, in_specs, outs, out_specs, held):
        fixed = [at_half(number, D, DK), at_half(number, CONV, 768), at_half(number, 2, DK)]
        first_held = 1 + len(parts) + len(ins) + 3
        return pl.pallas_call(
            functools.partial(first_kernel, number, q_places),
            out_shape=outs + (w_shape,) + kept,
            grid=(1,),
            in_specs=[pl.BlockSpec(memory_space=pltpu.SMEM)]
            + [anywhere] * len(parts)
            + in_specs
            + fixed
            + [anywhere] * len(held),
            out_specs=out_specs
            + (whole(*w_shape.shape),)
            + tuple(at_half(number, *k.shape[1:]) for k in kept),
            scratch_shapes=[pltpu.SemaphoreType.DMA((blocks,))],
            input_output_aliases={
                first_held + k: len(outs) + 1 + k for k in range(len(held))
            },
            compiler_params=pltpu.CompilerParams(vmem_limit_bytes=VMEM_LIMIT),
            cost_estimate=cost(10),
            name="delta_local",
        )(place, *parts, *ins, beta_pairs, conv_mine, bias_pairs, *held)

    wide_rest = relayed(wide_near + wide_rest, "z")[2:]
    wide_u = cross_fetched(jnp.stack(wide_near), True)
    normed, w_q_one, *held = local(
        0,
        q_parts,
        (x_frames, gain_one),
        [whole(2 * frame, D), whole(1, D)],
        (sds((2 * frame, D), BF16),),
        (whole(2 * frame, D),),
        (),
    )
    normed, w_q_one, held, wide_rest, wide_u, q_parts, w_down = fence(
        (normed, w_q_one, held, wide_rest, wide_u, q_parts, w_down)
    )

    wide_rest, wide_two = jnp.stack(wide_rest), cross_stack(wide_u)
    wide_v = cross_fetched(wide_rest, True)
    wide_u = cross_fetched(wide_two, False)
    down_z = fetched(w_down, "z")
    w_q_two, *held = local(
        1,
        q_parts,
        (after(normed, wide_rest, wide_two),),
        [whole(2 * frame, D)],
        (),
        (),
        tuple(held),
    )
    pre, qkv, inverse, factors, pd, rates = held
    w_q_one = w_q_one.reshape(D, 768)
    w_q_two = w_q_two.reshape(D, 768)
    (
        normed,
        w_q_one,
        w_q_two,
        pre,
        qkv,
        inverse,
        factors,
        pd,
        rates,
        down_z,
        wide_v,
    ) = fence(
        (
            normed,
            w_q_one,
            w_q_two,
            pre,
            qkv,
            inverse,
            factors,
            pd,
            rates,
            down_z,
            wide_v,
        )
    )

    every = all_ranges(pd.reshape(H, DK, 2 * DK))
    down_stack = jnp.stack(in_place(down_z, z))
    wide_v = cross_fetched(cross_stack(wide_v), False)
    every, wide_u, down_stack = fence((every, wide_u, down_stack))

    states = scan_states(every)
    def placed(parts, places, held):
        return pl.pallas_call(
            functools.partial(place_kernel, places, cuts, (nz, ny, nx)),
            out_shape=[sds((nz, ny, nx, both_rows, hi - lo), BF16) for lo, hi in cuts],
            in_specs=[pl.BlockSpec(memory_space=pltpu.SMEM)]
            + [pl.BlockSpec(memory_space=pltpu.VMEM)] * len(parts)
            + [anywhere] * len(held),
            out_specs=[anywhere] * len(cuts),
            input_output_aliases={1 + len(parts) + k: k for k in range(len(held))},
            scratch_shapes=[
                pltpu.SemaphoreType.DMA(
                    (sum(p.shape[0] * p.shape[1] for p in parts) * len(cuts),)
                )
            ],
            compiler_params=pltpu.CompilerParams(vmem_limit_bytes=VMEM_LIMIT),
            cost_estimate=cost(3),
            name="placed",
        )(place, *parts, *held)

    cuts = ((FF, FF + D // 2), (0, FF // 2), (FF // 2, FF))
    wide_places = spots((wide_u, wide_v))
    wide = ()
    if both_rows % 16 == 0:
        wide = tuple(placed(after(wide_u, states), wide_places[: len(wide_u)], ()))
    states = after(own_range(states), wide)
    down_parts = cross_fetched(after(down_stack, wide), True)
    gain_head = head_gain.astype(F32).reshape(1, DK)
    fresh, mixed, heads_mine = on_core(
        second_kernel,
        (sds((tall, 512), BF16), sds((tall, 512), F32), sds((tall, 512), BF16)),
        [lead(tall, 768), lead(4, rows, 2 * DK), quarter(), whole(1, DK)],
        (columns(tall, 256), columns(tall, 256), columns(tall, 256)),
        "delta_mix",
        2,
    )(qkv, factors, states, gain_head)
    heads_got = swap(heads_mine)
    wide, wide_v, states, fresh, mixed, heads_mine, heads_got = fence(
        (wide, wide_v, states, fresh, mixed, heads_mine, heads_got)
    )

    down_parts = cross_fetched(cross_stack(down_parts), False)
    if both_rows % 16 == 0:
        out_mine, w_gate, w_up = placed(wide_v, wide_places[len(wide_u) :], wide)
    else:
        wide = assembled((wide_u, wide_v))
        out_mine, w_gate, w_up = (wide[..., lo:hi] for lo, hi in cuts)
    out_mine, w_gate, w_up = (a.reshape(D, -1) for a in (out_mine, w_gate, w_up))
    out_got = swap(out_mine)
    full_out = jnp.concatenate(
        [jnp.where(first, out_mine, out_got), jnp.where(first, out_got, out_mine)], axis=1
    )
    heads_got = jnp.concatenate([heads_got[rows:], heads_got[:rows]], axis=0)
    heads = jnp.concatenate(
        [jnp.where(first, heads_mine, heads_got), jnp.where(first, heads_got, heads_mine)], axis=1
    )
    middle = x_both + jnp.dot(heads, full_out, preferred_element_type=F32)
    scale_two = lax.rsqrt(jnp.mean(middle * middle, axis=-1, keepdims=True) + EPS)
    unit_two = middle * scale_two
    normed_two = (unit_two * gain_two).astype(BF16)
    gate = jnp.dot(normed_two, w_gate, preferred_element_type=F32)
    up = jnp.dot(normed_two, w_up, preferred_element_type=F32)
    sig = jax.nn.sigmoid(gate)
    hidden = (gate * sig * up).astype(BF16)
    grad_down = jnp.einsum("nf,nd->fd", hidden, g_both, preferred_element_type=F32).astype(BF16)
    down_shares = late_shares(grid_of(grad_down))
    down_stage = cross_sent(down_shares, False)
    w_down_mine = cross_end(after(down_parts, down_shares)).reshape(chips * frows, D)
    hidden_grad = jnp.einsum("nd,fd->nf", g_both, w_down_mine, preferred_element_type=F32)
    up_grad = (hidden_grad * gate * sig).astype(BF16)
    gate_grad = (hidden_grad * up * sig * (1.0 + gate * (1.0 - sig))).astype(BF16)
    up_grad, gate_grad = fence((up_grad, gate_grad))

    grad_gate = jnp.einsum("nd,nf->df", normed_two, gate_grad, preferred_element_type=F32)
    gate_shares = late_shares(grid_of(grad_gate.astype(BF16)))
    gate_stage = cross_sent(gate_shares, False)
    normed_two_part = jnp.einsum(
        "nf,df->nd", after(gate_grad, gate_shares), w_gate, preferred_element_type=F32
    ) + jnp.einsum("nf,df->nd", up_grad, w_up, preferred_element_type=F32)
    part_low = normed_two_part.astype(BF16)
    part_got, down_stage = fence((swap(part_low), down_stage))
    grad_up = jnp.einsum(
        "nd,nf->df", after(normed_two, part_low), up_grad, preferred_element_type=F32
    ).astype(BF16)
    up_shares = late_shares(grid_of(grad_up))
    up_stage = cross_sent(up_shares, False)
    part_got = after(part_got, up_shares)
    part_got = jnp.concatenate([part_got[rows:], part_got[:rows]], axis=0)
    normed_two_grad = normed_two_part + part_got.astype(F32)
    grad_norm2 = jnp.sum(normed_two_grad[:rows] * unit_two[:rows], axis=0)
    inner = normed_two_grad * gain_two
    middle_grad = g_both.astype(F32) + scale_two * (
        inner - unit_two * jnp.mean(inner * unit_two, axis=-1, keepdims=True)
    )
    middle_low = middle_grad.astype(BF16)
    out_rows = lax.dynamic_slice_in_dim(full_out, core * 512, 512, 0)
    heads_grad = jnp.einsum("ne,de->nd", middle_low, out_rows, preferred_element_type=F32)
    start_grad, fresh_grad, query_grad, key_grad, gain_part = on_core(
        third_kernel,
        (
            sds((2, 4, DK, DK), BF16),
            sds((tall, 512), F32),
            sds((tall, 512), F32),
            sds((tall, 512), F32),
            sds((2, 8, DK), F32),
        ),
        [
            lead(tall, 768),
            lead(4, rows, 2 * DK),
            quarter(),
            columns(tall, 256),
            columns(tall, 256),
            columns(tall, 256),
            whole(1, DK),
        ],
        (
            lead(4, DK, DK),
            columns(tall, 256),
            columns(tall, 256),
            columns(tall, 256),
            lead(8, DK),
        ),
        "delta_back_local",
        5,
    )(qkv, factors, states, fresh, mixed, heads_grad, gain_head)
    (
        start_grad,
        fresh_grad,
        query_grad,
        key_grad,
        gain_part,
        middle_low,
        hidden,
    ) = fence(
        (
            start_grad,
            fresh_grad,
            query_grad,
            key_grad,
            gain_part,
            middle_low,
            hidden,
        )
    )

    start_grads = all_ranges(start_grad.reshape(H, DK, DK))
    low_cols = lax.dynamic_slice_in_dim(middle_low, core * 512, 512, 1)
    grad_out = jnp.einsum("nd,ne->de", heads, low_cols, preferred_element_type=F32)
    out_shares = late_shares(grid_of(grad_out.astype(BF16)))
    out_stage = cross_sent(out_shares, False)
    adjoints = scan_adjoints(every, after(start_grads, out_shares))
    down_shares = early_shares(after(down_stage, adjoints))
    down_stage = cross_sent(down_shares, True)
    gate_shares = early_shares(after(gate_stage, down_shares))
    gate_stage = cross_sent(gate_shares, True)
    up_shares = [
        jnp.concatenate(cut, axis=-1)
        for cut in zip(*(early_shares(stage) for stage in after((up_stage, out_stage), adjoints)))
    ]
    up_stage = cross_sent(up_shares, True)
    adjoints = own_range(adjoints)
    down_shares = shares(added(*after(down_stage, gate_shares)).astype(BF16), "z", 0)
    down_stage = sent(down_shares, "z")
    adjoints = after(adjoints, up_shares, down_shares)
    ext_grad, conv_part, logit_low, bias_part = on_core(
        fourth_kernel,
        (
            sds((2 * frame, 1536), BF16),
            sds((2, CONV, 768), F32),
            sds((2, tall, DK), BF16),
            sds((2, 2, DK), F32),
        ),
        [
            lead(tall, 768),
            lead(2 * frame, 768),
            lead(CONV, 768),
            lead(tall, DK),
            lead(4, rows, rows),
            lead(4, rows, 2 * DK),
            quarter(),
            quarter(),
            columns(tall, 256),
            columns(tall, 256),
            columns(tall, 256),
            columns(tall, 256),
        ],
        (columns(2 * frame, 768), lead(CONV, 768), lead(tall, DK), lead(2, DK)),
        "delta_back",
        15,
    )(qkv, pre, conv_mine, rates, inverse, factors, states, adjoints, fresh, fresh_grad, query_grad, key_grad)
    ext_grad, conv_part, logit_low, bias_part, gate_stage, up_stage, down_stage = fence(
        (ext_grad, conv_part, logit_low, bias_part, gate_stage, up_stage, down_stage)
    )

    ext_frames = ext_grad.reshape(2, frame, 1536)
    grad_q = jnp.einsum("nd,nf->df", normed, ext_grad, preferred_element_type=F32).astype(BF16)
    q_shares = late_shares(grid_of(grad_q))
    ext_frames, gate_stage, up_stage, q_shares = fence(
        (ext_frames, gate_stage, up_stage, q_shares)
    )
    q_stage = cross_sent(q_shares, False)
    sent_back = lax.ppermute(
        ext_frames[:, :HALO], SEQ, [(i + 1, i) for i in range(seq_devices - 1)]
    )
    wide_part = jnp.concatenate([added(*gate_stage), added(*up_stage)], axis=-1).astype(BF16)
    wide_own, ahead, behind = relays(shares(wide_part, "z", 0), "z")
    behind = turned(behind, "z", nz - 1)
    tail = ext_frames[:, frame - HALO :].astype(F32) + sent_back.astype(F32)
    pre_low = jnp.concatenate(
        [ext_frames[:, HALO : frame - HALO], tail.astype(BF16)], axis=1
    ).reshape(tall, 1536)
    normed_part = (
        jnp.einsum("nf,df->nd", pre_low[:, :768], w_q_one, preferred_element_type=F32)
        + jnp.einsum("nf,df->nd", pre_low[:, 768:], w_q_two, preferred_element_type=F32)
        + jnp.einsum("pnh,pdh->nd", logit_low, beta_pairs, preferred_element_type=F32)
    )
    part_low = normed_part[rows:].astype(BF16)
    down_part = jnp.dot(after(hidden, part_low), w_down_mine, preferred_element_type=F32)
    output = middle[:rows] + down_part[:rows]
    down_part = down_part[rows:].astype(BF16)
    part_low, ahead, behind, output, down_part = fence(
        (part_low, ahead, behind, output, down_part)
    )
    wide_stage = (wide_own, [turned(ahead, "z", 1), behind])
    normed_grad = normed_part[:rows] + swap(part_low).astype(F32)
    q_stage, normed_grad, normed, conv_part, logit_low, x_both = fence(
        (q_stage, normed_grad, normed, conv_part, logit_low, x_both)
    )

    q_shares, normed_grad, x_both = fence((early_shares(q_stage), normed_grad, x_both))
    q_stage = cross_sent(q_shares, True)
    x32 = x_both[:rows]
    scale_one = lax.rsqrt(jnp.mean(x32 * x32, axis=-1, keepdims=True) + EPS)
    unit_one = x32 * scale_one
    grad_norm1 = jnp.sum(normed_grad * unit_one, axis=0)
    inner_one = normed_grad * gain_one
    grad_input = middle_grad[:rows] + scale_one * (
        inner_one - unit_one * jnp.mean(inner_one * unit_one, axis=-1, keepdims=True)
    )
    grad_input = grad_input.reshape(1, rows, D)
    normed_tokens = normed.reshape(2, frame, D)[:, HALO:].reshape(tall, D)
    grad_beta = jnp.einsum(
        "nd,pnh->dph", normed_tokens, logit_low[:, :, :2], preferred_element_type=F32
    ).reshape(D, half)
    beta_full = jnp.where(
        first,
        jnp.pad(grad_beta, ((0, 0), (0, half))),
        jnp.pad(grad_beta, ((0, 0), (half, 0))),
    )
    conv_cols = conv_part.reshape(2, CONV, 3, 256).transpose(2, 0, 3, 1).reshape(3, 512, CONV)
    conv_full = jnp.where(
        first,
        jnp.pad(conv_cols, ((0, 0), (0, 512), (0, 0))),
        jnp.pad(conv_cols, ((0, 0), (512, 0), (0, 0))),
    )
    bias_heads = bias_part[:, :, :2].transpose(1, 0, 2).reshape(2, half)
    bias_heads = jnp.where(
        first,
        jnp.pad(bias_heads, ((0, 0), (0, half))),
        jnp.pad(bias_heads, ((0, 0), (half, 0))),
    )
    bias_grad = jnp.sum(choose_both[:, :, None] * bias_heads[:, None, :], axis=0)
    shared = jnp.concatenate([bias_grad.reshape(-1), gain_part[0, 0] + gain_part[1, 0]])
    shared = jnp.broadcast_to(shared, (2 * chips, shared.shape[0]))
    pack = jnp.concatenate(
        [
            grad_norm2.reshape(2 * chips, drows),
            beta_full.reshape(2 * chips, drows * H),
            conv_full.reshape(2 * chips, grows * CONV),
            shared,
        ],
        axis=1,
    )
    pack = jnp.pad(pack, ((0, 0), (0, -pack.shape[1] % DK)))
    norm_rows = jnp.pad(grad_norm1.reshape(2 * chips, drows), ((0, 0), (0, DK - drows)))
    pack = jnp.concatenate([norm_rows, pack], axis=1).reshape(chips, 2, -1)
    pack_own = lax.dynamic_index_in_dim(pack, core, 1, False)
    pack_got = swap(lax.dynamic_index_in_dim(pack, 1 - core, 1, False))
    pack = plane_shares((pack_own + pack_got).reshape(nz, ny, nx, -1))
    q_stage, pack = fence((q_stage, pack))

    q_shares = fence(shares(added(*q_stage).astype(BF16), "z", 0))
    q_own, ahead, behind = relays(q_shares, "z")
    behind = turned(behind, "z", nz - 1)
    output = (output + swap(after(down_part, q_shares)).astype(F32)).astype(BF16)
    output = output.reshape(1, rows, D)
    pack = plane_sum(pack)
    own_down = added(*after(down_stage, q_shares))
    wide_own = own_rows(added(*after(wide_stage, q_shares)), core)
    ahead, behind, pack, own_down, wide_own, output = fence(
        (ahead, behind, pack, own_down, wide_own, output)
    )
    q_stage = (q_own, [turned(ahead, "z", 1), behind])
    own_gu = (
        wide_own[..., :FF]
        .reshape(2, drows, 2, chips, frows)
        .transpose(1, 2, 3, 0, 4)
        .reshape(drows, 2 * FF)
    )
    own_out = wide_own[..., FF:].transpose(1, 0, 2).reshape(drows, D)
    mine = z_sum(pack)
    q_stage, mine, own_gu, own_down, own_out = fence((q_stage, mine, own_gu, own_down, own_out))

    q_own = own_rows(added(*q_stage), core)
    own_qkv = jnp.concatenate(
        [
            q_own[c, :, (hp * 3 + kind) * 256 : (hp * 3 + kind + 1) * 256]
            for kind in range(3)
            for c in range(2)
            for hp in range(2)
        ],
        axis=1,
    )
    own_g1 = mine[:drows]
    at = DK
    own_g2 = mine[at : at + drows]
    at += drows
    own_beta = mine[at : at + drows * H].reshape(drows, H)
    at += drows * H
    own_conv = mine[at : at + grows * CONV].reshape(grows, CONV)
    at += grows * CONV
    bias_total = mine[at : at + NDOM * H].reshape(NDOM, H)
    at += NDOM * H
    gain_total = mine[at : at + DK]
    return (
        output,
        grad_input,
        own_g1,
        own_qkv,
        own_beta,
        own_conv,
        bias_total,
        gain_total,
        own_out,
        own_g2,
        own_gu,
        own_down,
    )


def solution(mesh):
    seq, batch = mesh.shape["seq"], mesh.shape["batch"]
    plane = batch // 2
    fine = Mesh(mesh.devices.reshape(seq // plane, plane, plane, 2), ALL)
    tokens = P(("x", "core"), ("z", "y"), None)
    rows = P(ALL, None)
    vector = P(ALL)
    return jax.shard_map(
        shards,
        mesh=fine,
        in_specs=(
            tokens,
            P(("x", "core")),
            vector,
            rows,
            rows,
            rows,
            P(),
            P(),
            rows,
            vector,
            rows,
            rows,
            tokens,
        ),
        out_specs=(
            tokens,
            tokens,
            vector,
            rows,
            rows,
            rows,
            P(),
            P(),
            rows,
            vector,
            rows,
            rows,
        ),
        check_vma=False,
    )
```
